32 devices in a mesh: seq: 8 (over z, core), head: 4 (over y, x).
Axes of the slice: x: 2, y: 2, z: 4, core: 2. Of those that a mesh axis runs over, the one named last changes fastest.
Arguments:
- tokens: bfloat16 [8192, 1152], P('seq'), may hold values from -6 to 6
- conditioning: bfloat16 [16, 1152], replicated, may hold values from -6 to 6
- image_index: int32 [8192], replicated, may hold values from 0 to 15, as said below
- qkv_weight: bfloat16 [1152, 3, 1152], P(None, None, 'head'), may hold values from -0.1875 to 0.1875
- qv_bias: bfloat16 [2, 1152], P(None, 'head'), may hold values from -3 to 3
- out_weight: bfloat16 [1152, 1152], P('head'), may hold values from -2 to 2
- out_bias: bfloat16 [1152], replicated, may hold values from -3 to 3
- up_weight: bfloat16 [1152, 4608], P(None, 'head'), may hold values from -0.1875 to 0.1875
- up_bias: bfloat16 [4608], P('head'), may hold values from -3 to 3
- down_weight: bfloat16 [4608, 1152], P('head'), may hold values from -0.09375 to 0.09375
- down_bias: bfloat16 [1152], replicated, may hold values from -3 to 3
- ada_weight: bfloat16 [1152, 6, 1152], P(None, None, 'head'), may hold values from -0.1875 to 0.1875
- ada_bias: bfloat16 [6, 1152], P(None, 'head'), may hold values from -3 to 3
- cotangent: bfloat16 [8192, 1152], P('seq'), may hold values from -6 to 6
Outputs:
- layer_out: bfloat16 [8192, 1152], P('seq')
- grad_tokens: float32 [8192, 1152], P('seq')
- grad_conditioning: float32 [16, 1152], replicated
- grad_qkv_weight: float32 [1152, 3, 1152], P('seq', None, 'head')
- grad_qv_bias: float32 [2, 1152], P(None, 'head')
- grad_out_weight: float32 [1152, 1152], P('head', 'seq')
- grad_out_bias: float32 [1152], replicated
- grad_up_weight: float32 [1152, 4608], P('seq', 'head')
- grad_up_bias: float32 [4608], P('head')
- grad_down_weight: float32 [4608, 1152], P('head', 'seq')
- grad_down_bias: float32 [1152], replicated
- grad_ada_weight: float32 [1152, 6, 1152], P(None, None, 'head')
- grad_ada_bias: float32 [6, 1152], P(None, 'head')
The draws below stay inside these ranges and needn't reach their ends.
Inputs may be any that keep to these rules, and one draw needn't show every extreme that they name: `image_index`: never falls along the rows and every image 0 to 15 holds a row. Each image's rows lie inside two consecutive aligned blocks of 1024 rows; every border between two aligned blocks of 1024 rows lies inside some image.
All inputs are finite; a program needn't handle non-finite values.
Results may differ from the reference program's by a relative error of at most 0.02.
The reference program's roundings to bfloat16 on the way count: a program that leaves them out, or rounds other values in their place, can miss the bound.
Values may be sent and summed in bfloat16 or wider, within the bound.
No kernel may reach another device: no remote copies, remote signals or barrier semaphores. Data moves between devices by JAX's collectives and lax.ppermute only.
A program may use at most 320 MiB of HBM per device.

```python
import math
import jax
import jax.numpy as jnp
from jax import lax

D = 1152
HEADS = 16
HDIM = 72
FF = 4608
TOK_DEV = 1024
IMAGES = 16
HD = 1152
TOKENS = 8192


def draw_image_index(key, part):
    key = jax.random.fold_in(key, 7)
    first_key, second_key = jax.random.split(key)
    slots = TOKENS // TOK_DEV
    early = jax.random.randint(first_key, (slots,), TOK_DEV // 8, 3 * TOK_DEV // 8, dtype=jnp.int32)
    late = jax.random.randint(second_key, (slots,), TOK_DEV // 8, 3 * TOK_DEV // 8, dtype=jnp.int32)
    slot_ids = jnp.arange(slots, dtype=jnp.int32)
    slot_starts = slot_ids * TOK_DEV
    first_cut = jnp.where(slot_ids == 0, slot_starts, slot_starts + early)
    second_cut = slot_starts + TOK_DEV // 2 + late
    starts = jnp.stack([first_cut, second_cut], axis=-1).reshape(-1)
    row_ids = jnp.arange(TOKENS, dtype=jnp.int32)
    return jnp.sum((row_ids[:, None] >= starts[None, :]).astype(jnp.int32), axis=1) - 1


def block_scale(rng, shape, cuts, smallest, top_value):
    level, own = 1.0, jax.random.fold_in(rng, 6)
    for position, blocks in cuts:
        draws = jnp.exp(jax.random.uniform(jax.random.fold_in(own, position), (blocks,), jnp.float32, smallest / len(cuts), top_value / len(cuts)))
        level = level * jnp.repeat(draws, shape[position] // blocks).reshape([-1 if axis == position else 1 for axis in range(len(shape))])
    return level


def centred(stream_key, shape, scale, bound, cuts=(), kind=jnp.bfloat16):
    loudness = block_scale(stream_key, shape, cuts, -0.22, 0.18) if cuts else 1.0
    array = jax.random.normal(stream_key, shape, jnp.float32) * scale * loudness
    return jnp.minimum(jnp.maximum(array, -bound), bound).astype(kind)


def setup_inputs(seed: int = 0) -> dict:
    keys = jax.random.split(jax.random.key(seed), 15)
    return {
        "tokens": centred(keys[0], (TOKENS, D), 1.0, 6.0, ((0, 8),)),
        "conditioning": centred(keys[1], (IMAGES, D), 1.0, 6.0),
        "image_index": draw_image_index(jax.random.fold_in(keys[14], 71), 0),
        "qkv_weight": centred(keys[3], (D, 3, HD), D ** -0.5, 0.1875, ((2, 4),)),
        "qv_bias": centred(keys[4], (2, HD), 0.5, 3.0, ((1, 4),)),
        "out_weight": centred(keys[5], (HD, D), 8 ** -0.5, 2.0, ((0, 4),)),
        "out_bias": centred(keys[6], (D,), 0.5, 3.0),
        "up_weight": centred(keys[7], (D, FF), D ** -0.5, 0.1875, ((1, 4),)),
        "up_bias": centred(keys[8], (FF,), 0.5, 3.0, ((0, 4),)),
        "down_weight": centred(keys[9], (FF, D), FF ** -0.5, 0.09375, ((0, 4),)),
        "down_bias": centred(keys[10], (D,), 0.5, 3.0),
        "ada_weight": centred(keys[11], (D, 6, D), D ** -0.5, 0.1875, ((2, 4),)),
        "ada_bias": centred(keys[12], (6, D), 0.5, 3.0, ((1, 4),)),
        "cotangent": centred(keys[13], (TOKENS, D), 1.0, 6.0, ((0, 8),)),
    }


EPSILON = 1e-06
MASKED = -1e+30
PRECISE = lax.Precision.HIGHEST

@jax.custom_vjp
def low(v):
    return lax.optimization_barrier(v.astype(jnp.bfloat16)).astype(jnp.float32)

@jax.custom_vjp
def low_back(v):
    return v

def low_keep(v):
    return (low(v), None)

def low_pass(kept, grad):
    return (grad,)

def back_keep(v):
    return (v, None)

def back_low(kept, grad):
    return (low(grad),)
low.defvjp(low_keep, low_pass)
low_back.defvjp(back_keep, back_low)

def normalize(values):
    center = values - lax.optimization_barrier(jnp.mean(values, axis=-1, keepdims=True))
    return center * lax.rsqrt(lax.optimization_barrier(jnp.mean(center * center, axis=-1, keepdims=True)) + EPSILON)

def gelu_tanh(values):
    return jax.nn.gelu(values, approximate=True)

def attend(query_rows, key_rows, value_rows, image_index):
    block_rows = math.gcd(TOK_DEV, 512)
    number = TOKENS // block_rows
    window = 3 * TOK_DEV
    scaling = HDIM ** (-0.5)
    padded_images = jnp.pad(image_index, (TOK_DEV, TOK_DEV), constant_values=-1)

    def heads_first(values):
        return values.reshape(TOKENS, HEADS, HDIM).transpose(1, 0, 2)

    def one_head(operands):
        query_head, key_head, value_head = operands
        key_padded = jnp.pad(key_head, ((TOK_DEV, TOK_DEV), (0, 0)))
        value_padded = jnp.pad(value_head, ((TOK_DEV, TOK_DEV), (0, 0)))

        def one_block(block_index):
            row_start = block_index * block_rows
            window_start = row_start // TOK_DEV * TOK_DEV
            query_block = lax.dynamic_slice_in_dim(query_head, row_start, block_rows, 0)
            image_block = lax.dynamic_slice_in_dim(image_index, row_start, block_rows, 0)
            key_block = lax.dynamic_slice_in_dim(key_padded, window_start, window, 0)
            value_block = lax.dynamic_slice_in_dim(value_padded, window_start, window, 0)
            key_images = lax.dynamic_slice_in_dim(padded_images, window_start, window, 0)
            scores = low_back(jnp.dot(query_block, key_block.T, precision=PRECISE) * scaling)
            visible = image_block[:, None] == key_images[None, :]
            scores = jnp.where(visible, scores, MASKED)
            row_max = lax.optimization_barrier(jnp.max(scores, axis=-1, keepdims=True))
            weights = jnp.exp(scores - row_max)
            shares = weights / lax.optimization_barrier(jnp.sum(weights, axis=-1, keepdims=True))
            return jnp.dot(low(shares), value_block, precision=PRECISE)
        blocks = lax.map(jax.checkpoint(one_block), jnp.arange(number, dtype=jnp.int32))
        return blocks.reshape(TOKENS, HDIM)
    result = lax.map(one_head, (heads_first(query_rows), heads_first(key_rows), heads_first(value_rows)))
    return result.transpose(1, 0, 2).reshape(TOKENS, HEADS * HDIM)

def layer_forward(tokens, conditioning, qkv_weight, qv_bias, out_weight, out_bias, up_weight, up_bias, down_weight, down_bias, ada_weight, ada_bias, image_index):
    one_hot = (image_index[:, None] == jnp.arange(IMAGES, dtype=jnp.int32)[None, :]).astype(jnp.float32)
    cond_act = low(jax.nn.silu(conditioning))
    modulation = jnp.einsum('id,dkf->ikf', cond_act, ada_weight, precision=PRECISE) + ada_bias[None]
    per_row = [jnp.dot(one_hot, modulation[:, component], precision=PRECISE) for component in range(6)]
    shift_one, scale_one, gate_one, shift_two, scale_two, gate_two = per_row
    normed_one = normalize(tokens)
    hidden_one = low(normed_one * (1.0 + scale_one) + shift_one)
    projected = jnp.einsum('td,dkf->tkf', hidden_one, qkv_weight, precision=PRECISE)
    query_rows = low_back(low(projected[:, 0] + qv_bias[0]))
    key_rows = low_back(low(projected[:, 1]))
    value_rows = low_back(low(projected[:, 2] + qv_bias[1]))
    attended = attend(query_rows, key_rows, value_rows, image_index)
    attended_low = low_back(low(attended))
    attn_branch = low_back(jnp.dot(attended_low, out_weight, precision=PRECISE) + out_bias)
    middle = tokens + gate_one * attn_branch
    normed_two = normalize(middle)
    hidden_two = low(normed_two * (1.0 + scale_two) + shift_two)
    pre_act = low_back(jnp.dot(hidden_two, up_weight, precision=PRECISE) + up_bias)
    act_low = low(gelu_tanh(pre_act))
    mlp_branch = low_back(jnp.dot(act_low, down_weight, precision=PRECISE) + down_bias)
    return middle + gate_two * mlp_branch

def reference(tokens, conditioning, image_index, qkv_weight, qv_bias, out_weight, out_bias, up_weight, up_bias, down_weight, down_bias, ada_weight, ada_bias, cotangent):
    floats = tuple((argument.astype(jnp.float32) for argument in (tokens, conditioning, qkv_weight, qv_bias, out_weight, out_bias, up_weight, up_bias, down_weight, down_bias, ada_weight, ada_bias)))

    def forward(*operands):
        return layer_forward(*operands, image_index)
    layer_out, pull = jax.vjp(forward, *floats)
    gradients = pull(cotangent.astype(jnp.float32))
    return (layer_out.astype(jnp.bfloat16), gradients[0], gradients[1], gradients[2], gradients[3], gradients[4], gradients[5], gradients[6], gradients[7], gradients[8], gradients[9], gradients[10], gradients[11])
```

```python
import jax
import jax.numpy as jnp
from jax import lax
from jax.sharding import PartitionSpec as P

HDIM = 72


EPSILON = 1e-06
MASKED = -1e30
PRECISE = lax.Precision.HIGHEST
CHUNKS = 2


def peers(axis):
    return range(1, lax.axis_size(axis))


def swap(value, axis, mask):
    count = lax.axis_size(axis)
    return lax.ppermute(value, axis, [(i, i ^ mask) for i in range(count)])


def gather_pieces(value, axis):
    return [value] + [swap(value, axis, mask) for mask in peers(axis)]


def trade_pieces(blocks, axis):
    me = lax.axis_index(axis)
    own = lax.dynamic_index_in_dim(blocks, me, 0, keepdims=False)
    return [own] + [
        swap(lax.dynamic_index_in_dim(blocks, me ^ mask, 0, keepdims=False), axis, mask)
        for mask in peers(axis)
    ]


def place_pieces(pieces, axis, dim=0):
    me = lax.axis_index(axis)
    width = pieces[0].shape[dim]
    shape = list(pieces[0].shape)
    shape[dim] = width * len(pieces)
    result = jnp.zeros(shape, pieces[0].dtype)
    for mask, piece in enumerate(pieces):
        result = lax.dynamic_update_slice_in_dim(result, piece, (me ^ mask) * width, dim)
    return result


def butterfly_sum(value, axis):
    mask = 1
    while mask < lax.axis_size(axis):
        value = value + swap(value, axis, mask)
        mask *= 2
    return value


def three_parts(values):
    first = lax.reduce_precision(values, 8, 7)
    second = lax.reduce_precision(values - first, 8, 7)
    third = values - first - second
    return [part.astype(jnp.bfloat16) for part in (first, second, third)]


def image_sums(one_hot_low, values):
    first = lax.reduce_precision(values, 8, 7)
    second = (values - first).astype(jnp.bfloat16)
    return sum(
        lax.dot_general(
            one_hot_low, part, (((0,), (0,)), ((), ())), preferred_element_type=jnp.float32
        )
        for part in (first.astype(jnp.bfloat16), second)
    )


def extended(cells, sides, width):
    for axis, dim in sides:
        count = lax.axis_size(axis)
        ends = count - 1
        head = lax.slice_in_dim(cells, 0, width, axis=dim)
        tail = lax.slice_in_dim(cells, cells.shape[dim] - width, cells.shape[dim], axis=dim)
        cells = jnp.concatenate(
            [
                lax.ppermute(tail, axis, [(i, (i + 1) % count) for i in range(ends)]),
                cells,
                lax.ppermute(head, axis, [((i + 1) % count, i) for i in range(ends)]),
            ],
            axis=dim,
        )
    return cells


def normalize(values):
    center = values - jnp.mean(values, axis=-1, keepdims=True)
    inverse = lax.rsqrt(jnp.mean(center * center, axis=-1, keepdims=True) + EPSILON)
    return (center * inverse, inverse)


def norm_back(gradient, normed, inverse):
    return (
        gradient
        - jnp.mean(gradient, axis=-1, keepdims=True)
        - normed * jnp.mean(gradient * normed, axis=-1, keepdims=True)
    ) * inverse


def gelu_tanh(values):
    return jax.nn.gelu(values, approximate=True)


def split_heads(matrix, head_count):
    amount = matrix.shape[0]
    return matrix.reshape(amount, head_count, -1).transpose(1, 0, 2)


def join_heads(tensor):
    head_count, amount, head_size = tensor.shape
    return tensor.transpose(1, 0, 2).reshape(amount, head_count * head_size)


def score_grads(
    query_heads, grad_heads, key_heads, value_heads, visible, log_total, delta, scaling
):
    scores = (
        jnp.einsum("hqd,hkd->hqk", query_heads, key_heads, preferred_element_type=jnp.float32)
        * scaling
    )
    shares = jnp.where(visible, jnp.exp(scores - log_total[..., None]), 0.0)
    grad_shares = jnp.einsum(
        "hqd,hkd->hqk", grad_heads, value_heads, preferred_element_type=jnp.float32
    )
    grad_scores = (shares * (grad_shares - delta[..., None])).astype(jnp.bfloat16)
    return (shares.astype(jnp.bfloat16), grad_scores)


def on_device(
    tokens,
    conditioning,
    image_index,
    qkv_weight,
    qv_bias,
    out_weight,
    out_bias,
    up_weight,
    up_bias,
    down_weight,
    down_bias,
    ada_weight,
    ada_bias,
    cotangent,
):
    row_count, width = tokens.shape
    feature_count = qkv_weight.shape[2]
    head_count = feature_count // HDIM
    scaling = HDIM ** (-0.5)
    head_size = lax.axis_size("head")
    me = lax.axis_index("head")
    chunk_rows = row_count // CHUNKS
    own_rows = chunk_rows // head_size
    my_index = lax.axis_index("seq")
    my_images = lax.dynamic_slice_in_dim(image_index, my_index * row_count, row_count, 0)
    padded_images = jnp.pad(image_index, (row_count, row_count), constant_values=-1)
    wide_images = lax.dynamic_slice_in_dim(padded_images, my_index * row_count, 3 * row_count, 0)
    image_count = conditioning.shape[0]
    one_hot = (
        my_images[:, None] == jnp.arange(image_count, dtype=jnp.int32)[None, :]
    ).astype(jnp.bfloat16)

    def chunk_of(values, c):
        return lax.slice_in_dim(values, c * chunk_rows, (c + 1) * chunk_rows, axis=0)

    def own_of(values, c):
        return lax.dynamic_slice_in_dim(values, c * chunk_rows + me * own_rows, own_rows, 0)

    def own_all(values):
        return jnp.concatenate([own_of(values, c) for c in range(CHUNKS)], axis=0)

    cond_float = conditioning.astype(jnp.float32)
    cond_act = jax.nn.silu(cond_float).astype(jnp.bfloat16)
    mod_mine = jnp.einsum("id,dkf->ikf", cond_act, ada_weight, preferred_element_type=jnp.float32)
    mod_mine = mod_mine + ada_bias.astype(jnp.float32)[None]
    modulation = place_pieces(gather_pieces(mod_mine, "head"), "head", 2)
    out_full = jnp.stack(gather_pieces(out_weight, "head"))
    hot_three = jnp.concatenate([one_hot] * 3, axis=1)

    def per_row(hot, component):
        return jnp.dot(
            hot,
            jnp.concatenate(three_parts(modulation[:, component]), axis=0),
            preferred_element_type=jnp.float32,
        )

    shift_one, scale_one, gate_one, shift_two, scale_two, gate_two = [
        per_row(hot_three, component) for component in range(6)
    ]
    inputs = tokens.astype(jnp.float32)
    normed_one, inverse_one = normalize(inputs)
    hidden_one = (normed_one * (1.0 + scale_one) + shift_one).astype(jnp.bfloat16)
    projected = jnp.einsum(
        "td,dkf->tkf", hidden_one, qkv_weight, preferred_element_type=jnp.float32
    )
    bias_rows = qv_bias.astype(jnp.float32)
    query_low = (projected[:, 0] + bias_rows[0]).astype(jnp.bfloat16)
    key_low = projected[:, 1].astype(jnp.bfloat16)
    value_low = (projected[:, 2] + bias_rows[1]).astype(jnp.bfloat16)
    key_value = jnp.stack([key_low, value_low], axis=1)
    query_heads = split_heads(query_low, head_count)
    wide_kv = extended(key_value, (("seq", 0),), row_count)

    grad_out = cotangent.astype(jnp.float32)
    grad_mlp = (gate_two * grad_out).astype(jnp.bfloat16)
    grad_down_bias = jnp.sum(grad_mlp.astype(jnp.float32), axis=0)
    grad_act = jnp.dot(grad_mlp, down_weight.T, preferred_element_type=jnp.float32)

    wide_keys = split_heads(wide_kv[:, 0], head_count)
    wide_values = split_heads(wide_kv[:, 1], head_count)
    visible = (my_images[:, None] == wide_images[None, :])[None]
    scores = (
        jnp.einsum("hqd,hkd->hqk", query_heads, wide_keys, preferred_element_type=jnp.float32)
        * scaling
    )
    scores = jnp.where(visible, scores, MASKED)
    row_max = jnp.max(scores, axis=-1)
    weights = jnp.where(visible, jnp.exp(scores - row_max[..., None]), 0.0)
    row_total = jnp.sum(weights, axis=-1)
    log_total = row_max + jnp.log(row_total)
    shares = (weights / row_total[..., None]).astype(jnp.bfloat16)
    attended = jnp.einsum("hqk,hkd->hqd", shares, wide_values, preferred_element_type=jnp.float32)
    attended_low = join_heads(attended).astype(jnp.bfloat16)

    hidden_two, act_low, grad_pre = [], [], []
    mlp_parts, hidden_parts = [], []
    attn_own, middle_own, normed_own, inverse_own = [], [], [], []
    late_sums = []
    for c in range(CHUNKS):
        pieces = gather_pieces(chunk_of(attended_low, c), "head")
        attn_branch = sum(
            jnp.dot(piece, out_full[m], preferred_element_type=jnp.float32)
            for m, piece in enumerate(pieces)
        ) + out_bias.astype(jnp.float32)
        middle = chunk_of(inputs, c) + chunk_of(gate_one, c) * attn_branch
        normed_two, inverse_two = normalize(middle)
        hidden = (
            normed_two * (1.0 + chunk_of(scale_two, c)) + chunk_of(shift_two, c)
        ).astype(jnp.bfloat16)
        pre_act = jnp.dot(
            hidden, up_weight, preferred_element_type=jnp.float32
        ) + up_bias.astype(jnp.float32)
        act, gelu_pull = jax.vjp(gelu_tanh, pre_act)
        grad_p = gelu_pull(chunk_of(grad_act, c))[0].astype(jnp.bfloat16)
        part = jnp.dot(grad_p, up_weight.T, preferred_element_type=jnp.float32)
        hidden_parts.append(
            trade_pieces(
                part.astype(jnp.bfloat16).reshape(head_size, own_rows, width), "head"
            )
        )
        act = act.astype(jnp.bfloat16)
        mlp_part = jnp.dot(act, down_weight, preferred_element_type=jnp.float32)
        mlp_parts.append(
            trade_pieces(
                mlp_part.astype(jnp.bfloat16).reshape(head_size, own_rows, width), "head"
            )
        )
        hot = chunk_of(one_hot, c)
        late_sums.append(
            [
                image_sums(hot, part),
                image_sums(hot, part * normed_two),
                image_sums(hot, chunk_of(grad_out, c) * mlp_part),
            ]
        )
        hidden_two.append(hidden)
        act_low.append(act)
        grad_pre.append(grad_p)

        def mine(values):
            return lax.dynamic_slice_in_dim(values, me * own_rows, own_rows, 0)

        attn_own.append(mine(attn_branch))
        middle_own.append(mine(middle))
        normed_own.append(mine(normed_two))
        inverse_own.append(mine(inverse_two))
    hidden_two = jnp.concatenate(hidden_two, axis=0)
    act_low = jnp.concatenate(act_low, axis=0)
    grad_pre = jnp.concatenate(grad_pre, axis=0)

    grad_middle_own, grad_attended_rows, grad_attn_rows = [], [], []
    gate_sums, grad_out_bias = 0.0, 0.0
    for c in range(CHUNKS):
        grad_hidden_two = sum(piece.astype(jnp.float32) for piece in hidden_parts[c])
        grad_middle = own_of(grad_out, c) + norm_back(
            grad_hidden_two * (1.0 + own_of(scale_two, c)), normed_own[c], inverse_own[c]
        )
        grad_attn = (own_of(gate_one, c) * grad_middle).astype(jnp.bfloat16)
        blocks = jnp.stack(
            [
                lax.dot_general(
                    grad_attn,
                    out_full[m],
                    (((1,), (1,)), ((), ())),
                    preferred_element_type=jnp.float32,
                ).astype(jnp.bfloat16)
                for m in range(head_size)
            ]
        )
        got = [blocks[0]] + [swap(blocks[m], "head", m) for m in peers("head")]
        grad_attended_rows.append(place_pieces(got, "head", 0))
        grad_attn_rows.append(place_pieces(gather_pieces(grad_attn, "head"), "head", 0))
        grad_middle_own.append(grad_middle)
        gate_sums = gate_sums + image_sums(own_of(one_hot, c), grad_middle * attn_own[c])
        grad_out_bias = grad_out_bias + jnp.sum(grad_attn.astype(jnp.float32), axis=0)
    grad_attended = jnp.concatenate(grad_attended_rows, axis=0)
    grad_attn = jnp.concatenate(grad_attn_rows, axis=0)

    grad_heads = split_heads(grad_attended, head_count)
    delta = jnp.sum(grad_heads.astype(jnp.float32) * attended, axis=-1)
    shares_low, grad_scores = score_grads(
        query_heads, grad_heads, wide_keys, wide_values, visible, log_total, delta, scaling
    )
    grad_query_heads = (
        jnp.einsum("hqk,hkd->hqd", grad_scores, wide_keys, preferred_element_type=jnp.float32)
        * scaling
    )
    grad_keys_wide = (
        jnp.einsum("hqk,hqd->hkd", grad_scores, query_heads, preferred_element_type=jnp.float32)
        * scaling
    )
    grad_values_wide = jnp.einsum(
        "hqk,hqd->hkd", shares_low, grad_heads, preferred_element_type=jnp.float32
    )
    grad_wide = jnp.stack([join_heads(grad_keys_wide), join_heads(grad_values_wide)], axis=1)
    outward = jnp.concatenate(
        [grad_wide[:row_count], grad_wide[2 * row_count :]], axis=0
    ).astype(jnp.bfloat16)
    inward = extended(outward, (("seq", 0),), row_count)
    grad_kv_mine = (
        grad_wide[row_count : 2 * row_count]
        + inward[:row_count].astype(jnp.float32)
        + inward[3 * row_count :].astype(jnp.float32)
    )
    grad_key_low = grad_kv_mine[:, 0].astype(jnp.bfloat16)
    grad_value_low = grad_kv_mine[:, 1].astype(jnp.bfloat16)
    grad_query_low = join_heads(grad_query_heads).astype(jnp.bfloat16)
    grad_qkv = jnp.stack([grad_query_low, grad_key_low, grad_value_low], axis=1)
    grad_qv_bias = jnp.stack(
        [
            jnp.sum(grad_query_low.astype(jnp.float32), axis=0),
            jnp.sum(grad_value_low.astype(jnp.float32), axis=0),
        ]
    )

    one_parts = []
    first_sums = []
    for c in range(CHUNKS):
        part = jnp.einsum(
            "tkf,dkf->td", chunk_of(grad_qkv, c), qkv_weight, preferred_element_type=jnp.float32
        )
        one_parts.append(
            trade_pieces(
                part.astype(jnp.bfloat16).reshape(head_size, own_rows, width), "head"
            )
        )
        hot = chunk_of(one_hot, c)
        first_sums.append(
            [image_sums(hot, part), image_sums(hot, part * chunk_of(normed_one, c))]
        )
    token_rows, out_rows = [], []
    for c in range(CHUNKS):
        grad_hidden_one = sum(piece.astype(jnp.float32) for piece in one_parts[c])
        rows = grad_middle_own[c] + norm_back(
            grad_hidden_one * (1.0 + own_of(scale_one, c)),
            own_of(normed_one, c),
            own_of(inverse_one, c),
        )
        token_rows.append(
            place_pieces(gather_pieces(rows.astype(jnp.bfloat16), "head"), "head", 0)
        )
        mlp_branch = sum(
            piece.astype(jnp.float32) for piece in mlp_parts[c]
        ) + down_bias.astype(jnp.float32)
        rows = (middle_own[c] + own_of(gate_two, c) * mlp_branch).astype(jnp.bfloat16)
        out_rows.append(place_pieces(gather_pieces(rows, "head"), "head", 0))
    grad_tokens = jnp.concatenate(token_rows, axis=0).astype(jnp.float32)
    layer_out = jnp.concatenate(out_rows, axis=0)

    columns = ada_weight.shape[2]

    def to_owners(values):
        amount = values.shape[0]
        blocks = values.reshape(amount, head_size, columns).transpose(1, 0, 2)
        return sum(trade_pieces(blocks, "head"))

    late = [sum(values) for values in zip(*late_sums)]
    late_mine = to_owners(
        jnp.concatenate([gate_sums] + late + [grad_out_bias[None]], axis=0)
    )
    bias_sums = jnp.dot(one_hot.T, cotangent, preferred_element_type=jnp.float32)
    bias_sums = bias_sums * down_bias.astype(jnp.float32)
    bias_sums = lax.dynamic_slice_in_dim(bias_sums, me * columns, columns, 1)
    late_mine = lax.dynamic_update_slice_in_dim(
        late_mine,
        lax.slice_in_dim(late_mine, 3 * image_count, 4 * image_count, axis=0) + bias_sums,
        3 * image_count,
        0,
    )
    grad_up_bias = jnp.sum(grad_pre.astype(jnp.float32), axis=0)
    low_bias = jnp.concatenate([grad_up_bias, grad_down_bias])
    late_mine = butterfly_sum(late_mine, "seq")
    low_bias = butterfly_sum(low_bias, "seq")
    grad_up_bias, grad_down_bias = jnp.split(low_bias, [grad_up_bias.shape[0]])
    first = [sum(values) for values in zip(*first_sums)]
    first_mine = to_owners(jnp.concatenate(first, axis=0))
    first_mine = butterfly_sum(jnp.concatenate([first_mine, grad_qv_bias], axis=0), "seq")
    grad_qv_bias = first_mine[2 * image_count :]
    grad_mod = jnp.stack(
        [
            first_mine[:image_count],
            first_mine[image_count : 2 * image_count],
            late_mine[:image_count],
            late_mine[image_count : 2 * image_count],
            late_mine[2 * image_count : 3 * image_count],
                late_mine[3 * image_count : 4 * image_count],
        ],
        axis=1,
    )
    grad_ada_bias = jnp.sum(grad_mod, axis=0)
    grad_ada_weight = jnp.einsum(
        "id,ikf->dkf", cond_act.astype(jnp.float32), grad_mod, precision=PRECISE
    )
    grad_cond_act = jnp.einsum(
        "ikf,dkf->id", grad_mod, ada_weight.astype(jnp.float32), precision=PRECISE
    )
    spread_bias = lax.dynamic_update_slice(
        jnp.zeros((1, width), jnp.float32), late_mine[4 * image_count :], (0, me * columns)
    )
    last = butterfly_sum(jnp.concatenate([grad_cond_act, spread_bias], axis=0), "head")
    _, silu_pull = jax.vjp(jax.nn.silu, cond_float)
    grad_conditioning = silu_pull(last[:image_count])[0]
    grad_out_bias = last[image_count]

    def weight_sum(parts):
        low = [part.astype(jnp.bfloat16) for part in parts]
        total = lax.psum_scatter(
            jnp.concatenate(low, axis=1), "seq", scatter_dimension=0, tiled=True
        ).astype(jnp.float32)
        cuts = [part.shape[1] for part in parts]
        result, place = [], 0
        for cut in cuts:
            result.append(lax.slice_in_dim(total, place, place + cut, axis=1))
            place += cut
        return result

    def outer(left, right):
        return lax.dot_general(
            left, right, (((0,), (0,)), ((), ())), preferred_element_type=jnp.float32
        )

    grad_up_weight, grad_down_weight = weight_sum(
        [outer(hidden_two, grad_pre), outer(grad_mlp, act_low)]
    )
    grad_out_weight, grad_qkv_weight = weight_sum(
        [
            outer(grad_attn, attended_low),
            outer(hidden_one, grad_qkv.reshape(row_count, 3 * feature_count)),
        ]
    )
    return (
        layer_out,
        grad_tokens,
        grad_conditioning,
        grad_qkv_weight.reshape(-1, 3, feature_count),
        grad_qv_bias,
        grad_out_weight.T,
        grad_out_bias,
        grad_up_weight,
        grad_up_bias,
        grad_down_weight.T,
        grad_down_bias,
        grad_ada_weight,
        grad_ada_bias,
    )


def solution(mesh):
    placed = (
        P("seq", None),
        P(),
        P(),
        P(None, None, "head"),
        P(None, "head"),
        P("head", None),
        P(),
        P(None, "head"),
        P("head"),
        P("head", None),
        P(),
        P(None, None, "head"),
        P(None, "head"),
        P("seq", None),
    )
    return jax.shard_map(
        on_device,
        mesh=mesh,
        in_specs=placed,
        out_specs=(
            P("seq", None),
            P("seq", None),
            P(),
            P("seq", None, "head"),
            P(None, "head"),
            P("head", "seq"),
            P(),
            P("seq", "head"),
            P("head"),
            P("head", "seq"),
            P(),
            P(None, None, "head"),
            P(None, "head"),
        ),
        check_vma=False,
    )
```

```python
import functools

import jax
import jax.numpy as jnp
from jax import lax
from jax.experimental import pallas as pl
from jax.experimental.pallas import tpu as pltpu
from jax.sharding import PartitionSpec as P

HDIM = 72


EPSILON = 1e-06
MASKED = -1e30
PRECISE = lax.Precision.HIGHEST
CHUNKS = 2
KEY_TILE = 512
QUERY_BLOCK = 256
ROW_BLOCK = 256
ROOT = 0.7978845608028654
CUBIC = 0.044715


def peers(axis):
    return range(1, lax.axis_size(axis))


def swap(value, axis, mask):
    count = lax.axis_size(axis)
    return lax.ppermute(value, axis, [(i, i ^ mask) for i in range(count)])


def gather_pieces(value, axis):
    return [value] + [swap(value, axis, mask) for mask in peers(axis)]


def butterfly_sum(value, axis):
    mask = 1
    while mask < lax.axis_size(axis):
        value = value + swap(value, axis, mask)
        mask *= 2
    return value


def three_parts(values):
    first = lax.reduce_precision(values, 8, 7)
    second = lax.reduce_precision(values - first, 8, 7)
    third = values - first - second
    return [part.astype(jnp.bfloat16) for part in (first, second, third)]


def swap_pieces(pieces, axis):
    return [pieces[0]] + [swap(pieces[mask], axis, mask) for mask in peers(axis)]


def pick(which, cases):
    result = cases[0]
    for number, case in enumerate(cases[1:], 1):
        result = jnp.where(which == number, case, result)
    return result


def step_along(value, axis, ahead):
    count = lax.axis_size(axis)
    pairs = [(i, i + 1) if ahead else (i + 1, i) for i in range(count - 1)]
    return lax.ppermute(value, axis, pairs)


LOG2E = 1.4426950408889634
MIB = 1 << 20


def head_window(head, features):
    place = head * HDIM
    start = place // 128 * 128
    return start, min(features, start + 256)


def head_only(block, head):
    features = block.shape[1]
    start, stop = head_window(head, features)
    window = block[:, start:stop]
    lane = lax.broadcasted_iota(jnp.int32, window.shape, 1) + (start - head * HDIM)
    return jnp.where((lane >= 0) & (lane < HDIM), window, jnp.zeros_like(window))


def visible_keys(first_ref, length_ref, base, tile_rows):
    first = first_ref[...] - base
    place = lax.broadcasted_iota(jnp.int32, (tile_rows, first.shape[1]), 0)
    offset = place - first
    return (offset >= 0) & (offset < length_ref[...])


def rows_dot(left, right):
    return lax.dot_general(
        left, right, (((1,), (1,)), ((), ())), preferred_element_type=jnp.float32
    )


def attend_kernel(
    low_ref, high_ref, first_ref, length_ref, query_ref, *refs, sources, tile, step_base
):
    kv_refs = refs[: len(sources)]
    low_out, wide_out, log_out, total, row_max, row_sum = refs[len(sources) :]
    features = query_ref.shape[1]
    heads = features // HDIM
    amount = query_ref.shape[0]
    step = pl.program_id(0) + step_base
    queries = [head_only(query_ref[...], head) for head in range(heads)]
    rescale = HDIM ** (-0.5) * LOG2E
    total[...] = jnp.zeros_like(total)
    row_max[...] = jnp.full_like(row_max, MASKED)
    row_sum[...] = jnp.zeros_like(row_sum)
    for source, kv_ref in zip(sources, kv_refs):
        tiles = kv_ref.shape[1] // tile

        def body(number, carry):
            place = pl.multiple_of((number - source * tiles) * tile, tile)
            keys = kv_ref[0, pl.ds(place, tile), :]
            values = kv_ref[1, pl.ds(place, tile), :].astype(jnp.float32).T
            seen = visible_keys(first_ref, length_ref, number * tile, tile)
            for head in range(heads):
                start, stop = head_window(head, features)
                scores = rows_dot(keys[:, start:stop], queries[head])
                scores = jnp.where(seen, scores, MASKED)
                old = row_max[head : head + 1, :]
                new = jnp.maximum(old, jnp.max(scores, axis=0, keepdims=True))
                shrink = jnp.exp2((old - new) * rescale)
                shares = jnp.exp2((scores - new) * rescale)
                row_max[head : head + 1, :] = new
                row_sum[head : head + 1, :] = row_sum[
                    head : head + 1, :
                ] * shrink + jnp.sum(shares, axis=0, keepdims=True)
                place_rows = slice(head * HDIM, (head + 1) * HDIM)
                total[place_rows, :] = total[place_rows, :] * shrink + jnp.dot(
                    values[place_rows, :].astype(jnp.bfloat16),
                    shares.astype(jnp.bfloat16),
                    preferred_element_type=jnp.float32,
                )
            return carry

        lax.fori_loop(
            jnp.maximum(low_ref[step], source * tiles),
            jnp.minimum(high_ref[step], (source + 1) * tiles),
            body,
            0,
        )
    log_out[...] = row_max[...] * rescale + jnp.log2(row_sum[...])
    for head in range(heads):
        place_rows = slice(head * HDIM, (head + 1) * HDIM)
        total[place_rows, :] = total[place_rows, :] / row_sum[head : head + 1, :]
    wide_out[...] = total[...]
    low_out[...] = total[...].T.astype(jnp.bfloat16)


def attend(lows, highs, firsts, lengths, query, kvs, tile, block, chunk, chunks):
    rows, features = query.shape
    heads = features // HDIM
    amount = rows // chunks
    steps = amount // block
    base = chunk * steps
    whole = pl.BlockSpec(kvs[0].shape, lambda i, *_: (0, 0, 0))
    across = pl.BlockSpec((1, block), lambda i, *_: (0, base + i))
    return pl.pallas_call(
        functools.partial(
            attend_kernel, sources=tuple(range(len(kvs))), tile=tile, step_base=base
        ),
        grid_spec=pltpu.PrefetchScalarGridSpec(
            num_scalar_prefetch=2,
            grid=(steps,),
            in_specs=[across, across, pl.BlockSpec((block, features), lambda i, *_: (base + i, 0))]
            + [whole] * len(kvs),
            out_specs=[
                pl.BlockSpec((block, features), lambda i, *_: (i, 0)),
                pl.BlockSpec((features, block), lambda i, *_: (0, i)),
                pl.BlockSpec((heads, block), lambda i, *_: (0, i)),
            ],
            scratch_shapes=[
                pltpu.VMEM((features, block), jnp.float32),
                pltpu.VMEM((heads, block), jnp.float32),
                pltpu.VMEM((heads, block), jnp.float32),
            ],
        ),
        out_shape=[
            jax.ShapeDtypeStruct((amount, features), jnp.bfloat16),
            jax.ShapeDtypeStruct((features, amount), jnp.float32),
            jax.ShapeDtypeStruct((heads, amount), jnp.float32),
        ],
        compiler_params=pltpu.CompilerParams(vmem_limit_bytes=24 * MIB),
        cost_estimate=pl.CostEstimate(
            flops=amount * 4096 * 1152, bytes_accessed=5 * MIB, transcendentals=0
        ),
    )(lows, highs, firsts, lengths, query, *kvs)


def attend_back_kernel(
    low_ref, high_ref, spot_ref, first_ref, length_ref, log_ref, query_ref, wide_ref, *refs,
    sources, tile, last, peer_count
):
    count = len(sources)
    kv_refs = refs[:count]
    pieces = refs[count:-4]
    if last:
        start_ref, pieces = pieces[-1], pieces[:-1]
    query_out, kv_out, total, kv_total = refs[-4:]
    piece_rows = pieces[0].shape[0]
    features = query_ref.shape[1]
    heads = features // HDIM
    step = pl.program_id(0)
    scaling = HDIM ** (-0.5)
    rescale = scaling * LOG2E

    @pl.when(step == 0)
    def _():
        kv_total[...] = jnp.zeros_like(kv_total)

    total[...] = start_ref[...] if last else jnp.zeros_like(total)
    queries = [head_only(query_ref[...], head) for head in range(heads)]
    parts = []
    for place in range(query_ref.shape[0] // piece_rows):
        block = step * (query_ref.shape[0] // piece_rows) + place
        part = jnp.zeros_like(pieces[0][...])
        for spot, piece in enumerate(pieces):
            owner = (spot_ref[0] ^ (spot % peer_count)) + spot // peer_count * peer_count
            part = jnp.where(block == owner, piece[...], part)
        parts.append(part)
    grad_rows = jnp.concatenate(parts, axis=0)
    grads = [head_only(grad_rows, head) for head in range(heads)]
    products = grad_rows.astype(jnp.float32).T * wide_ref[...]
    deltas = [
        jnp.sum(products[head * HDIM : (head + 1) * HDIM, :], axis=0, keepdims=True)
        for head in range(heads)
    ]
    for spot, (source, kv_ref) in enumerate(zip(sources, kv_refs)):
        tiles = kv_ref.shape[1] // tile

        def body(number, carry):
            place = pl.multiple_of((number - source * tiles) * tile, tile)
            rows = pl.ds(place, tile)
            keys = kv_ref[0, rows, :]
            values = kv_ref[1, rows, :]
            keys_down = keys.astype(jnp.float32).T
            seen = visible_keys(first_ref, length_ref, number * tile, tile)
            for head in range(heads):
                start, stop = head_window(head, features)
                scores = rows_dot(keys[:, start:stop], queries[head])
                shares = jnp.where(
                    seen, jnp.exp2(scores * rescale - log_ref[head : head + 1, :]), 0.0
                )
                grad_shares = rows_dot(values[:, start:stop], grads[head])
                grad_scores = (shares * (grad_shares - deltas[head])).astype(jnp.bfloat16)
                kv_total[spot, 1, rows, start:stop] += jnp.dot(
                    shares.astype(jnp.bfloat16), grads[head], preferred_element_type=jnp.float32
                )
                kv_total[spot, 0, rows, start:stop] += jnp.dot(
                    grad_scores, queries[head], preferred_element_type=jnp.float32
                )
                place_rows = slice(head * HDIM, (head + 1) * HDIM)
                total[place_rows, :] += jnp.dot(
                    keys_down[place_rows, :].astype(jnp.bfloat16),
                    grad_scores,
                    preferred_element_type=jnp.float32,
                )
            return carry

        lax.fori_loop(
            jnp.maximum(low_ref[step], source * tiles),
            jnp.minimum(high_ref[step], (source + 1) * tiles),
            body,
            0,
        )
    if last:
        query_out[...] = (total[...].T * scaling).astype(query_out.dtype)
    else:
        query_out[...] = total[...]

    @pl.when(step == pl.num_programs(0) - 1)
    def _():
        for spot in range(count):
            kv_out[spot, 0] = (kv_total[spot, 0] * scaling).astype(kv_out.dtype)
            kv_out[spot, 1] = kv_total[spot, 1].astype(kv_out.dtype)


def attend_back(
    spot, ranges, logs, query, grads, wide, kvs, sources, tile, block, started=None
):
    lows, highs, firsts, lengths = ranges
    pieces = [piece for chunk in grads for piece in chunk]

    rows, features = query.shape
    heads = features // HDIM
    steps = rows // block
    last = started is not None
    whole = pl.BlockSpec(kvs[0].shape, lambda i, *_: (0, 0, 0))
    across = pl.BlockSpec((1, block), lambda i, *_: (0, i))
    down = pl.BlockSpec((block, features), lambda i, *_: (i, 0))
    turned = pl.BlockSpec((features, block), lambda i, *_: (0, i))
    kv_shape = (len(kvs), 2, rows, features)
    return pl.pallas_call(
        functools.partial(
            attend_back_kernel, sources=sources, tile=tile, last=last, peer_count=len(grads[0])
        ),
        grid_spec=pltpu.PrefetchScalarGridSpec(
            num_scalar_prefetch=3,
            grid=(steps,),
            in_specs=[
                across,
                across,
                pl.BlockSpec((heads, block), lambda i, *_: (0, i)),
                down,
                turned,
            ]
            + [whole] * len(kvs)
            + [fixed(pieces[0].shape)] * len(pieces)
            + ([turned] if last else []),
            out_specs=[
                down if last else turned,
                pl.BlockSpec(kv_shape, lambda i, *_: (0, 0, 0, 0)),
            ],
            scratch_shapes=[
                pltpu.VMEM((features, block), jnp.float32),
                pltpu.VMEM(kv_shape, jnp.float32),
            ],
        ),
        out_shape=[
            jax.ShapeDtypeStruct((rows, features), jnp.bfloat16)
            if last
            else jax.ShapeDtypeStruct((features, rows), jnp.float32),
            jax.ShapeDtypeStruct(kv_shape, jnp.float32 if last else jnp.bfloat16),
        ],
        compiler_params=pltpu.CompilerParams(vmem_limit_bytes=40 * MIB),
        cost_estimate=pl.CostEstimate(
            flops=rows * (8192 if last else 2048) * 1152,
            bytes_accessed=10 * MIB,
            transcendentals=0,
        ),
    )(
        lows, highs, spot, firsts, lengths, logs, query, wide, *kvs, *pieces,
        *([started] if last else []),
    )


def key_ranges(my_images, wide_images, image_count, tile, block):
    images = jnp.arange(image_count, dtype=jnp.int32)
    before = jnp.sum((wide_images[None, :] < images[:, None]).astype(jnp.int32), axis=1)
    amount = jnp.sum((wide_images[None, :] == images[:, None]).astype(jnp.int32), axis=1)
    mine = (my_images[None, :] == images[:, None]).astype(jnp.int32)
    firsts = jnp.sum(mine * before[:, None], axis=0)
    lengths = jnp.sum(mine * amount[:, None], axis=0)
    ends = firsts + lengths
    lows = firsts[::block] // tile
    highs = (ends[block - 1 :: block] + tile - 1) // tile
    return lows, highs, firsts[None, :], lengths[None, :]


def cost(flops, moved):
    return pl.CostEstimate(flops=int(flops), bytes_accessed=int(moved), transcendentals=0)


def normed_rows(values):
    center = values - jnp.mean(values, axis=-1, keepdims=True)
    inverse = lax.rsqrt(jnp.mean(center * center, axis=-1, keepdims=True) + EPSILON)
    return center * inverse, inverse


def spread(hot_ref, table_ref):
    return jnp.dot(hot_ref[...], table_ref[...], preferred_element_type=jnp.float32)


def add_image_sums(sum_ref, spot, hot_ref, image_count, values):
    hot = hot_ref[:, :image_count]
    first = values.astype(jnp.bfloat16)
    second = (values - first.astype(jnp.float32)).astype(jnp.bfloat16)
    for part in (first, second):
        sum_ref[spot] += lax.dot_general(
            hot, part, (((0,), (0,)), ((), ())), preferred_element_type=jnp.float32
        )


def clear_at_start(*refs):
    @pl.when(pl.program_id(0) == 0)
    def _():
        for ref in refs:
            ref[...] = jnp.zeros_like(ref)


def fixed(shape):
    return pl.BlockSpec(shape, lambda i, *_: (0,) * len(shape))


def down(rows, width, base=0):
    return pl.BlockSpec((rows, width), lambda i, *_: (base + i, 0))


def column(table_rows, width, component):
    return pl.BlockSpec((None, table_rows, width), lambda i, *_: (component, 0, 0))


def shaped(shape, kind=jnp.bfloat16):
    return jax.ShapeDtypeStruct(shape, kind)


def hand_out(spot_ref, outs, values):
    rows = outs[0].shape[0]
    amount = values.shape[0] // rows
    for place in range(amount):
        target = pl.program_id(0) * amount + place
        piece = values[place * rows : (place + 1) * rows, :].astype(outs[0].dtype)
        for mask, out in enumerate(outs):

            @pl.when(target == spot_ref[0] ^ mask)
            def _(out=out, piece=piece):
                out[...] = piece


def grid_with(spot_count, grid, in_specs, out_specs):
    return pltpu.PrefetchScalarGridSpec(
        num_scalar_prefetch=spot_count, grid=grid, in_specs=in_specs, out_specs=out_specs
    )


def project_kernel(
    token_ref, hot_ref, shift_ref, scale_ref, weight_ref, bias_ref, hidden_out, query_out, kv_out
):
    normed, _ = normed_rows(token_ref[...].astype(jnp.float32))
    hidden = normed * (1.0 + spread(hot_ref, scale_ref)) + spread(hot_ref, shift_ref)
    hidden = hidden.astype(jnp.bfloat16)
    hidden_out[...] = hidden

    def projected(c):
        product = jnp.dot(hidden, weight_ref[c], preferred_element_type=jnp.float32)
        if c != 1:
            product = product + bias_ref[c // 2 : c // 2 + 1, :].astype(jnp.float32)
        return product.astype(jnp.bfloat16)

    kv_out[0] = projected(1)
    kv_out[1] = projected(2)
    query_out[...] = projected(0)


def project(tokens, hot, table, weight, bias, block):
    rows, width = tokens.shape
    features = weight.shape[2]
    high = table.shape[1]
    return pl.pallas_call(
        project_kernel,
        grid=(rows // block,),
        in_specs=[
            down(block, width),
            down(block, hot.shape[1]),
            column(high, width, 0),
            column(high, width, 1),
            fixed(weight.shape),
            fixed(bias.shape),
        ],
        out_specs=[
            down(block, width),
            down(block, features),
            pl.BlockSpec((2, block, features), lambda i: (0, i, 0)),
        ],
        out_shape=[
            shaped((rows, width)),
            shaped((rows, features)),
            shaped((2, rows, features)),
        ],
        compiler_params=pltpu.CompilerParams(vmem_limit_bytes=32 * MIB),
        cost_estimate=cost(6 * rows * width * features, 8 * MIB),
    )(tokens, hot, table, table, weight, bias)


def grad_act_kernel(cot_ref, hot_ref, gate_ref, weight_ref, grad_out, act_out, bias_out):
    clear_at_start(bias_out)
    grad = (spread(hot_ref, gate_ref) * cot_ref[...].astype(jnp.float32)).astype(jnp.bfloat16)
    grad_out[...] = grad
    bias_out[...] += jnp.sum(grad.astype(jnp.float32), axis=0, keepdims=True)
    act_out[...] = rows_dot(grad, weight_ref[...])


def grad_act_of(cotangent, hot, table, weight, block):
    rows, width = cotangent.shape
    units = weight.shape[0]
    return pl.pallas_call(
        grad_act_kernel,
        grid=(rows // block,),
        in_specs=[
            down(block, width),
            down(block, hot.shape[1]),
            column(table.shape[1], width, 5),
            fixed(weight.shape),
        ],
        out_specs=[down(block, width), down(block, units), fixed((1, width))],
        out_shape=[
            shaped((rows, width)),
            shaped((rows, units), jnp.float32),
            shaped((1, width), jnp.float32),
        ],
        compiler_params=pltpu.CompilerParams(vmem_limit_bytes=32 * MIB),
        cost_estimate=cost(2 * rows * width * units, 12 * MIB),
    )(cotangent, hot, table, weight)


def middle_kernel(spot_ref, *refs, count, image_count):
    pieces, out_refs = refs[:count], refs[count : 2 * count]
    (
        token_ref, hot_ref, gate_ref, shift_ref, scale_ref, out_bias_ref, up_ref, up_bias_ref,
        grad_act_ref, attn_out, hidden_out, act_out, grad_out, sum_out, bias_out,
    ) = refs[2 * count : -count]
    clear_at_start(sum_out, bias_out)
    attn = out_bias_ref[...].astype(jnp.float32)
    for piece, out_ref in zip(pieces, out_refs):
        attn = attn + jnp.dot(piece[...], out_ref[...], preferred_element_type=jnp.float32)
    attn_out[...] = attn
    middle = token_ref[...].astype(jnp.float32) + spread(hot_ref, gate_ref) * attn
    normed, _ = normed_rows(middle)
    hidden = normed * (1.0 + spread(hot_ref, scale_ref)) + spread(hot_ref, shift_ref)
    hidden = hidden.astype(jnp.bfloat16)
    hidden_out[...] = hidden
    pre = jnp.dot(hidden, up_ref[...], preferred_element_type=jnp.float32)
    pre = pre + up_bias_ref[...].astype(jnp.float32)
    square = pre * pre
    bend = jnp.tanh(ROOT * pre * (1.0 + CUBIC * square))
    half = 0.5 * (1.0 + bend)
    act_out[...] = (pre * half).astype(jnp.bfloat16)
    slope = half + 0.5 * ROOT * pre * (1.0 - bend * bend) * (1.0 + 3.0 * CUBIC * square)
    grad = (grad_act_ref[...] * slope).astype(jnp.bfloat16)
    grad_out[...] = grad
    bias_out[...] += jnp.sum(grad.astype(jnp.float32), axis=0, keepdims=True)
    part = rows_dot(grad, up_ref[...])
    hand_out(spot_ref, refs[-count:], part)
    add_image_sums(sum_out, 0, hot_ref, image_count, part)
    add_image_sums(sum_out, 1, hot_ref, image_count, part * normed)


def middle_of(
    spot, pieces, tokens, hot, table, out_full, out_bias, up_weight, up_bias, grad_act,
    image_count, block, chunk,
):
    rows, features = pieces[0].shape
    width, units = up_weight.shape
    high = table.shape[1]
    count = len(pieces)
    base = chunk * (rows // block)
    return pl.pallas_call(
        functools.partial(middle_kernel, count=count, image_count=image_count),
        grid_spec=grid_with(
            1,
            (rows // block,),
            [down(block, features)] * count
            + [fixed((features, width))] * count
            + [
                down(block, width, base),
                down(block, hot.shape[1], base),
                column(high, width, 2),
                column(high, width, 3),
                column(high, width, 4),
                fixed(out_bias.shape),
                fixed(up_weight.shape),
                fixed(up_bias.shape),
                down(block, units, base),
            ],
            [
                down(block, width),
                down(block, width),
                down(block, units),
                down(block, units),
                fixed((2, image_count, width)),
                fixed((1, units)),
            ]
            + [fixed((rows // count, width))] * count,
        ),
        out_shape=[
            shaped((rows, width), jnp.float32),
            shaped((rows, width)),
            shaped((rows, units)),
            shaped((rows, units)),
            shaped((2, image_count, width), jnp.float32),
            shaped((1, units), jnp.float32),
        ]
        + [shaped((rows // count, width))] * count,
        compiler_params=pltpu.CompilerParams(vmem_limit_bytes=48 * MIB),
        cost_estimate=cost(6 * rows * width * units, 16 * MIB),
    )(
        spot, *pieces, *out_full, tokens, hot, table, table, table, out_bias, up_weight, up_bias,
        grad_act,
    )


def mlp_kernel(spot_ref, act_ref, weight_ref, cot_ref, hot_ref, sum_out, *outs, image_count):
    clear_at_start(sum_out)
    part = jnp.dot(act_ref[...], weight_ref[...], preferred_element_type=jnp.float32)
    hand_out(spot_ref, outs, part)
    add_image_sums(sum_out, 0, hot_ref, image_count, part * cot_ref[...].astype(jnp.float32))


def mlp_of(spot, act, weight, cotangent, hot, image_count, block, chunk, count):
    rows, units = act.shape
    width = weight.shape[1]
    base = chunk * (rows // block)
    return pl.pallas_call(
        functools.partial(mlp_kernel, image_count=image_count),
        grid_spec=grid_with(
            1,
            (rows // block,),
            [
                down(block, units),
                fixed(weight.shape),
                down(block, width, base),
                down(block, hot.shape[1], base),
            ],
            [fixed((1, image_count, width))] + [fixed((rows // count, width))] * count,
        ),
        out_shape=[shaped((1, image_count, width), jnp.float32)]
        + [shaped((rows // count, width))] * count,
        compiler_params=pltpu.CompilerParams(vmem_limit_bytes=32 * MIB),
        cost_estimate=cost(2 * rows * width * units, 8 * MIB),
    )(spot, act, weight, cotangent, hot)


def norm_back_rows(gradient, normed, inverse):
    return (
        gradient
        - jnp.mean(gradient, axis=-1, keepdims=True)
        - normed * jnp.mean(gradient * normed, axis=-1, keepdims=True)
    ) * inverse


def sum_of(pieces):
    total = pieces[0][...].astype(jnp.float32)
    for piece in pieces[1:]:
        total = total + piece[...].astype(jnp.float32)
    return total


def grad_middle_kernel(spot_ref, *refs, count, image_count):
    pieces, out_refs = refs[:count], refs[count : 2 * count]
    (
        attn_ref, token_ref, cot_ref, hot_ref, gate_ref, scale_ref, middle_out, attn_out, sum_out,
        bias_out,
    ) = refs[2 * count : -count]
    gate = spread(hot_ref, gate_ref)
    attn = attn_ref[...]
    normed, inverse = normed_rows(token_ref[...].astype(jnp.float32) + gate * attn)
    gradient = sum_of(pieces) * (1.0 + spread(hot_ref, scale_ref))
    grad_middle = cot_ref[...].astype(jnp.float32) + norm_back_rows(gradient, normed, inverse)
    middle_out[...] = grad_middle
    grad_attn = (gate * grad_middle).astype(jnp.bfloat16)
    attn_out[...] = grad_attn
    for out_ref, block_out in zip(out_refs, refs[-count:]):
        block_out[...] = rows_dot(grad_attn, out_ref[...]).astype(jnp.bfloat16)
    bias_out[...] = jnp.sum(grad_attn.astype(jnp.float32), axis=0, keepdims=True)
    sum_out[...] = jnp.zeros_like(sum_out)
    add_image_sums(sum_out, 0, hot_ref, image_count, grad_middle * attn)


def owned(rows, width, base):
    return pl.BlockSpec((rows, width), lambda i, spot: (base + spot[0], 0))


def grad_middle_of(spot, pieces, attn, tokens, cotangent, hot, table, out_full, image_count, chunk):
    rows, width = pieces[0].shape
    features = out_full[0].shape[0]
    high = table.shape[1]
    count = len(pieces)
    base = chunk * count
    return pl.pallas_call(
        functools.partial(grad_middle_kernel, count=count, image_count=image_count),
        grid_spec=grid_with(
            1,
            (1,),
            [fixed((rows, width))] * count
            + [fixed((features, width))] * count
            + [
                owned(rows, width, 0),
                owned(rows, width, base),
                owned(rows, width, base),
                owned(rows, hot.shape[1], base),
                column(high, width, 2),
                column(high, width, 4),
            ],
            [
                fixed((rows, width)),
                fixed((rows, width)),
                fixed((1, image_count, width)),
                fixed((1, width)),
            ]
            + [fixed((rows, features))] * count,
        ),
        out_shape=[
            shaped((rows, width), jnp.float32),
            shaped((rows, width)),
            shaped((1, image_count, width), jnp.float32),
            shaped((1, width), jnp.float32),
        ]
        + [shaped((rows, features))] * count,
        compiler_params=pltpu.CompilerParams(vmem_limit_bytes=32 * MIB),
        cost_estimate=cost(2 * rows * width * width, 5 * MIB),
    )(spot, *pieces, *out_full, attn, tokens, cotangent, hot, table, table)


def layer_out_kernel(spot_ref, *refs, count):
    pieces = refs[:count]
    attn_ref, token_ref, hot_ref, gate_ref, gate_two_ref, bias_ref, rows_out = refs[count:]
    middle = token_ref[...].astype(jnp.float32) + spread(hot_ref, gate_ref) * attn_ref[...]
    mlp = sum_of(pieces) + bias_ref[...].astype(jnp.float32)
    rows_out[...] = (middle + spread(hot_ref, gate_two_ref) * mlp).astype(jnp.bfloat16)


def layer_out_of(spot, pieces, attn, tokens, hot, table, bias, chunk):
    rows, width = pieces[0].shape
    high = table.shape[1]
    base = chunk * len(pieces)
    return pl.pallas_call(
        functools.partial(layer_out_kernel, count=len(pieces)),
        grid_spec=pltpu.PrefetchScalarGridSpec(
            num_scalar_prefetch=1,
            grid=(1,),
            in_specs=[fixed((rows, width))] * len(pieces)
            + [
                owned(rows, width, 0),
                owned(rows, width, base),
                owned(rows, hot.shape[1], base),
                column(high, width, 2),
                column(high, width, 5),
                fixed(bias.shape),
            ],
            out_specs=fixed((rows, width)),
        ),
        out_shape=shaped((rows, width)),
        compiler_params=pltpu.CompilerParams(vmem_limit_bytes=16 * MIB),
        cost_estimate=cost(rows * width * 64, 3 * MIB),
    )(spot, *pieces, attn, tokens, hot, table, table, bias)


def grad_tokens_kernel(spot_ref, *refs, count):
    pieces = refs[:count]
    token_ref, hot_ref, scale_ref, middle_ref, rows_out = refs[count:]
    normed, inverse = normed_rows(token_ref[...].astype(jnp.float32))
    gradient = sum_of(pieces) * (1.0 + spread(hot_ref, scale_ref))
    rows_out[...] = (middle_ref[...] + norm_back_rows(gradient, normed, inverse)).astype(
        jnp.bfloat16
    )


def grad_tokens_of(spot, pieces, tokens, hot, table, grad_middle, chunk):
    rows, width = pieces[0].shape
    base = chunk * len(pieces)
    return pl.pallas_call(
        functools.partial(grad_tokens_kernel, count=len(pieces)),
        grid_spec=pltpu.PrefetchScalarGridSpec(
            num_scalar_prefetch=1,
            grid=(1,),
            in_specs=[fixed((rows, width))] * len(pieces)
            + [
                owned(rows, width, base),
                owned(rows, hot.shape[1], base),
                column(table.shape[1], width, 1),
                fixed((rows, width)),
            ],
            out_specs=fixed((rows, width)),
        ),
        out_shape=shaped((rows, width)),
        compiler_params=pltpu.CompilerParams(vmem_limit_bytes=16 * MIB),
        cost_estimate=cost(rows * width * 64, 3 * MIB),
    )(spot, *pieces, tokens, hot, table, grad_middle)


def grad_hidden_kernel(
    spot_ref, query_ref, near_ref, after_ref, before_ref, weight_ref, token_ref, hot_ref, kv_out,
    sum_out, bias_out, *outs, image_count,
):
    clear_at_start(sum_out, bias_out)
    normed, _ = normed_rows(token_ref[...].astype(jnp.float32))
    query = query_ref[...]
    part = rows_dot(query, weight_ref[0])
    bias_out[0:1] += jnp.sum(query.astype(jnp.float32), axis=0, keepdims=True)
    for c in range(2):
        total = (
            near_ref[0, c]
            + after_ref[c].astype(jnp.float32)
            + before_ref[c].astype(jnp.float32)
        ).astype(jnp.bfloat16)
        kv_out[c] = total
        part = part + rows_dot(total, weight_ref[c + 1])
        if c == 1:
            bias_out[1:2] += jnp.sum(total.astype(jnp.float32), axis=0, keepdims=True)
    hand_out(spot_ref, outs, part)
    add_image_sums(sum_out, 0, hot_ref, image_count, part)
    add_image_sums(sum_out, 1, hot_ref, image_count, part * normed)


def grad_hidden_of(
    spot, query, near, after, before, weight, tokens, hot, image_count, block, chunk, chunks, count
):
    rows, features = query.shape
    rows = rows // chunks
    width = tokens.shape[1]
    base = chunk * (rows // block)
    pair = pl.BlockSpec((2, block, features), lambda i, *_: (0, base + i, 0))
    return pl.pallas_call(
        functools.partial(grad_hidden_kernel, image_count=image_count),
        grid_spec=grid_with(
            1,
            (rows // block,),
            [
                down(block, features, base),
                pl.BlockSpec((1, 2, block, features), lambda i, *_: (0, 0, base + i, 0)),
                pair,
                pair,
                fixed(weight.shape),
                down(block, width, base),
                down(block, hot.shape[1], base),
            ],
            [
                pl.BlockSpec((2, block, features), lambda i, *_: (0, i, 0)),
                fixed((2, image_count, width)),
                fixed((2, features)),
            ]
            + [fixed((rows // count, width))] * count,
        ),
        out_shape=[
            shaped((2, rows, features)),
            shaped((2, image_count, width), jnp.float32),
            shaped((2, features), jnp.float32),
        ]
        + [shaped((rows // count, width))] * count,
        compiler_params=pltpu.CompilerParams(vmem_limit_bytes=32 * MIB),
        cost_estimate=cost(6 * rows * width * features, 8 * MIB),
    )(spot, query, near, after, before, weight, tokens, hot)


def place_kernel(spot_ref, *refs, count, held):
    out = refs[-1]
    place = pl.program_id(0) % count
    for c in range(held):
        for mask in range(count):

            @pl.when(
                (place == spot_ref[0] ^ mask) & (pl.program_id(0) // count == c)
            )
            def _(piece=refs[c * count + mask]):
                out[...] = piece[...].astype(out.dtype)


def place_rows(spot, chunks, kind, total=None, base=0, before=None):
    count = len(chunks[0])
    rows, width = chunks[0][0].shape
    pieces = [piece for chunk in chunks for piece in chunk]
    total = total or len(pieces) * rows
    extra = [] if before is None else [before]
    return pl.pallas_call(
        functools.partial(place_kernel, count=count, held=len(chunks)),
        grid_spec=grid_with(
            1,
            (len(pieces),),
            [fixed((rows, width))] * len(pieces) + [pl.BlockSpec(memory_space=pl.ANY)] * len(extra),
            pl.BlockSpec((rows, width), lambda i, *_: (base + i, 0)),
        ),
        out_shape=shaped((total, width), kind),
        input_output_aliases={1 + len(pieces): 0} if extra else {},
        compiler_params=pltpu.CompilerParams(vmem_limit_bytes=16 * MIB),
        cost_estimate=cost(0, 4 * MIB),
    )(spot, *pieces, *extra)


def turned_dot(left, right):
    return lax.dot_general(
        left, right, (((0,), (0,)), ((), ())), preferred_element_type=jnp.float32
    )


def mlp_weights_kernel(grad_ref, *refs, chunks):
    hidden, pre, act = refs[:chunks], refs[chunks : 2 * chunks], refs[2 * chunks : 3 * chunks]
    out = refs[-1]
    units = pre[0].shape[1]
    rows = pre[0].shape[0]
    up, low = 0.0, 0.0
    for c in range(chunks):
        up = up + turned_dot(hidden[c][...], pre[c][...])
        low = low + turned_dot(grad_ref[c * rows : (c + 1) * rows, :], act[c][...])
    out[:, :units] = up.astype(jnp.bfloat16)
    out[:, units:] = low.astype(jnp.bfloat16)


def mlp_weights(grad_mlp, hidden, pre, act):
    rows, width = grad_mlp.shape
    chunks = len(hidden)
    units = pre[0].shape[1]
    if units % 128:
        joined = [jnp.concatenate(parts, axis=0) for parts in (hidden, pre, act)]
        sides = [turned_dot(joined[0], joined[1]), turned_dot(grad_mlp, joined[2])]
        return jnp.concatenate([side.astype(jnp.bfloat16) for side in sides], axis=1)
    part = width // 3
    across = lambda high: pl.BlockSpec((high, part), lambda i: (0, i))
    return pl.pallas_call(
        functools.partial(mlp_weights_kernel, chunks=chunks),
        grid=(3,),
        in_specs=[across(rows)]
        + [across(rows // chunks)] * chunks
        + [fixed((rows // chunks, units))] * (2 * chunks),
        out_specs=pl.BlockSpec((part, 2 * units), lambda i: (i, 0)),
        out_shape=shaped((width, 2 * units)),
        compiler_params=pltpu.CompilerParams(vmem_limit_bytes=48 * MIB),
        cost_estimate=cost(4 * rows * width * units, 16 * MIB),
    )(grad_mlp, *hidden, *pre, *act)


def attn_weights_kernel(grad_ref, hidden_ref, query_ref, *refs, chunks):
    attended, kv, out = refs[:chunks], refs[chunks : 2 * chunks], refs[-1]
    rows = attended[0].shape[0]
    hidden = hidden_ref[...]
    parts = [0.0, turned_dot(hidden, query_ref[...]), 0.0, 0.0]
    for c in range(chunks):
        mine = slice(c * rows, (c + 1) * rows)
        parts[0] = parts[0] + turned_dot(grad_ref[mine, :], attended[c][...])
        for k in range(2):
            parts[2 + k] = parts[2 + k] + turned_dot(hidden_ref[mine, :], kv[c][k])
    out[...] = jnp.concatenate([part.astype(jnp.bfloat16) for part in parts], axis=1)


def attn_weights(grad_attn, hidden, grad_query, attended, grad_kv):
    rows, width = hidden.shape
    chunks = len(attended)
    features = grad_query.shape[1]
    part = width // 3
    across = pl.BlockSpec((rows, part), lambda i: (0, i))
    return pl.pallas_call(
        functools.partial(attn_weights_kernel, chunks=chunks),
        grid=(3,),
        in_specs=[across, across, fixed(grad_query.shape)]
        + [fixed(attended[0].shape)] * chunks
        + [fixed(grad_kv[0].shape)] * chunks,
        out_specs=pl.BlockSpec((part, 4 * features), lambda i: (i, 0)),
        out_shape=shaped((width, 4 * features)),
        compiler_params=pltpu.CompilerParams(vmem_limit_bytes=48 * MIB),
        cost_estimate=cost(8 * rows * width * features, 12 * MIB),
    )(grad_attn, hidden, grad_query, *attended, *grad_kv)


def on_device(
    tokens,
    conditioning,
    image_index,
    qkv_weight,
    qv_bias,
    out_weight,
    out_bias,
    up_weight,
    up_bias,
    down_weight,
    down_bias,
    ada_weight,
    ada_bias,
    cotangent,
):
    row_count, width = tokens.shape
    feature_count = qkv_weight.shape[2]
    head_size = lax.axis_size("head")
    me = lax.axis_index("head")
    spot = me.astype(jnp.int32).reshape(1)
    my_index = lax.axis_index("seq")
    image_count = conditioning.shape[0]
    columns = ada_weight.shape[2]
    my_images = lax.dynamic_slice_in_dim(image_index, my_index * row_count, row_count, 0)
    edge = jnp.full((row_count,), -1, jnp.int32)
    padded_images = jnp.concatenate([edge, image_index, edge + (image_count + 1)])
    wide_images = lax.dynamic_slice_in_dim(padded_images, my_index * row_count, 3 * row_count, 0)
    ranges = key_ranges(my_images, wide_images, image_count, KEY_TILE, QUERY_BLOCK)
    images = jnp.tile(jnp.arange(image_count, dtype=jnp.int32), 3)
    hot = (my_images[:, None] == images[None, :]).astype(jnp.bfloat16)

    cond_float = conditioning.astype(jnp.float32)
    cond_act = jax.nn.silu(cond_float).astype(jnp.bfloat16)
    mod_mine = jnp.einsum("id,dkf->kif", cond_act, ada_weight, preferred_element_type=jnp.float32)
    mod_mine = mod_mine + ada_bias.astype(jnp.float32)[:, None]
    mod_pieces = gather_pieces(mod_mine, "head")
    modulation = jnp.concatenate([pick(me ^ j, mod_pieces) for j in range(head_size)], axis=2)
    table = jnp.concatenate(three_parts(modulation), axis=1)
    out_full = gather_pieces(out_weight, "head")

    weight = qkv_weight.transpose(1, 0, 2)
    hidden_one, query, key_value = project(tokens, hot, table, weight, qv_bias, ROW_BLOCK)
    kv_before = step_along(key_value, "seq", True)
    kv_after = step_along(key_value, "seq", False)
    grad_mlp, grad_act, grad_down_bias = grad_act_of(
        cotangent, hot, table, down_weight, ROW_BLOCK
    )
    kvs = [kv_before, key_value, kv_after]
    attended, attended_wide, logs = zip(
        *[
            attend(*ranges, query, kvs, KEY_TILE, QUERY_BLOCK, c, CHUNKS)
            for c in range(CHUNKS)
        ]
    )
    attended_wide = jnp.concatenate(attended_wide, axis=1)
    logs = jnp.concatenate(logs, axis=1)

    out_bias = out_bias[None]
    up_bias = up_bias[None]
    attn, hidden_two, act, grad_pre, late_sums, up_sums, hidden_pieces = [], [], [], [], [], [], []
    for c in range(CHUNKS):
        got = middle_of(
            spot, gather_pieces(attended[c], "head"), tokens, hot, table, out_full, out_bias,
            up_weight, up_bias, grad_act, image_count, ROW_BLOCK, c,
        )
        for values, kept in zip((attn, hidden_two, act, grad_pre, late_sums, up_sums), got):
            values.append(kept)
        hidden_pieces.append(swap_pieces(got[6:], "head"))

    grad_middle, grad_attn, grad_attended, gate_sums, out_sums = [], [], [], [], []
    for c in range(CHUNKS):
        got = grad_middle_of(
            spot, hidden_pieces[c], attn[c], tokens, cotangent, hot, table, out_full,
            image_count, c,
        )
        grad_middle.append(got[0])
        grad_attn.append(gather_pieces(got[1], "head"))
        gate_sums.append(got[2])
        out_sums.append(got[3])
        grad_attended.append(swap_pieces(got[4:], "head"))

    query_started, kv_far = attend_back(
        spot, ranges, logs, query, grad_attended, attended_wide, [kv_before, kv_after], (0, 2),
        KEY_TILE, QUERY_BLOCK,
    )
    from_after = step_along(kv_far[0], "seq", False)
    from_before = step_along(kv_far[1], "seq", True)
    grad_query, kv_near = attend_back(
        spot, ranges, logs, query, grad_attended, attended_wide, [key_value], (1,),
        KEY_TILE, QUERY_BLOCK, started=query_started,
    )

    grad_kv, first_sums, qv_sums, one_pieces = [], [], [], []
    for c in range(CHUNKS):
        got = grad_hidden_of(
            spot, grad_query, kv_near, from_after, from_before, weight, tokens, hot, image_count,
            ROW_BLOCK, c, CHUNKS, head_size,
        )
        grad_kv.append(got[0])
        first_sums.append(got[1])
        qv_sums.append(got[2])
        one_pieces.append(swap_pieces(got[3:], "head"))
    grad_tokens = None
    for c in range(CHUNKS):
        rows = grad_tokens_of(spot, one_pieces[c], tokens, hot, table, grad_middle[c], c)
        grad_tokens = place_rows(
            spot, [gather_pieces(rows, "head")], jnp.float32, row_count, c * head_size, grad_tokens
        )

    mlp_sums, out_rows = [], []
    for c in range(CHUNKS):
        got = mlp_of(
            spot, act[c], down_weight, cotangent, hot, image_count, ROW_BLOCK, c, head_size
        )
        mlp_sums.append(got[0])
        rows = layer_out_of(
            spot, swap_pieces(got[1:], "head"), attn[c], tokens, hot, table, down_bias[None], c
        )
        out_rows.append(gather_pieces(rows, "head"))
    layer_out = place_rows(spot, out_rows, jnp.bfloat16)

    def own_columns(values):
        return [values[:, j * columns : (j + 1) * columns] for j in range(head_size)]

    def to_owners(values):
        parts = own_columns(values)
        return sum(swap_pieces([pick(me ^ mask, parts) for mask in range(head_size)], "head"))

    late = jnp.concatenate(
        [sum(gate_sums)[0], sum(late_sums).reshape(2 * image_count, width)]
        + [sum(mlp_sums)[0], sum(out_sums)],
        axis=0,
    )
    cot_sums = lax.dot_general(
        hot[:, :image_count], cotangent, (((0,), (0,)), ((), ())),
        preferred_element_type=jnp.float32,
    )
    cot_sums = pick(me, own_columns(cot_sums * down_bias.astype(jnp.float32)[None]))
    late_mine = to_owners(late) + jnp.pad(cot_sums, ((3 * image_count, 1), (0, 0)))
    late_mine = butterfly_sum(late_mine, "seq")
    low_bias = butterfly_sum(jnp.concatenate([sum(up_sums), grad_down_bias], axis=1), "seq")[0]
    units = up_weight.shape[1]
    grad_up_bias, grad_down_bias = low_bias[:units], low_bias[units:]
    first_mine = to_owners(sum(first_sums).reshape(2 * image_count, width))
    first_mine = butterfly_sum(jnp.concatenate([first_mine, sum(qv_sums)], axis=0), "seq")
    grad_qv_bias = first_mine[2 * image_count :]
    grad_mod = jnp.concatenate(
        [first_mine[: 2 * image_count], late_mine[: 4 * image_count]], axis=0
    ).reshape(6, image_count, columns)
    grad_ada_bias = jnp.sum(grad_mod, axis=1)
    grad_ada_weight = jnp.einsum(
        "id,kif->dkf", cond_act.astype(jnp.float32), grad_mod, precision=PRECISE
    )
    grad_cond_act = jnp.einsum(
        "kif,dkf->id", grad_mod, ada_weight.astype(jnp.float32), precision=PRECISE
    )
    out_sum = late_mine[4 * image_count :]
    spread_bias = jnp.concatenate(
        [jnp.where(me == j, out_sum, 0.0) for j in range(head_size)], axis=1
    )
    last = butterfly_sum(jnp.concatenate([grad_cond_act, spread_bias], axis=0), "head")
    _, silu_pull = jax.vjp(jax.nn.silu, cond_float)
    grad_conditioning = silu_pull(last[:image_count])[0]
    grad_out_bias = last[image_count]

    mlp_total = lax.psum_scatter(
        mlp_weights(grad_mlp, hidden_two, grad_pre, act), "seq", scatter_dimension=0, tiled=True
    ).astype(jnp.float32)
    attn_total = lax.psum_scatter(
        attn_weights(
            place_rows(spot, grad_attn, jnp.bfloat16), hidden_one, grad_query, attended, grad_kv
        ),
        "seq", scatter_dimension=0, tiled=True,
    ).astype(jnp.float32)
    return (
        layer_out,
        grad_tokens,
        grad_conditioning,
        attn_total[:, feature_count:].reshape(-1, 3, feature_count),
        grad_qv_bias,
        attn_total[:, :feature_count].T,
        grad_out_bias,
        mlp_total[:, :units],
        grad_up_bias,
        mlp_total[:, units:].T,
        grad_down_bias,
        grad_ada_weight,
        grad_ada_bias,
    )


def solution(mesh):
    placed = (
        P("seq", None),
        P(),
        P(),
        P(None, None, "head"),
        P(None, "head"),
        P("head", None),
        P(),
        P(None, "head"),
        P("head"),
        P("head", None),
        P(),
        P(None, None, "head"),
        P(None, "head"),
        P("seq", None),
    )
    return jax.shard_map(
        on_device,
        mesh=mesh,
        in_specs=placed,
        out_specs=(
            P("seq", None),
            P("seq", None),
            P(),
            P("seq", None, "head"),
            P(None, "head"),
            P("head", "seq"),
            P(),
            P("seq", "head"),
            P("head"),
            P("head", "seq"),
            P(),
            P(None, None, "head"),
            P(None, "head"),
        ),
        check_vma=False,
    )
```

```python
import functools

import jax
import jax.numpy as jnp
from jax import lax
from jax.experimental import pallas as pl
from jax.experimental.pallas import tpu as pltpu
from jax.sharding import PartitionSpec as P

HDIM = 72


EPSILON = 1e-06
MASKED = -1e30
PRECISE = lax.Precision.HIGHEST
CHUNKS = 2
KEY_TILE = 512
QUERY_BLOCK = 256
ROW_BLOCK = 256
ROOT = 0.7978845608028654
CUBIC = 0.044715
LOG2E = 1.4426950408889634
MIB = 1 << 20
PACE = 1.15e9


def peers(axis):
    return range(1, lax.axis_size(axis))


def swap(value, axis, mask):
    count = lax.axis_size(axis)
    return lax.ppermute(value, axis, [(i, i ^ mask) for i in range(count)])


def gather_pieces(value, axis):
    return [value] + [swap(value, axis, mask) for mask in peers(axis)]


def fold_pieces(stack, axis):
    amount = stack.shape[0]
    while amount > 1:
        amount //= 2
        stack = stack[:amount] + swap(stack[amount:], axis, amount)
    return stack[0]


def swap_pieces(pieces, axis):
    return [pieces[0]] + [swap(pieces[mask], axis, mask) for mask in peers(axis)]


def butterfly_sum(value, axis):
    mask = 1
    while mask < lax.axis_size(axis):
        value = value + swap(value, axis, mask)
        mask *= 2
    return value


def step_along(value, axis, ahead):
    count = lax.axis_size(axis)
    pairs = [(i, i + 1) if ahead else (i + 1, i) for i in range(count - 1)]
    return lax.ppermute(value, axis, pairs)


def three_parts(values):
    first = lax.reduce_precision(values, 8, 7)
    second = lax.reduce_precision(values - first, 8, 7)
    third = values - first - second
    return [part.astype(jnp.bfloat16) for part in (first, second, third)]


def pick(which, cases):
    result = cases[0]
    for number, case in enumerate(cases[1:], 1):
        result = jnp.where(which == number, case, result)
    return result


def tied_call(
    kernel, prefetch, operands, after, *, grid, in_specs, out_specs, out_shape, vmem, cost,
    scratch_shapes=(), into=(),
):
    after = [*into, *after]
    count, ties = len(prefetch), len(after)

    def body(*refs):
        return kernel(*refs[:count], *refs[count + ties :])

    return pl.pallas_call(
        body,
        grid_spec=pltpu.PrefetchScalarGridSpec(
            num_scalar_prefetch=count,
            grid=grid,
            in_specs=[pl.BlockSpec(memory_space=pl.ANY)] * ties + in_specs,
            out_specs=out_specs,
            scratch_shapes=scratch_shapes,
        ),
        out_shape=out_shape,
        input_output_aliases={count + number: number for number in range(len(into))},
        compiler_params=pltpu.CompilerParams(vmem_limit_bytes=vmem * MIB),
        cost_estimate=cost,
    )(*prefetch, *after, *operands)


def cost(micros):
    return pl.CostEstimate(
        flops=max(1, int(micros * PACE)), bytes_accessed=1, transcendentals=0
    )


def fixed(shape):
    return pl.BlockSpec(shape, lambda i, *_: (0,) * len(shape))


def held(shape):
    return pl.BlockSpec(
        shape, lambda i, *_: (0,) * len(shape), pipeline_mode=pl.Buffered(buffer_count=1)
    )


def down(rows, width, base=0):
    return pl.BlockSpec((rows, width), lambda i, *_: (base + i, 0))


def owned(rows, width, base):
    return pl.BlockSpec((rows, width), lambda i, spot: (base + spot[0], 0))


def column(table_rows, width, component):
    return pl.BlockSpec(
        (None, table_rows, width),
        lambda i, *_: (component, 0, 0),
        pipeline_mode=pl.Buffered(buffer_count=1),
    )


def whole_lanes(width):
    return -(-width // 128) * 128


def shaped(shape, kind=jnp.bfloat16):
    return jax.ShapeDtypeStruct(shape, kind)


def rows_dot(left, right):
    return lax.dot_general(
        left, right, (((1,), (1,)), ((), ())), preferred_element_type=jnp.float32
    )


def turned_dot(left, right):
    return lax.dot_general(
        left, right, (((0,), (0,)), ((), ())), preferred_element_type=jnp.float32
    )


def normed_rows(values):
    center = values - jnp.mean(values, axis=-1, keepdims=True)
    inverse = lax.rsqrt(jnp.mean(center * center, axis=-1, keepdims=True) + EPSILON)
    return center * inverse, inverse


def norm_back_rows(gradient, normed, inverse):
    return (
        gradient
        - jnp.mean(gradient, axis=-1, keepdims=True)
        - normed * jnp.mean(gradient * normed, axis=-1, keepdims=True)
    ) * inverse


def spread(hot_ref, table_ref):
    return jnp.dot(hot_ref[...], table_ref[...], preferred_element_type=jnp.float32)


def add_image_sums(sum_ref, spot, hot_ref, image_count, values):
    hot = hot_ref[:, :image_count]
    first = values.astype(jnp.bfloat16)
    second = (values - first.astype(jnp.float32)).astype(jnp.bfloat16)
    sum_ref[spot] += turned_dot(hot, first) + turned_dot(hot, second)


def clear_at_start(*refs):
    @pl.when(pl.program_id(0) == 0)
    def _():
        for ref in refs:
            ref[...] = jnp.zeros_like(ref)


def hand_out(spot_ref, outs, values, own):
    amount = values.shape[0] // own
    for place in range(amount):
        target = pl.program_id(0) * amount + place
        piece = values[place * own : (place + 1) * own, :].astype(outs[0].dtype)
        rows = pl.ds(pl.multiple_of(target // len(outs) * own, own), own)
        for mask, out in enumerate(outs):

            @pl.when(target % len(outs) == spot_ref[0] ^ mask)
            def _(out=out, piece=piece, rows=rows):
                out[rows, :] = piece


def sum_of(pieces):
    total = pieces[0][...].astype(jnp.float32)
    for piece in pieces[1:]:
        total = total + piece[...].astype(jnp.float32)
    return total


def head_window(place, features):
    start = place // 128 * 128
    return slice(start, min(features, start + 256))


def head_only(block, place):
    lanes = head_window(place, block.shape[1])
    window = block[:, lanes]
    lane = lax.broadcasted_iota(jnp.int32, window.shape, 1) + (lanes.start - place)
    return jnp.where((lane >= 0) & (lane < HDIM), window, jnp.zeros_like(window))


def visible_keys(first_ref, length_ref, base, tile_rows):
    first = first_ref[...] - base
    place = lax.broadcasted_iota(jnp.int32, (tile_rows, first.shape[1]), 0)
    offset = place - first
    return (offset >= 0) & (offset < length_ref[...])


def each_tile(low, high, source, tiles, body):
    lax.fori_loop(
        jnp.maximum(low, source * tiles),
        jnp.minimum(high, (source + 1) * tiles),
        lambda number, carry: body(number, carry),
        0,
    )


def attend_kernel(
    low_ref, high_ref, first_ref, length_ref, query_ref, *refs, tile, step_base
):
    kv_refs = refs[:3]
    low_out, wide_out, log_out, total, row_max, row_sum = refs[3:]
    features = query_ref.shape[1]
    heads = features // HDIM
    step = pl.program_id(0) + step_base
    queries = [head_only(query_ref[...], head * HDIM) for head in range(heads)]
    rescale = HDIM ** (-0.5) * LOG2E
    value_start = features // 128 * 128
    total[...] = jnp.zeros_like(total)
    row_max[...] = jnp.full_like(row_max, MASKED)
    row_sum[...] = jnp.zeros_like(row_sum)
    for source, kv_ref in enumerate(kv_refs):
        tiles = kv_ref.shape[0] // tile

        def body(number, carry, source=source, kv_ref=kv_ref, tiles=tiles):
            rows = pl.ds(pl.multiple_of((number - source * tiles) * tile, tile), tile)
            keys = kv_ref[rows, :features]
            values = kv_ref[rows, value_start:].astype(jnp.float32).T
            seen = visible_keys(first_ref, length_ref, number * tile, tile)
            for head in range(heads):
                scores = rows_dot(keys[:, head_window(head * HDIM, features)], queries[head])
                scores = jnp.where(seen, scores, MASKED)
                old = row_max[head : head + 1, :]
                new = jnp.maximum(old, jnp.max(scores, axis=0, keepdims=True))
                shrink = jnp.exp2((old - new) * rescale)
                shares = jnp.exp2((scores - new) * rescale)
                row_max[head : head + 1, :] = new
                row_sum[head : head + 1, :] = row_sum[
                    head : head + 1, :
                ] * shrink + jnp.sum(shares, axis=0, keepdims=True)
                mine = slice(head * HDIM, (head + 1) * HDIM)
                place = features - value_start + head * HDIM
                total[mine, :] = total[mine, :] * shrink + jnp.dot(
                    values[place : place + HDIM, :].astype(jnp.bfloat16),
                    shares.astype(jnp.bfloat16),
                    preferred_element_type=jnp.float32,
                )
            return carry

        each_tile(low_ref[step], high_ref[step], source, tiles, body)
    log_out[...] = row_max[...] * rescale + jnp.log2(row_sum[...])
    for head in range(heads):
        mine = slice(head * HDIM, (head + 1) * HDIM)
        total[mine, :] = total[mine, :] / row_sum[head : head + 1, :]
    wide_out[...] = total[...]
    low_out[...] = total[...].T.astype(jnp.bfloat16)


def attend(ranges, query, kvs, tile, block, chunk, chunks, after):
    lows, highs, firsts, lengths = ranges
    rows, features = query.shape
    heads = features // HDIM
    amount = rows // chunks
    steps = amount // block
    base = chunk * steps
    across = pl.BlockSpec((1, block), lambda i, *_: (0, base + i))
    return tied_call(
        functools.partial(attend_kernel, tile=tile, step_base=base),
        (lows, highs),
        (firsts, lengths, query, *kvs),
        after,
        grid=(steps,),
        in_specs=[across, across, down(block, features, base)] + [held(kvs[0].shape)] * 3,
        out_specs=[
            down(block, features),
            pl.BlockSpec((features, block), lambda i, *_: (0, i)),
            pl.BlockSpec((heads, block), lambda i, *_: (0, i)),
        ],
        out_shape=[
            shaped((amount, features)),
            shaped((features, amount), jnp.float32),
            shaped((heads, amount), jnp.float32),
        ],
        scratch_shapes=[
            pltpu.VMEM((features, block), jnp.float32),
            pltpu.VMEM((heads, block), jnp.float32),
            pltpu.VMEM((heads, block), jnp.float32),
        ],
        vmem=16,
        cost=cost(10),
    )


def attend_back_steps(
    step, low_ref, high_ref, first_ref, length_ref, log_ref, query_ref, grad_rows, wide, kv_refs,
    sources, total, kv_totals, tile,
):
    features = query_ref.shape[1]
    heads = features // HDIM
    rescale = HDIM ** (-0.5) * LOG2E
    queries = [head_only(query_ref[...], head * HDIM) for head in range(heads)]
    shifted = jnp.concatenate([jnp.zeros_like(grad_rows), grad_rows], axis=1)
    grads = [head_only(shifted, features + head * HDIM) for head in range(heads)]
    products = grad_rows.astype(jnp.float32).T * wide
    deltas = [
        jnp.sum(products[head * HDIM : (head + 1) * HDIM, :], axis=0, keepdims=True)
        for head in range(heads)
    ]
    for source, kv_ref, kv_total in zip(sources, kv_refs, kv_totals):
        tiles = kv_ref.shape[0] // tile

        def body(number, carry, source=source, kv_ref=kv_ref, kv_total=kv_total, tiles=tiles):
            rows = pl.ds(pl.multiple_of((number - source * tiles) * tile, tile), tile)
            pairs = kv_ref[rows, :]
            keys_down = kv_ref[rows, :features].astype(jnp.float32).T
            seen = visible_keys(first_ref, length_ref, number * tile, tile)
            for head in range(heads):
                key_lanes = head_window(head * HDIM, features)
                value_lanes = head_window(features + head * HDIM, 2 * features)
                scores = rows_dot(pairs[:, key_lanes], queries[head])
                shares = jnp.where(
                    seen, jnp.exp2(scores * rescale - log_ref[head : head + 1, :]), 0.0
                )
                grad_shares = rows_dot(pairs[:, value_lanes], grads[head])
                grad_scores = (shares * (grad_shares - deltas[head])).astype(jnp.bfloat16)
                kv_total[rows, value_lanes] += jnp.dot(
                    shares.astype(jnp.bfloat16), grads[head], preferred_element_type=jnp.float32
                )
                kv_total[rows, key_lanes] += jnp.dot(
                    grad_scores, queries[head], preferred_element_type=jnp.float32
                )
                mine = slice(head * HDIM, (head + 1) * HDIM)
                total[mine, :] += jnp.dot(
                    keys_down[mine, :].astype(jnp.bfloat16),
                    grad_scores,
                    preferred_element_type=jnp.float32,
                )
            return carry

        each_tile(low_ref[step], high_ref[step], source, tiles, body)


def write_pairs(out, kv_total, features):
    values = kv_total[...]
    lane = lax.broadcasted_iota(jnp.int32, values.shape, 1)
    out[...] = jnp.where(lane < features, values * HDIM ** (-0.5), values).astype(out.dtype)


def attend_far_kernel(
    low_ref, high_ref, spot_ref, first_ref, length_ref, log_ref, query_ref, wide_ref, before_ref,
    after_ref, *refs, tile, count,
):
    pieces = refs[:-7]
    query_out, grad_out, before_out, after_out, total, before_total, after_total = refs[-7:]
    step = pl.program_id(0)
    block, features = query_ref.shape
    piece_rows = pieces[0].shape[0]
    clear_at_start(before_total, after_total)
    total[...] = jnp.zeros_like(total)
    parts = []
    for place in range(block // piece_rows):
        target = step * (block // piece_rows) + place
        part = jnp.zeros_like(pieces[0][...])
        for number, piece in enumerate(pieces):
            owner = (spot_ref[0] ^ (number % count)) + number // count * count
            part = jnp.where(target == owner, piece[...], part)
        parts.append(part)
    grad_rows = jnp.concatenate(parts, axis=0)
    grad_out[...] = grad_rows
    attend_back_steps(
        step, low_ref, high_ref, first_ref, length_ref, log_ref, query_ref, grad_rows,
        wide_ref[...], (before_ref, after_ref), (0, 2), total, (before_total, after_total), tile,
    )
    query_out[...] = total[...]

    @pl.when(step == pl.num_programs(0) - 1)
    def _():
        write_pairs(before_out, before_total, features)
        write_pairs(after_out, after_total, features)


def attend_near_kernel(
    low_ref, high_ref, first_ref, length_ref, log_ref, query_ref, wide_ref, kv_ref, grad_ref,
    start_ref, query_out, kv_out, total, kv_total, *, tile,
):
    step = pl.program_id(0)
    clear_at_start(kv_total)
    total[...] = start_ref[...]
    attend_back_steps(
        step, low_ref, high_ref, first_ref, length_ref, log_ref, query_ref, grad_ref[...],
        wide_ref[...], (kv_ref,), (1,), total, (kv_total,), tile,
    )
    query_out[...] = (total[...].T * HDIM ** (-0.5)).astype(query_out.dtype)

    @pl.when(step == pl.num_programs(0) - 1)
    def _():
        write_pairs(kv_out, kv_total, query_ref.shape[1])


def attend_far(spot, ranges, logs, query, grads, wide, before, later, tile, block, after):
    lows, highs, firsts, lengths = ranges
    pieces = [piece for chunk in grads for piece in chunk]
    rows, features = query.shape
    across = pl.BlockSpec((1, block), lambda i, *_: (0, i))
    turned = pl.BlockSpec((features, block), lambda i, *_: (0, i))
    logged = pl.BlockSpec((features // HDIM, block), lambda i, *_: (0, i))
    pairs = (rows, whole_lanes(2 * features))
    return tied_call(
        functools.partial(attend_far_kernel, tile=tile, count=len(grads[0])),
        (lows, highs, spot),
        (firsts, lengths, logs, query, wide, before, later, *pieces),
        after,
        grid=(rows // block,),
        in_specs=[across, across, logged, down(block, features), turned, held(pairs), held(pairs)]
        + [held(pieces[0].shape)] * len(pieces),
        out_specs=[turned, down(block, features), fixed(pairs), fixed(pairs)],
        out_shape=[
            shaped((features, rows), jnp.float32),
            shaped((rows, features)),
            shaped(pairs),
            shaped(pairs),
        ],
        scratch_shapes=[
            pltpu.VMEM((features, block), jnp.float32),
            pltpu.VMEM(pairs, jnp.float32),
            pltpu.VMEM(pairs, jnp.float32),
        ],
        vmem=28,
        cost=cost(8),
    )


def attend_near(ranges, logs, query, grad, wide, kv, started, tile, block, after):
    lows, highs, firsts, lengths = ranges
    rows, features = query.shape
    across = pl.BlockSpec((1, block), lambda i, *_: (0, i))
    turned = pl.BlockSpec((features, block), lambda i, *_: (0, i))
    logged = pl.BlockSpec((features // HDIM, block), lambda i, *_: (0, i))
    pairs = (rows, whole_lanes(2 * features))
    return tied_call(
        functools.partial(attend_near_kernel, tile=tile),
        (lows, highs),
        (firsts, lengths, logs, query, wide, kv, grad, started),
        after,
        grid=(rows // block,),
        in_specs=[
            across, across, logged, down(block, features), turned, held(pairs),
            down(block, features), turned,
        ],
        out_specs=[down(block, features), fixed(pairs)],
        out_shape=[shaped((rows, features)), shaped(pairs, jnp.float32)],
        scratch_shapes=[
            pltpu.VMEM((features, block), jnp.float32),
            pltpu.VMEM(pairs, jnp.float32),
        ],
        vmem=24,
        cost=cost(16),
    )


def key_ranges(my_images, wide_images, image_count, tile, block):
    images = jnp.arange(image_count, dtype=jnp.int32)
    before = jnp.sum((wide_images[None, :] < images[:, None]).astype(jnp.int32), axis=1)
    amount = jnp.sum((wide_images[None, :] == images[:, None]).astype(jnp.int32), axis=1)
    mine = (my_images[None, :] == images[:, None]).astype(jnp.int32)
    firsts = jnp.sum(mine * before[:, None], axis=0)
    lengths = jnp.sum(mine * amount[:, None], axis=0)
    ends = firsts + lengths
    lows = firsts[::block] // tile
    highs = (ends[block - 1 :: block] + tile - 1) // tile
    return lows, highs, firsts[None, :], lengths[None, :]


def project_kernel(
    token_ref, hot_ref, shift_ref, scale_ref, weight_ref, bias_ref, hidden_out, query_out, kv_out
):
    features = query_out.shape[1]
    normed, _ = normed_rows(token_ref[...].astype(jnp.float32))
    hidden = normed * (1.0 + spread(hot_ref, scale_ref)) + spread(hot_ref, shift_ref)
    hidden = hidden.astype(jnp.bfloat16)
    hidden_out[...] = hidden
    projected = jnp.dot(hidden, weight_ref[...], preferred_element_type=jnp.float32)
    projected = (projected + bias_ref[...]).astype(jnp.bfloat16)
    query_out[...] = projected[:, :features]
    spare = kv_out.shape[1] - 2 * features
    empty = jnp.zeros((projected.shape[0], spare), projected.dtype)
    kv_out[...] = jnp.concatenate([projected[:, features:], empty][: 1 + (spare > 0)], axis=1)


def project(tokens, hot, table, weight, bias, block, after):
    rows, width = tokens.shape
    features = weight.shape[1] // 3
    high = table.shape[1]
    return tied_call(
        project_kernel,
        (),
        (tokens, hot, table, table, weight, bias),
        after,
        grid=(rows // block,),
        in_specs=[
            down(block, width),
            down(block, hot.shape[1]),
            column(high, width, 0),
            column(high, width, 1),
            held(weight.shape),
            held(bias.shape),
        ],
        out_specs=[
            down(block, width),
            down(block, features),
            down(block, whole_lanes(2 * features)),
        ],
        out_shape=[
            shaped((rows, width)),
            shaped((rows, features)),
            shaped((rows, whole_lanes(2 * features))),
        ],
        vmem=20,
        cost=cost(6),
    )


def grad_act_kernel(
    cot_ref, hot_ref, gate_ref, weight_ref, grad_out, act_out, bias_out, sum_out, *, image_count
):
    clear_at_start(bias_out, sum_out)
    cot = cot_ref[...]
    grad = (spread(hot_ref, gate_ref) * cot.astype(jnp.float32)).astype(jnp.bfloat16)
    grad_out[...] = grad
    bias_out[...] += jnp.sum(grad.astype(jnp.float32), axis=0, keepdims=True)
    sum_out[...] += turned_dot(hot_ref[:, :image_count], cot)
    act_out[...] = rows_dot(grad, weight_ref[...])


def grad_act_of(cotangent, hot, table, weight, image_count, block, after):
    rows, width = cotangent.shape
    units = weight.shape[0]
    return tied_call(
        functools.partial(grad_act_kernel, image_count=image_count),
        (),
        (cotangent, hot, table, weight),
        after,
        grid=(rows // block,),
        in_specs=[
            down(block, width),
            down(block, hot.shape[1]),
            column(table.shape[1], width, 5),
            held(weight.shape),
        ],
        out_specs=[
            down(block, width),
            down(block, units),
            fixed((1, width)),
            fixed((image_count, width)),
        ],
        out_shape=[
            shaped((rows, width)),
            shaped((rows, units), jnp.float32),
            shaped((1, width), jnp.float32),
            shaped((image_count, width), jnp.float32),
        ],
        vmem=20,
        cost=cost(5),
    )


def peer_rows(spot_ref, mask, rows):
    return pl.ds(pl.multiple_of((spot_ref[0] ^ mask) * rows, rows), rows)


def middle_kernel(spot_ref, *refs, count, image_count):
    pieces = refs[:count]
    (
        out_ref, token_ref, hot_ref, gate_ref, shift_ref, scale_ref, out_bias_ref, up_ref,
        up_bias_ref, grad_act_ref, attn_out, hidden_out, act_out, grad_out, sum_out, bias_out,
    ) = refs[count:-count]
    clear_at_start(sum_out, bias_out)
    attn = out_bias_ref[...].astype(jnp.float32)
    for mask, piece in enumerate(pieces):
        rows = peer_rows(spot_ref, mask, piece.shape[1])
        attn = attn + jnp.dot(piece[...], out_ref[rows, :], preferred_element_type=jnp.float32)
    attn_out[...] = attn
    middle = token_ref[...].astype(jnp.float32) + spread(hot_ref, gate_ref) * attn
    normed, _ = normed_rows(middle)
    hidden = normed * (1.0 + spread(hot_ref, scale_ref)) + spread(hot_ref, shift_ref)
    hidden = hidden.astype(jnp.bfloat16)
    hidden_out[...] = hidden
    pre = jnp.dot(hidden, up_ref[...], preferred_element_type=jnp.float32)
    pre = pre + up_bias_ref[...].astype(jnp.float32)
    square = pre * pre
    bend = jnp.tanh(ROOT * pre * (1.0 + CUBIC * square))
    half = 0.5 * (1.0 + bend)
    act_out[...] = (pre * half).astype(jnp.bfloat16)
    slope = half + 0.5 * ROOT * pre * (1.0 - bend * bend) * (1.0 + 3.0 * CUBIC * square)
    grad = (grad_act_ref[...] * slope).astype(jnp.bfloat16)
    grad_out[...] = grad
    bias_out[...] += jnp.sum(grad.astype(jnp.float32), axis=0, keepdims=True)
    part = rows_dot(grad, up_ref[...])
    hand_out(spot_ref, refs[-count:], part, refs[-1].shape[0])
    add_image_sums(sum_out, 0, hot_ref, image_count, part)
    add_image_sums(sum_out, 1, hot_ref, image_count, part * normed)


def middle_of(
    spot, pieces, tokens, hot, table, out_full, out_bias, up_weight, up_bias, grad_act,
    image_count, block, chunk, into, after,
):
    rows, features = pieces[0].shape
    width, units = up_weight.shape
    whole = tokens.shape[0]
    high = table.shape[1]
    count = len(pieces)
    base = chunk * (rows // block)
    return tied_call(
        functools.partial(middle_kernel, count=count, image_count=image_count),
        (spot,),
        (
            *pieces, out_full, tokens, hot, table, table, table, out_bias, up_weight, up_bias,
            grad_act,
        ),
        after,
        grid=(rows // block,),
        in_specs=[down(block, features)] * count
        + [
            held(out_full.shape),
            down(block, width, base),
            down(block, hot.shape[1], base),
            column(high, width, 2),
            column(high, width, 3),
            column(high, width, 4),
            held(out_bias.shape),
            held(up_weight.shape),
            held(up_bias.shape),
            down(block, units, base),
        ],
        out_specs=[
            down(block, width, base),
            down(block, width, base),
            down(block, units, base),
            down(block, units, base),
            fixed((2, image_count, width)),
            fixed((1, units)),
        ]
        + [fixed((rows // count, width))] * count,
        into=into,
        out_shape=[
            shaped((whole, width), jnp.float32),
            shaped((whole, width)),
            shaped((whole, units)),
            shaped((whole, units)),
            shaped((2, image_count, width), jnp.float32),
            shaped((1, units), jnp.float32),
        ]
        + [shaped((rows // count, width))] * count,
        vmem=36,
        cost=cost(12),
    )


def mlp_kernel(act_ref, weight_ref, cot_ref, hot_ref, part_out, sum_out, *, image_count):
    clear_at_start(sum_out)
    part = jnp.dot(act_ref[...], weight_ref[...], preferred_element_type=jnp.float32)
    part_out[...] = part.astype(jnp.bfloat16)
    add_image_sums(sum_out, 0, hot_ref, image_count, part * cot_ref[...].astype(jnp.float32))


def mlp_of(act, weight, cotangent, hot, image_count, block, after):
    rows, units = act.shape
    width = weight.shape[1]
    return tied_call(
        functools.partial(mlp_kernel, image_count=image_count),
        (),
        (act, weight, cotangent, hot),
        after,
        grid=(rows // block,),
        in_specs=[
            down(block, units),
            held(weight.shape),
            down(block, width),
            down(block, hot.shape[1]),
        ],
        out_specs=[down(block, width), fixed((1, image_count, width))],
        out_shape=[shaped((rows, width)), shaped((1, image_count, width), jnp.float32)],
        vmem=20,
        cost=cost(6),
    )


def grad_middle_kernel(spot_ref, *refs, count, image_count):
    pieces = refs[:count]
    (
        out_ref, attn_ref, token_ref, cot_ref, hot_ref, gate_ref, scale_ref, middle_out, attn_out,
        sum_out, bias_out,
    ) = refs[count:-count]
    gate = spread(hot_ref, gate_ref)
    attn = attn_ref[...]
    normed, inverse = normed_rows(token_ref[...].astype(jnp.float32) + gate * attn)
    gradient = sum_of(pieces) * (1.0 + spread(hot_ref, scale_ref))
    grad_middle = cot_ref[...].astype(jnp.float32) + norm_back_rows(gradient, normed, inverse)
    middle_out[...] = grad_middle
    grad_attn = (gate * grad_middle).astype(jnp.bfloat16)
    attn_out[...] = grad_attn
    for mask, block_out in enumerate(refs[-count:]):
        rows = peer_rows(spot_ref, mask, block_out.shape[1])
        block_out[...] = rows_dot(grad_attn, out_ref[rows, :]).astype(jnp.bfloat16)
    bias_out[...] = jnp.sum(grad_attn.astype(jnp.float32), axis=0, keepdims=True)
    sum_out[...] = jnp.zeros_like(sum_out)
    add_image_sums(sum_out, 0, hot_ref, image_count, grad_middle * attn)


def grad_middle_of(
    spot, pieces, attn, tokens, cotangent, hot, table, out_full, image_count, chunk, after
):
    rows, width = pieces[0].shape
    features = out_full.shape[0] // len(pieces)
    high = table.shape[1]
    count = len(pieces)
    base = chunk * count
    return tied_call(
        functools.partial(grad_middle_kernel, count=count, image_count=image_count),
        (spot,),
        (*pieces, out_full, attn, tokens, cotangent, hot, table, table),
        after,
        grid=(1,),
        in_specs=[held((rows, width))] * count
        + [
            held(out_full.shape),
            owned(rows, width, base),
            owned(rows, width, base),
            owned(rows, width, base),
            owned(rows, hot.shape[1], base),
            column(high, width, 2),
            column(high, width, 4),
        ],
        out_specs=[
            fixed((rows, width)),
            fixed((rows, width)),
            fixed((1, image_count, width)),
            fixed((1, width)),
        ]
        + [fixed((rows, features))] * count,
        out_shape=[
            shaped((rows, width), jnp.float32),
            shaped((rows, width)),
            shaped((1, image_count, width), jnp.float32),
            shaped((1, width), jnp.float32),
        ]
        + [shaped((rows, features))] * count,
        vmem=16,
        cost=cost(4),
    )


def layer_out_kernel(
    mlp_ref, attn_ref, token_ref, hot_ref, gate_ref, gate_two_ref, bias_ref, rows_out
):
    middle = token_ref[...].astype(jnp.float32) + spread(hot_ref, gate_ref) * attn_ref[...]
    mlp = mlp_ref[...].astype(jnp.float32) + bias_ref[...].astype(jnp.float32)
    rows_out[...] = (middle + spread(hot_ref, gate_two_ref) * mlp).astype(jnp.bfloat16)


def layer_out_of(mlp, attn, tokens, hot, table, bias, block, after):
    rows, width = tokens.shape
    high = table.shape[1]
    return tied_call(
        layer_out_kernel,
        (),
        (mlp, attn, tokens, hot, table, table, bias),
        after,
        grid=(rows // block,),
        in_specs=[
            down(block, width),
            down(block, width),
            down(block, width),
            down(block, hot.shape[1]),
            column(high, width, 2),
            column(high, width, 5),
            held(bias.shape),
        ],
        out_specs=down(block, width),
        out_shape=shaped((rows, width)),
        vmem=20,
        cost=cost(4),
    )


def owned_chunks(rows, width, count):
    return pl.BlockSpec((rows, width), lambda c, spot: (c * count + spot[0], 0))


def grad_tokens_kernel(spot_ref, *refs, count):
    pieces = refs[:count]
    token_ref, hot_ref, scale_ref, *middle_refs, rows_out = refs[count:]
    normed, inverse = normed_rows(token_ref[...].astype(jnp.float32))
    gradient = sum_of(pieces) * (1.0 + spread(hot_ref, scale_ref))
    middle = pick(pl.program_id(0), [middle_ref[...] for middle_ref in middle_refs])
    rows_out[...] = (middle + norm_back_rows(gradient, normed, inverse)).astype(jnp.bfloat16)


def grad_tokens_of(spot, pieces, tokens, hot, table, grad_middle, after):
    chunks = len(grad_middle)
    rows, width = grad_middle[0].shape
    count = len(pieces)
    return tied_call(
        functools.partial(grad_tokens_kernel, count=count),
        (spot,),
        (*pieces, tokens, hot, table, *grad_middle),
        after,
        grid=(chunks,),
        in_specs=[down(rows, width)] * count
        + [
            owned_chunks(rows, width, count),
            owned_chunks(rows, hot.shape[1], count),
            column(table.shape[1], width, 1),
        ]
        + [held((rows, width))] * chunks,
        out_specs=down(rows, width),
        out_shape=shaped((rows * chunks, width)),
        vmem=12,
        cost=cost(4),
    )


def grad_hidden_kernel(
    spot_ref, query_ref, near_ref, later_ref, before_ref, weight_ref, token_ref, hot_ref, all_out,
    sum_out, bias_out, *outs, image_count, own,
):
    clear_at_start(sum_out, bias_out)
    normed, _ = normed_rows(token_ref[...].astype(jnp.float32))
    pairs = (
        near_ref[...] + later_ref[...].astype(jnp.float32) + before_ref[...].astype(jnp.float32)
    ).astype(jnp.bfloat16)
    features = query_ref.shape[1]
    grad = jnp.concatenate([query_ref[...], pairs[:, : 2 * features]], axis=1)
    all_out[...] = grad
    bias_out[...] += jnp.sum(grad.astype(jnp.float32), axis=0, keepdims=True)
    part = rows_dot(grad, weight_ref[...])
    hand_out(spot_ref, outs, part, own)
    add_image_sums(sum_out, 0, hot_ref, image_count, part)
    add_image_sums(sum_out, 1, hot_ref, image_count, part * normed)


def grad_hidden_of(
    spot, query, near, later, before, weight, tokens, hot, image_count, block, own, count, after
):
    rows, features = query.shape
    width = tokens.shape[1]
    pair = down(block, whole_lanes(2 * features))
    return tied_call(
        functools.partial(grad_hidden_kernel, image_count=image_count, own=own),
        (spot,),
        (query, near, later, before, weight, tokens, hot),
        after,
        grid=(rows // block,),
        in_specs=[
            down(block, features),
            pair,
            pair,
            pair,
            held(weight.shape),
            down(block, width),
            down(block, hot.shape[1]),
        ],
        out_specs=[
            down(block, 3 * features),
            fixed((2, image_count, width)),
            fixed((1, 3 * features)),
        ]
        + [fixed((rows // count, width))] * count,
        out_shape=[
            shaped((rows, 3 * features)),
            shaped((2, image_count, width), jnp.float32),
            shaped((1, 3 * features), jnp.float32),
        ]
        + [shaped((rows // count, width))] * count,
        vmem=20,
        cost=cost(8),
    )


def place_kernel(spot_ref, *refs, chunks):
    out, pieces = refs[-1], refs[:-1]
    own = out.shape[0]
    for c in range(chunks):
        for mask, piece in enumerate(pieces):

            @pl.when(pl.program_id(0) == (spot_ref[0] ^ mask) + c * len(pieces))
            def _(piece=piece, c=c):
                out[...] = piece[c * own : (c + 1) * own, :].astype(out.dtype)


def place_rows(spot, pieces, chunks, kind, after):
    rows, width = pieces[0].shape
    own = rows // chunks
    return tied_call(
        functools.partial(place_kernel, chunks=chunks),
        (spot,),
        pieces,
        after,
        grid=(len(pieces) * chunks,),
        in_specs=[held((rows, width))] * len(pieces),
        out_specs=down(own, width),
        out_shape=shaped((rows * len(pieces), width), kind),
        vmem=12,
        cost=cost(3),
    )


def split_kernel(spot_ref, *refs, sizes, kept, count):
    values, place = [], 0
    for size in sizes:
        values.append(sum_of(refs[place : place + size]))
        place += size
    values = jnp.concatenate(values, axis=0)
    columns = values.shape[1] // count
    split_out, kept_out = refs[-2:]
    for mask in range(count):
        result = values[:, :columns]
        for j in range(1, count):
            result = jnp.where(
                spot_ref[0] ^ mask == j, values[:, j * columns : (j + 1) * columns], result
            )
        split_out[mask] = result
    rows = []
    for size in kept:
        value = sum_of(refs[place : place + size])
        place += size
        for j in range(value.shape[1] // columns):
            rows.append(value[:, j * columns : (j + 1) * columns])
    kept_out[...] = jnp.concatenate(rows, axis=0)


def split_columns(spot, groups, kept, count, after):
    operands = [value for group in groups + kept for value in group]
    rows = sum(group[0].shape[0] for group in groups)
    columns = operands[0].shape[1] // count
    shapes = [
        (count, rows, columns),
        (sum(group[0].shape[1] for group in kept) // columns, columns),
    ]
    return tied_call(
        functools.partial(
            split_kernel,
            sizes=[len(group) for group in groups],
            kept=[len(group) for group in kept],
            count=count,
        ),
        (spot,),
        operands,
        after,
        grid=(1,),
        in_specs=[held(value.shape) for value in operands],
        out_specs=[fixed(shape) for shape in shapes],
        out_shape=[shaped(shape, jnp.float32) for shape in shapes],
        vmem=12,
        cost=cost(1),
    )


def mlp_weights_kernel(hidden_ref, grad_ref, pre_ref, act_ref, *refs):
    own_refs, own_out, out = refs[:-2], refs[-2], refs[-1]
    units = pre_ref.shape[1]
    own = own_refs[0].shape[0]

    @pl.when(pl.program_id(0) == 0)
    def _():
        for c, own_ref in enumerate(own_refs):
            own_out[c * own : (c + 1) * own, :] = own_ref[...]

    out[:, :units] = turned_dot(hidden_ref[...], pre_ref[...]).astype(jnp.bfloat16)
    out[:, units:] = turned_dot(grad_ref[...], act_ref[...]).astype(jnp.bfloat16)


def mlp_weights(grad_mlp, hidden, pre, act, owned_rows, after):
    rows, width = grad_mlp.shape
    units = pre.shape[1]
    if units % 128:
        sides = [turned_dot(hidden, pre), turned_dot(grad_mlp, act)]
        joined = jnp.concatenate([side.astype(jnp.bfloat16) for side in sides], axis=1)
        return jnp.concatenate(owned_rows, axis=0), joined
    part = width // 3
    across = pl.BlockSpec((rows, part), lambda i, *_: (0, i))
    own = owned_rows[0].shape
    all_owned = (own[0] * len(owned_rows), width)
    return tied_call(
        mlp_weights_kernel,
        (),
        (hidden, grad_mlp, pre, act, *owned_rows),
        after,
        grid=(3,),
        in_specs=[across, across, held((rows, units)), held((rows, units))]
        + [held(own)] * len(owned_rows),
        out_specs=[
            fixed(all_owned),
            pl.BlockSpec((part, 2 * units), lambda i, *_: (i, 0)),
        ],
        out_shape=[shaped(all_owned), shaped((width, 2 * units))],
        vmem=28,
        cost=cost(7),
    )


def attn_weights_kernel(spot_ref, side_ref, hidden_ref, *refs, chunks, count, blocks):
    grad_ref, attended = refs[0], refs[1 : 1 + chunks]
    pieces, outs = refs[1 + chunks : 1 + chunks + count], refs[1 + chunks + count :]
    own = pieces[0].shape[0] // chunks
    high, low = turned_dot(hidden_ref[...], grad_ref[...]), 0.0
    for mask, piece in enumerate(pieces):
        place = pl.ds(pl.multiple_of((spot_ref[0] ^ mask) * own, own), own)
        theirs = jnp.concatenate([attended[c][place, :] for c in range(chunks)], axis=0)
        low = low + turned_dot(piece[...], theirs)
    total = jnp.concatenate([low.astype(jnp.bfloat16), high.astype(jnp.bfloat16)], axis=1)
    if not blocks:
        outs[0][...] = total
        return
    size = total.shape[0] // blocks
    for pair in range(blocks // 2):
        left = total[2 * pair * size : (2 * pair + 1) * size, :]
        right = total[(2 * pair + 1) * size : (2 * pair + 2) * size, :]
        outs[0][pair] = jnp.where(side_ref[0] == 0, left, right)
        outs[1][pair] = jnp.where(side_ref[0] == 0, right, left)


def attn_weights(spot, side, hidden, attended, grad, pieces, blocks, after):
    rows, width = hidden.shape
    chunks = len(attended)
    features = attended[0].shape[1]
    operands = (hidden, grad, *attended, *pieces)
    if blocks:
        shapes = [(blocks // 2, width // blocks, 4 * features)] * 2
    else:
        shapes = [(width, 4 * features)]
    return tied_call(
        functools.partial(
            attn_weights_kernel, chunks=chunks, count=len(pieces), blocks=blocks
        ),
        (spot, side),
        operands,
        after,
        grid=(1,),
        in_specs=[held(value.shape) for value in operands],
        out_specs=[fixed(shape) for shape in shapes],
        out_shape=[shaped(shape) for shape in shapes],
        vmem=40,
        cost=cost(7),
    )


def fold_kernel(side_ref, kept_ref, got_ref, keep_out, send_out):
    for pair in range(keep_out.shape[0]):
        left, right = [
            kept_ref[block].astype(jnp.float32) + got_ref[block].astype(jnp.float32)
            for block in (2 * pair, 2 * pair + 1)
        ]
        keep_out[pair] = jnp.where(side_ref[0] == 0, left, right).astype(keep_out.dtype)
        send_out[pair] = jnp.where(side_ref[0] == 0, right, left).astype(send_out.dtype)


def fold_blocks(side, kept, got, after):
    blocks, size, width = kept.shape
    shape = (blocks // 2, size, width)
    return tied_call(
        fold_kernel,
        (side,),
        (kept, got),
        after,
        grid=(1,),
        in_specs=[held(kept.shape)] * 2,
        out_specs=[fixed(shape)] * 2,
        out_shape=[shaped(shape)] * 2,
        vmem=12,
        cost=cost(2),
    )


def attn_total_kernel(*refs, count):
    pieces, (out_out, qkv_out) = refs[:count], refs[count:]
    total = sum_of(pieces)[0]
    features = out_out.shape[0]
    out_out[...] = total[:, :features].T
    for c in range(3):
        qkv_out[c] = total[:, (c + 1) * features : (c + 2) * features]


def attn_total_of(pieces, features, after):
    _, size, width = pieces[0].shape
    return tied_call(
        functools.partial(attn_total_kernel, count=len(pieces)),
        (),
        pieces,
        after,
        grid=(1,),
        in_specs=[held((1, size, width))] * len(pieces),
        out_specs=[fixed((features, size)), fixed((3, size, features))],
        out_shape=[
            shaped((features, size), jnp.float32),
            shaped((3, size, features), jnp.float32),
        ],
        vmem=12,
        cost=cost(1),
    )


def on_device(
    tokens,
    conditioning,
    image_index,
    qkv_weight,
    qv_bias,
    out_weight,
    out_bias,
    up_weight,
    up_bias,
    down_weight,
    down_bias,
    ada_weight,
    ada_bias,
    cotangent,
):
    row_count, width = tokens.shape
    feature_count = qkv_weight.shape[2]
    head_size = lax.axis_size("head")
    me = lax.axis_index("head")
    spot = me.astype(jnp.int32).reshape(1)
    my_index = lax.axis_index("seq")
    seq_size = lax.axis_size("seq")
    side = (my_index % 2).astype(jnp.int32).reshape(1)
    blocks = seq_size if width % (16 * seq_size) == 0 else 0
    image_count = conditioning.shape[0]
    columns = ada_weight.shape[2]
    my_images = lax.dynamic_slice_in_dim(image_index, my_index * row_count, row_count, 0)
    edge = jnp.full((row_count,), -1, jnp.int32)
    padded_images = jnp.concatenate([edge, image_index, edge + (image_count + 1)])
    wide_images = lax.dynamic_slice_in_dim(padded_images, my_index * row_count, 3 * row_count, 0)
    ranges = key_ranges(my_images, wide_images, image_count, KEY_TILE, QUERY_BLOCK)
    images = jnp.tile(jnp.arange(image_count, dtype=jnp.int32), 3)
    hot = (my_images[:, None] == images[None, :]).astype(jnp.bfloat16)

    out_full = lax.all_gather(out_weight, "head", axis=0, tiled=True)
    cond_float = conditioning.astype(jnp.float32)
    cond_act = jax.nn.silu(cond_float).astype(jnp.bfloat16)
    mod_mine = jnp.einsum("id,dkf->kif", cond_act, ada_weight, preferred_element_type=jnp.float32)
    mod_mine = mod_mine + ada_bias.astype(jnp.float32)[:, None]
    mod_pieces = gather_pieces(mod_mine, "head")
    modulation = jnp.concatenate([pick(me ^ j, mod_pieces) for j in range(head_size)], axis=2)
    table = jnp.concatenate(three_parts(modulation), axis=1)

    weight = qkv_weight.reshape(width, 3 * feature_count)
    qv_wide = qv_bias.astype(jnp.float32)
    bias = jnp.concatenate([qv_wide[0], jnp.zeros_like(qv_wide[0]), qv_wide[1]])[None]
    hidden_one, query, kv = project(tokens, hot, table, weight, bias, ROW_BLOCK, [])
    kv_before = step_along(kv, "seq", True)
    kv_after = step_along(kv, "seq", False)
    grad_mlp, grad_act, grad_down_bias, cot_sums = grad_act_of(
        cotangent, hot, table, down_weight, image_count, ROW_BLOCK, [hidden_one]
    )
    kvs = [kv_before, kv, kv_after]
    attended, attended_wide, logs, last = [], [], [], [grad_down_bias]
    for c in range(CHUNKS):
        got = attend(ranges, query, kvs, KEY_TILE, QUERY_BLOCK, c, CHUNKS, last)
        for values, kept in zip((attended, attended_wide, logs), got):
            values.append(kept)
        last = [got[2]]
    attended_wide = jnp.concatenate(attended_wide, axis=1)
    logs = jnp.concatenate(logs, axis=1)

    late_sums, up_sums, hidden_pieces, into, last = [], [], [], [], [logs]
    for c in range(CHUNKS):
        got = middle_of(
            spot, gather_pieces(attended[c], "head"), tokens, hot, table, out_full, out_bias[None],
            up_weight, up_bias[None], grad_act, image_count, ROW_BLOCK, c, into, last,
        )
        into = got[:4]
        late_sums.append(got[4].reshape(2 * image_count, width))
        up_sums.append(got[5])
        hidden_pieces.append(swap_pieces(got[6:], "head"))
        last = []
    attn, hidden_two, act, grad_pre = into
    mlp_part, mlp_sums = mlp_of(
        act, down_weight, cotangent, hot, image_count, ROW_BLOCK, hidden_pieces[0]
    )
    mlp = lax.psum(mlp_part, "head")

    grad_middle, grad_attn, grad_attended, gate_sums, out_sums = [], [], [], [], []
    last = [mlp_sums]
    for c in range(CHUNKS):
        got = grad_middle_of(
            spot, hidden_pieces[c], attn, tokens, cotangent, hot, table, out_full, image_count, c,
            last,
        )
        grad_middle.append(got[0])
        grad_attn.append(got[1])
        gate_sums.append(got[2][0])
        out_sums.append(got[3])
        grad_attended.append(swap_pieces(got[4:], "head"))
        last = [got[3]]
    grad_own, weight_part = mlp_weights(
        grad_mlp, hidden_two, grad_pre, act, grad_attn, last + grad_attended[0]
    )

    query_started, grad_rows, to_before, to_after = attend_far(
        spot, ranges, logs, query, grad_attended, attended_wide, kv_before, kv_after,
        KEY_TILE, QUERY_BLOCK, [grad_own],
    )
    grad_attn = gather_pieces(grad_own, "head")
    from_after = step_along(to_before, "seq", False)
    from_before = step_along(to_after, "seq", True)
    grad_query, kv_near = attend_near(
        ranges, logs, query, grad_rows, attended_wide, kv, query_started, KEY_TILE, QUERY_BLOCK,
        [],
    )

    grad_all, first_sums, qkv_sums, *one_pieces = grad_hidden_of(
        spot, grad_query, kv_near, from_after, from_before, weight, tokens, hot, image_count,
        ROW_BLOCK, row_count // CHUNKS // head_size, head_size, grad_attn,
    )
    one_pieces = swap_pieces(one_pieces, "head")
    attn_part = attn_weights(
        spot, side, hidden_one, attended, grad_all, grad_attn, blocks, []
    )
    layer_out = layer_out_of(
        mlp, attn, tokens, hot, table, down_bias[None], ROW_BLOCK, [attn_part[0]]
    )
    own_tokens = grad_tokens_of(
        spot, one_pieces, tokens, hot, table, grad_middle, [layer_out]
    )
    sum_stack, kept_rows = split_columns(
        spot,
        [[first_sums.reshape(2 * image_count, width)], gate_sums, late_sums, [mlp_sums[0]]]
        + [out_sums],
        [[qkv_sums], up_sums, [grad_down_bias]],
        head_size,
        [own_tokens],
    )
    token_pieces = gather_pieces(own_tokens, "head")
    if blocks:
        kept, sent = attn_part
        mask = 1
        while mask < blocks // 2:
            mask *= 2
            kept, sent = fold_blocks(
                ((my_index // mask) % 2).astype(jnp.int32).reshape(1),
                kept,
                swap(sent, "seq", mask // 2),
                [kept_rows],
            )
        attn_got = [kept, swap(sent, "seq", mask)]
    own_down = lax.dynamic_slice_in_dim(down_bias, me * columns, columns, 0).astype(jnp.float32)
    own_cot = lax.dynamic_slice_in_dim(cot_sums, me * columns, columns, 1) * own_down[None]
    mods = 6 * image_count
    sums = fold_pieces(sum_stack, "head")
    sums = sums + jnp.pad(own_cot, ((5 * image_count, 1), (0, 0)))
    sums = butterfly_sum(jnp.concatenate([sums, kept_rows], axis=0), "seq")
    grad_mod = sums[:mods].reshape(6, image_count, columns)
    out_sum = sums[mods : mods + 1]
    grad_qv_bias = sums[mods + 1 : mods + 4 : 2]
    low_bias = sums[mods + 4 :].reshape(-1)
    units = up_weight.shape[1]
    grad_up_bias, grad_down_bias = low_bias[:units], low_bias[units:]
    mod_parts = jnp.concatenate(three_parts(grad_mod), axis=1)
    grad_cond_act = jnp.einsum(
        "kif,dkf->id", mod_parts, ada_weight, preferred_element_type=jnp.float32
    )
    grad_cond_act = jnp.sum(grad_cond_act.reshape(3, image_count, width), axis=0)
    spread_bias = jnp.concatenate(
        [jnp.where(me == j, out_sum, 0.0) for j in range(head_size)], axis=1
    )
    final = butterfly_sum(jnp.concatenate([grad_cond_act, spread_bias], axis=0), "head")
    _, silu_pull = jax.vjp(jax.nn.silu, cond_float)
    grad_conditioning = silu_pull(final[:image_count])[0]
    grad_out_bias = final[image_count]
    grad_ada_bias = jnp.sum(grad_mod, axis=1)
    grad_ada_weight = jnp.einsum(
        "id,kif->dkf",
        jnp.concatenate([cond_act] * 3, axis=0),
        mod_parts,
        preferred_element_type=jnp.float32,
    )

    grad_tokens = place_rows(spot, token_pieces, CHUNKS, jnp.float32, [])
    mlp_total = lax.psum_scatter(weight_part, "seq", scatter_dimension=0, tiled=True)
    mlp_total = mlp_total.astype(jnp.float32)
    if blocks:
        grad_out_weight, grad_qkv = attn_total_of(attn_got, feature_count, [])
        grad_qkv_weight = grad_qkv.transpose(1, 0, 2)
    else:
        attn_total = lax.psum_scatter(attn_part[0], "seq", scatter_dimension=0, tiled=True)
        attn_total = attn_total.astype(jnp.float32)
        grad_out_weight = attn_total[:, :feature_count].T
        grad_qkv_weight = attn_total[:, feature_count:].reshape(-1, 3, feature_count)
    return (
        layer_out,
        grad_tokens,
        grad_conditioning,
        grad_qkv_weight,
        grad_qv_bias,
        grad_out_weight,
        grad_out_bias,
        mlp_total[:, :units],
        grad_up_bias,
        mlp_total[:, units:].T,
        grad_down_bias,
        grad_ada_weight,
        grad_ada_bias,
    )


def solution(mesh):
    placed = (
        P("seq", None),
        P(),
        P(),
        P(None, None, "head"),
        P(None, "head"),
        P("head", None),
        P(),
        P(None, "head"),
        P("head"),
        P("head", None),
        P(),
        P(None, None, "head"),
        P(None, "head"),
        P("seq", None),
    )
    return jax.shard_map(
        on_device,
        mesh=mesh,
        in_specs=placed,
        out_specs=(
            P("seq", None),
            P("seq", None),
            P(),
            P("seq", None, "head"),
            P(None, "head"),
            P("head", "seq"),
            P(),
            P("seq", "head"),
            P("head"),
            P("head", "seq"),
            P(),
            P(None, None, "head"),
            P(None, "head"),
        ),
        check_vma=False,
    )
```

```python
import functools

import jax
import jax.numpy as jnp
from jax import lax
from jax.experimental import pallas as pl
from jax.experimental.pallas import tpu as pltpu
from jax.sharding import PartitionSpec as P

HDIM = 72


EPSILON = 1e-06
MASKED = -1e30
PRECISE = lax.Precision.HIGHEST
CHUNKS = 2
KEY_TILE = 512
QUERY_BLOCK = 256
ROW_BLOCK = 256
ROOT = 0.7978845608028654
CUBIC = 0.044715
LOG2E = 1.4426950408889634
MIB = 1 << 20
PACE = 1.15e9


def peers(axis):
    return range(1, lax.axis_size(axis))


def swap(value, axis, mask):
    count = lax.axis_size(axis)
    return lax.ppermute(value, axis, [(i, i ^ mask) for i in range(count)])


def gather_pieces(value, axis):
    return [value] + [swap(value, axis, mask) for mask in peers(axis)]


def fold_pieces(stack, axis):
    amount = stack.shape[0]
    while amount > 1:
        amount //= 2
        stack = stack[:amount] + swap(stack[amount:], axis, amount)
    return stack[0]


def swap_pieces(pieces, axis):
    return [pieces[0]] + [swap(pieces[mask], axis, mask) for mask in peers(axis)]


def butterfly_sum(value, axis):
    mask = 1
    while mask < lax.axis_size(axis):
        value = value + swap(value, axis, mask)
        mask *= 2
    return value


def step_along(value, axis, ahead):
    count = lax.axis_size(axis)
    pairs = [(i, i + 1) if ahead else (i + 1, i) for i in range(count - 1)]
    return lax.ppermute(value, axis, pairs)


def three_parts(values):
    first = lax.reduce_precision(values, 8, 7)
    second = lax.reduce_precision(values - first, 8, 7)
    third = values - first - second
    return [part.astype(jnp.bfloat16) for part in (first, second, third)]


def pick(which, cases):
    result = cases[0]
    for number, case in enumerate(cases[1:], 1):
        result = jnp.where(which == number, case, result)
    return result


def tied_call(
    kernel, prefetch, operands, after, *, grid, in_specs, out_specs, out_shape, vmem, cost,
    scratch_shapes=(), into=(),
):
    after = [*into, *after]
    count, ties = len(prefetch), len(after)

    def body(*refs):
        return kernel(*refs[:count], *refs[count + ties :])

    return pl.pallas_call(
        body,
        grid_spec=pltpu.PrefetchScalarGridSpec(
            num_scalar_prefetch=count,
            grid=grid,
            in_specs=[pl.BlockSpec(memory_space=pl.ANY)] * ties + in_specs,
            out_specs=out_specs,
            scratch_shapes=scratch_shapes,
        ),
        out_shape=out_shape,
        input_output_aliases={count + number: number for number in range(len(into))},
        compiler_params=pltpu.CompilerParams(vmem_limit_bytes=vmem * MIB),
        cost_estimate=cost,
    )(*prefetch, *after, *operands)


def cost(micros):
    return pl.CostEstimate(
        flops=max(1, int(micros * PACE)), bytes_accessed=1, transcendentals=0
    )


def fixed(shape):
    return pl.BlockSpec(shape, lambda i, *_: (0,) * len(shape))


def held(shape):
    return pl.BlockSpec(
        shape, lambda i, *_: (0,) * len(shape), pipeline_mode=pl.Buffered(buffer_count=1)
    )


def down(rows, width, base=0):
    return pl.BlockSpec((rows, width), lambda i, *_: (base + i, 0))


def owned(rows, width, base):
    return pl.BlockSpec((rows, width), lambda i, spot: (base + spot[0], 0))


def column(table_rows, width, component):
    return pl.BlockSpec(
        (None, table_rows, width),
        lambda i, *_: (component, 0, 0),
        pipeline_mode=pl.Buffered(buffer_count=1),
    )


def whole_lanes(width):
    return -(-width // 128) * 128


def shaped(shape, kind=jnp.bfloat16):
    return jax.ShapeDtypeStruct(shape, kind)


def rows_dot(left, right):
    return lax.dot_general(
        left, right, (((1,), (1,)), ((), ())), preferred_element_type=jnp.float32
    )


def turned_dot(left, right):
    return lax.dot_general(
        left, right, (((0,), (0,)), ((), ())), preferred_element_type=jnp.float32
    )


def normed_rows(values):
    center = values - jnp.mean(values, axis=-1, keepdims=True)
    inverse = lax.rsqrt(jnp.mean(center * center, axis=-1, keepdims=True) + EPSILON)
    return center * inverse, inverse


def norm_back_rows(gradient, normed, inverse):
    return (
        gradient
        - jnp.mean(gradient, axis=-1, keepdims=True)
        - normed * jnp.mean(gradient * normed, axis=-1, keepdims=True)
    ) * inverse


def spread(hot_ref, table_ref):
    return jnp.dot(hot_ref[...], table_ref[...], preferred_element_type=jnp.float32)


def add_image_sums(sum_ref, spot, hot_ref, image_count, values):
    hot = hot_ref[:, :image_count]
    first = values.astype(jnp.bfloat16)
    second = (values - first.astype(jnp.float32)).astype(jnp.bfloat16)
    sum_ref[spot] += turned_dot(hot, first) + turned_dot(hot, second)


def clear_at_start(*refs):
    @pl.when(pl.program_id(0) == 0)
    def _():
        for ref in refs:
            ref[...] = jnp.zeros_like(ref)


def hand_out(spot_ref, outs, values, own):
    amount = values.shape[0] // own
    for place in range(amount):
        target = pl.program_id(0) * amount + place
        piece = values[place * own : (place + 1) * own, :].astype(outs[0].dtype)
        rows = pl.ds(pl.multiple_of(target // len(outs) * own, own), own)
        for mask, out in enumerate(outs):

            @pl.when(target % len(outs) == spot_ref[0] ^ mask)
            def _(out=out, piece=piece, rows=rows):
                out[rows, :] = piece


def sum_of(pieces):
    total = pieces[0][...].astype(jnp.float32)
    for piece in pieces[1:]:
        total = total + piece[...].astype(jnp.float32)
    return total


def head_window(place, features):
    start = place // 128 * 128
    return slice(start, min(features, start + 256))


def head_only(block, place):
    lanes = head_window(place, block.shape[1])
    window = block[:, lanes]
    lane = lax.broadcasted_iota(jnp.int32, window.shape, 1) + (lanes.start - place)
    return jnp.where((lane >= 0) & (lane < HDIM), window, jnp.zeros_like(window))


def visible_keys(first_ref, length_ref, base, tile_rows):
    first = first_ref[...] - base
    place = lax.broadcasted_iota(jnp.int32, (tile_rows, first.shape[1]), 0)
    offset = place - first
    return (offset >= 0) & (offset < length_ref[...])


def each_tile(low, high, source, tiles, body):
    lax.fori_loop(
        jnp.maximum(low, source * tiles),
        jnp.minimum(high, (source + 1) * tiles),
        lambda number, carry: body(number, carry),
        0,
    )


def attend_kernel(
    low_ref, high_ref, first_ref, length_ref, query_ref, *refs, tile, step_base
):
    kv_refs = refs[:3]
    low_out, wide_out, log_out, total, row_max, row_sum = refs[3:]
    features = query_ref.shape[1]
    heads = features // HDIM
    step = pl.program_id(0) + step_base
    queries = [head_only(query_ref[...], head * HDIM) for head in range(heads)]
    rescale = HDIM ** (-0.5) * LOG2E
    value_start = features // 128 * 128
    total[...] = jnp.zeros_like(total)
    row_max[...] = jnp.full_like(row_max, MASKED)
    row_sum[...] = jnp.zeros_like(row_sum)
    for source, kv_ref in enumerate(kv_refs):
        tiles = kv_ref.shape[0] // tile

        def body(number, carry, source=source, kv_ref=kv_ref, tiles=tiles):
            rows = pl.ds(pl.multiple_of((number - source * tiles) * tile, tile), tile)
            keys = kv_ref[rows, :features]
            values = kv_ref[rows, value_start:].astype(jnp.float32).T
            seen = visible_keys(first_ref, length_ref, number * tile, tile)
            for head in range(heads):
                scores = rows_dot(keys[:, head_window(head * HDIM, features)], queries[head])
                scores = jnp.where(seen, scores, MASKED)
                old = row_max[head : head + 1, :]
                new = jnp.maximum(old, jnp.max(scores, axis=0, keepdims=True))
                shrink = jnp.exp2((old - new) * rescale)
                shares = jnp.exp2((scores - new) * rescale)
                row_max[head : head + 1, :] = new
                row_sum[head : head + 1, :] = row_sum[
                    head : head + 1, :
                ] * shrink + jnp.sum(shares, axis=0, keepdims=True)
                mine = slice(head * HDIM, (head + 1) * HDIM)
                place = features - value_start + head * HDIM
                total[mine, :] = total[mine, :] * shrink + jnp.dot(
                    values[place : place + HDIM, :].astype(jnp.bfloat16),
                    shares.astype(jnp.bfloat16),
                    preferred_element_type=jnp.float32,
                )
            return carry

        each_tile(low_ref[step], high_ref[step], source, tiles, body)
    log_out[...] = row_max[...] * rescale + jnp.log2(row_sum[...])
    for head in range(heads):
        mine = slice(head * HDIM, (head + 1) * HDIM)
        total[mine, :] = total[mine, :] / row_sum[head : head + 1, :]
    wide_out[...] = total[...]
    low_out[...] = total[...].T.astype(jnp.bfloat16)


def attend(ranges, query, kvs, tile, block, chunk, chunks, after):
    lows, highs, firsts, lengths = ranges
    rows, features = query.shape
    heads = features // HDIM
    amount = rows // chunks
    steps = amount // block
    base = chunk * steps
    across = pl.BlockSpec((1, block), lambda i, *_: (0, base + i))
    return tied_call(
        functools.partial(attend_kernel, tile=tile, step_base=base),
        (lows, highs),
        (firsts, lengths, query, *kvs),
        after,
        grid=(steps,),
        in_specs=[across, across, down(block, features, base)] + [held(kvs[0].shape)] * 3,
        out_specs=[
            down(block, features),
            pl.BlockSpec((features, block), lambda i, *_: (0, i)),
            pl.BlockSpec((heads, block), lambda i, *_: (0, i)),
        ],
        out_shape=[
            shaped((amount, features)),
            shaped((features, amount), jnp.float32),
            shaped((heads, amount), jnp.float32),
        ],
        scratch_shapes=[
            pltpu.VMEM((features, block), jnp.float32),
            pltpu.VMEM((heads, block), jnp.float32),
            pltpu.VMEM((heads, block), jnp.float32),
        ],
        vmem=16,
        cost=cost(10),
    )


def attend_back_steps(
    step, low_ref, high_ref, first_ref, length_ref, log_ref, query_ref, grad_rows, wide, kv_refs,
    sources, total, kv_totals, tile,
):
    features = query_ref.shape[1]
    heads = features // HDIM
    rescale = HDIM ** (-0.5) * LOG2E
    queries = [head_only(query_ref[...], head * HDIM) for head in range(heads)]
    shifted = jnp.concatenate([jnp.zeros_like(grad_rows), grad_rows], axis=1)
    grads = [head_only(shifted, features + head * HDIM) for head in range(heads)]
    products = grad_rows.astype(jnp.float32).T * wide
    deltas = [
        jnp.sum(products[head * HDIM : (head + 1) * HDIM, :], axis=0, keepdims=True)
        for head in range(heads)
    ]
    for source, kv_ref, kv_total in zip(sources, kv_refs, kv_totals):
        tiles = kv_ref.shape[0] // tile

        def body(number, carry, source=source, kv_ref=kv_ref, kv_total=kv_total, tiles=tiles):
            rows = pl.ds(pl.multiple_of((number - source * tiles) * tile, tile), tile)
            pairs = kv_ref[rows, :]
            keys_down = kv_ref[rows, :features].astype(jnp.float32).T
            seen = visible_keys(first_ref, length_ref, number * tile, tile)
            for head in range(heads):
                key_lanes = head_window(head * HDIM, features)
                value_lanes = head_window(features + head * HDIM, 2 * features)
                scores = rows_dot(pairs[:, key_lanes], queries[head])
                shares = jnp.where(
                    seen, jnp.exp2(scores * rescale - log_ref[head : head + 1, :]), 0.0
                )
                grad_shares = rows_dot(pairs[:, value_lanes], grads[head])
                grad_scores = (shares * (grad_shares - deltas[head])).astype(jnp.bfloat16)
                kv_total[rows, value_lanes] += jnp.dot(
                    shares.astype(jnp.bfloat16), grads[head], preferred_element_type=jnp.float32
                )
                kv_total[rows, key_lanes] += jnp.dot(
                    grad_scores, queries[head], preferred_element_type=jnp.float32
                )
                mine = slice(head * HDIM, (head + 1) * HDIM)
                total[mine, :] += jnp.dot(
                    keys_down[mine, :].astype(jnp.bfloat16),
                    grad_scores,
                    preferred_element_type=jnp.float32,
                )
            return carry

        each_tile(low_ref[step], high_ref[step], source, tiles, body)


def write_pairs(out, kv_total, features):
    values = kv_total[...]
    lane = lax.broadcasted_iota(jnp.int32, values.shape, 1)
    out[...] = jnp.where(lane < features, values * HDIM ** (-0.5), values).astype(out.dtype)


def attend_far_kernel(
    low_ref, high_ref, spot_ref, first_ref, length_ref, log_ref, query_ref, wide_ref, before_ref,
    after_ref, *refs, tile, own,
):
    pieces = refs[:-7]
    query_out, grad_out, before_out, after_out, total, before_total, after_total = refs[-7:]
    step = pl.program_id(0)
    block, features = query_ref.shape
    clear_at_start(before_total, after_total)
    total[...] = jnp.zeros_like(total)
    parts = []
    for place in range(block // own):
        target = step * (block // own) + place
        rows = pl.ds(pl.multiple_of(target // len(pieces) * own, own), own)
        part = jnp.zeros((own, features), query_ref.dtype)
        for mask, piece in enumerate(pieces):
            part = jnp.where(target % len(pieces) == spot_ref[0] ^ mask, piece[rows, :], part)
        parts.append(part)
    grad_rows = jnp.concatenate(parts, axis=0)
    grad_out[...] = grad_rows
    attend_back_steps(
        step, low_ref, high_ref, first_ref, length_ref, log_ref, query_ref, grad_rows,
        wide_ref[...], (before_ref, after_ref), (0, 2), total, (before_total, after_total), tile,
    )
    query_out[...] = total[...]

    @pl.when(step == pl.num_programs(0) - 1)
    def _():
        write_pairs(before_out, before_total, features)
        write_pairs(after_out, after_total, features)


def attend_near_kernel(
    low_ref, high_ref, first_ref, length_ref, log_ref, query_ref, wide_ref, kv_ref, grad_ref,
    start_ref, query_out, kv_out, total, kv_total, *, tile,
):
    step = pl.program_id(0)
    clear_at_start(kv_total)
    total[...] = start_ref[...]
    attend_back_steps(
        step, low_ref, high_ref, first_ref, length_ref, log_ref, query_ref, grad_ref[...],
        wide_ref[...], (kv_ref,), (1,), total, (kv_total,), tile,
    )
    query_out[...] = (total[...].T * HDIM ** (-0.5)).astype(query_out.dtype)

    @pl.when(step == pl.num_programs(0) - 1)
    def _():
        write_pairs(kv_out, kv_total, query_ref.shape[1])


def attend_far(
    spot, ranges, logs, query, pieces, wide, before, later, tile, block, own, after
):
    lows, highs, firsts, lengths = ranges
    rows, features = query.shape
    across = pl.BlockSpec((1, block), lambda i, *_: (0, i))
    turned = pl.BlockSpec((features, block), lambda i, *_: (0, i))
    logged = pl.BlockSpec((features // HDIM, block), lambda i, *_: (0, i))
    pairs = (rows, whole_lanes(2 * features))
    return tied_call(
        functools.partial(attend_far_kernel, tile=tile, own=own),
        (lows, highs, spot),
        (firsts, lengths, logs, query, wide, before, later, *pieces),
        after,
        grid=(rows // block,),
        in_specs=[across, across, logged, down(block, features), turned, held(pairs), held(pairs)]
        + [held(pieces[0].shape)] * len(pieces),
        out_specs=[turned, down(block, features), fixed(pairs), fixed(pairs)],
        out_shape=[
            shaped((features, rows), jnp.float32),
            shaped((rows, features)),
            shaped(pairs),
            shaped(pairs),
        ],
        scratch_shapes=[
            pltpu.VMEM((features, block), jnp.float32),
            pltpu.VMEM(pairs, jnp.float32),
            pltpu.VMEM(pairs, jnp.float32),
        ],
        vmem=28,
        cost=cost(8),
    )


def attend_near(ranges, logs, query, grad, wide, kv, started, tile, block, after):
    lows, highs, firsts, lengths = ranges
    rows, features = query.shape
    across = pl.BlockSpec((1, block), lambda i, *_: (0, i))
    turned = pl.BlockSpec((features, block), lambda i, *_: (0, i))
    logged = pl.BlockSpec((features // HDIM, block), lambda i, *_: (0, i))
    pairs = (rows, whole_lanes(2 * features))
    return tied_call(
        functools.partial(attend_near_kernel, tile=tile),
        (lows, highs),
        (firsts, lengths, logs, query, wide, kv, grad, started),
        after,
        grid=(rows // block,),
        in_specs=[
            across, across, logged, down(block, features), turned, held(pairs),
            down(block, features), turned,
        ],
        out_specs=[down(block, features), fixed(pairs)],
        out_shape=[shaped((rows, features)), shaped(pairs, jnp.float32)],
        scratch_shapes=[
            pltpu.VMEM((features, block), jnp.float32),
            pltpu.VMEM(pairs, jnp.float32),
        ],
        vmem=24,
        cost=cost(16),
    )


def key_ranges(my_images, wide_images, image_count, tile, block):
    images = jnp.arange(image_count, dtype=jnp.int32)
    before = jnp.sum((wide_images[None, :] < images[:, None]).astype(jnp.int32), axis=1)
    amount = jnp.sum((wide_images[None, :] == images[:, None]).astype(jnp.int32), axis=1)
    mine = (my_images[None, :] == images[:, None]).astype(jnp.int32)
    firsts = jnp.sum(mine * before[:, None], axis=0)
    lengths = jnp.sum(mine * amount[:, None], axis=0)
    ends = firsts + lengths
    lows = firsts[::block] // tile
    highs = (ends[block - 1 :: block] + tile - 1) // tile
    return lows, highs, firsts[None, :], lengths[None, :]


def project_kernel(
    token_ref, hot_ref, shift_ref, scale_ref, weight_ref, bias_ref, hidden_out, query_out, kv_out
):
    features = query_out.shape[1]
    normed, _ = normed_rows(token_ref[...].astype(jnp.float32))
    hidden = normed * (1.0 + spread(hot_ref, scale_ref)) + spread(hot_ref, shift_ref)
    hidden = hidden.astype(jnp.bfloat16)
    hidden_out[...] = hidden
    projected = jnp.dot(hidden, weight_ref[...], preferred_element_type=jnp.float32)
    projected = (projected + bias_ref[...]).astype(jnp.bfloat16)
    query_out[...] = projected[:, :features]
    spare = kv_out.shape[1] - 2 * features
    empty = jnp.zeros((projected.shape[0], spare), projected.dtype)
    kv_out[...] = jnp.concatenate([projected[:, features:], empty][: 1 + (spare > 0)], axis=1)


def project(tokens, hot, table, weight, bias, block, after):
    rows, width = tokens.shape
    features = weight.shape[1] // 3
    high = table.shape[1]
    return tied_call(
        project_kernel,
        (),
        (tokens, hot, table, table, weight, bias),
        after,
        grid=(rows // block,),
        in_specs=[
            down(block, width),
            down(block, hot.shape[1]),
            column(high, width, 0),
            column(high, width, 1),
            held(weight.shape),
            held(bias.shape),
        ],
        out_specs=[
            down(block, width),
            down(block, features),
            down(block, whole_lanes(2 * features)),
        ],
        out_shape=[
            shaped((rows, width)),
            shaped((rows, features)),
            shaped((rows, whole_lanes(2 * features))),
        ],
        vmem=20,
        cost=cost(6),
    )


def grad_act_kernel(
    cot_ref, hot_ref, gate_ref, weight_ref, grad_out, act_out, bias_out, sum_out, *, image_count
):
    clear_at_start(bias_out, sum_out)
    cot = cot_ref[...]
    grad = (spread(hot_ref, gate_ref) * cot.astype(jnp.float32)).astype(jnp.bfloat16)
    grad_out[...] = grad
    bias_out[...] += jnp.sum(grad.astype(jnp.float32), axis=0, keepdims=True)
    sum_out[...] += turned_dot(hot_ref[:, :image_count], cot)
    act_out[...] = rows_dot(grad, weight_ref[...])


def grad_act_of(cotangent, hot, table, weight, image_count, block, after):
    rows, width = cotangent.shape
    units = weight.shape[0]
    return tied_call(
        functools.partial(grad_act_kernel, image_count=image_count),
        (),
        (cotangent, hot, table, weight),
        after,
        grid=(rows // block,),
        in_specs=[
            down(block, width),
            down(block, hot.shape[1]),
            column(table.shape[1], width, 5),
            held(weight.shape),
        ],
        out_specs=[
            down(block, width),
            down(block, units),
            fixed((1, width)),
            fixed((image_count, width)),
        ],
        out_shape=[
            shaped((rows, width)),
            shaped((rows, units), jnp.float32),
            shaped((1, width), jnp.float32),
            shaped((image_count, width), jnp.float32),
        ],
        vmem=20,
        cost=cost(5),
    )


def peer_rows(spot_ref, mask, rows):
    return pl.ds(pl.multiple_of((spot_ref[0] ^ mask) * rows, rows), rows)


def middle_kernel(spot_ref, *refs, count, image_count):
    pieces = refs[:count]
    (
        out_ref, token_ref, hot_ref, gate_ref, shift_ref, scale_ref, out_bias_ref, up_ref,
        up_bias_ref, grad_act_ref, attn_out, hidden_out, act_out, grad_out, sum_out, bias_out,
    ) = refs[count:-count]
    clear_at_start(sum_out, bias_out)
    attn = out_bias_ref[...].astype(jnp.float32)
    for mask, piece in enumerate(pieces):
        rows = peer_rows(spot_ref, mask, piece.shape[1])
        attn = attn + jnp.dot(piece[...], out_ref[rows, :], preferred_element_type=jnp.float32)
    attn_out[...] = attn
    middle = token_ref[...].astype(jnp.float32) + spread(hot_ref, gate_ref) * attn
    normed, _ = normed_rows(middle)
    hidden = normed * (1.0 + spread(hot_ref, scale_ref)) + spread(hot_ref, shift_ref)
    hidden = hidden.astype(jnp.bfloat16)
    hidden_out[...] = hidden
    pre = jnp.dot(hidden, up_ref[...], preferred_element_type=jnp.float32)
    pre = pre + up_bias_ref[...].astype(jnp.float32)
    square = pre * pre
    bend = jnp.tanh(ROOT * pre * (1.0 + CUBIC * square))
    half = 0.5 * (1.0 + bend)
    act_out[...] = (pre * half).astype(jnp.bfloat16)
    slope = half + 0.5 * ROOT * pre * (1.0 - bend * bend) * (1.0 + 3.0 * CUBIC * square)
    grad = (grad_act_ref[...] * slope).astype(jnp.bfloat16)
    grad_out[...] = grad
    bias_out[...] += jnp.sum(grad.astype(jnp.float32), axis=0, keepdims=True)
    part = rows_dot(grad, up_ref[...])
    hand_out(spot_ref, refs[-count:], part, refs[-1].shape[0])
    add_image_sums(sum_out, 0, hot_ref, image_count, part)
    add_image_sums(sum_out, 1, hot_ref, image_count, part * normed)


def middle_of(
    spot, pieces, tokens, hot, table, out_full, out_bias, up_weight, up_bias, grad_act,
    image_count, block, chunk, into, after,
):
    rows, features = pieces[0].shape
    width, units = up_weight.shape
    whole = tokens.shape[0]
    high = table.shape[1]
    count = len(pieces)
    base = chunk * (rows // block)
    return tied_call(
        functools.partial(middle_kernel, count=count, image_count=image_count),
        (spot,),
        (
            *pieces, out_full, tokens, hot, table, table, table, out_bias, up_weight, up_bias,
            grad_act,
        ),
        after,
        grid=(rows // block,),
        in_specs=[down(block, features)] * count
        + [
            held(out_full.shape),
            down(block, width, base),
            down(block, hot.shape[1], base),
            column(high, width, 2),
            column(high, width, 3),
            column(high, width, 4),
            held(out_bias.shape),
            held(up_weight.shape),
            held(up_bias.shape),
            down(block, units, base),
        ],
        out_specs=[
            down(block, width, base),
            down(block, width, base),
            down(block, units, base),
            down(block, units, base),
            fixed((2, image_count, width)),
            fixed((1, units)),
        ]
        + [fixed((rows // count, width))] * count,
        into=into,
        out_shape=[
            shaped((whole, width), jnp.float32),
            shaped((whole, width)),
            shaped((whole, units)),
            shaped((whole, units)),
            shaped((2, image_count, width), jnp.float32),
            shaped((1, units), jnp.float32),
        ]
        + [shaped((rows // count, width))] * count,
        vmem=36,
        cost=cost(12),
    )


def mlp_kernel(act_ref, weight_ref, cot_ref, hot_ref, part_out, sum_out, *, image_count):
    clear_at_start(sum_out)
    part = jnp.dot(act_ref[...], weight_ref[...], preferred_element_type=jnp.float32)
    part_out[...] = part.astype(jnp.bfloat16)
    add_image_sums(sum_out, 0, hot_ref, image_count, part * cot_ref[...].astype(jnp.float32))


def mlp_of(act, weight, cotangent, hot, image_count, block, after):
    rows, units = act.shape
    width = weight.shape[1]
    return tied_call(
        functools.partial(mlp_kernel, image_count=image_count),
        (),
        (act, weight, cotangent, hot),
        after,
        grid=(rows // block,),
        in_specs=[
            down(block, units),
            held(weight.shape),
            down(block, width),
            down(block, hot.shape[1]),
        ],
        out_specs=[down(block, width), fixed((1, image_count, width))],
        out_shape=[shaped((rows, width)), shaped((1, image_count, width), jnp.float32)],
        vmem=20,
        cost=cost(6),
    )


def owned_chunks(rows, width, count):
    return pl.BlockSpec((rows, width), lambda c, spot: (c * count + spot[0], 0))


def grad_middle_kernel(spot_ref, *refs, count, chunks, image_count):
    pieces = refs[: count * chunks]
    (
        out_ref, attn_ref, token_ref, cot_ref, hot_ref, gate_ref, scale_ref, middle_out, attn_out,
        sum_out, bias_out,
    ) = refs[count * chunks : -count]
    clear_at_start(sum_out, bias_out)
    gate = spread(hot_ref, gate_ref)
    attn = attn_ref[...]
    normed, inverse = normed_rows(token_ref[...].astype(jnp.float32) + gate * attn)
    hidden = pick(
        pl.program_id(0), [sum_of(pieces[c * count : (c + 1) * count]) for c in range(chunks)]
    )
    gradient = hidden * (1.0 + spread(hot_ref, scale_ref))
    grad_middle = cot_ref[...].astype(jnp.float32) + norm_back_rows(gradient, normed, inverse)
    middle_out[...] = grad_middle
    grad_attn = (gate * grad_middle).astype(jnp.bfloat16)
    attn_out[...] = grad_attn
    for mask, block_out in enumerate(refs[-count:]):
        rows = peer_rows(spot_ref, mask, block_out.shape[1])
        block_out[...] = rows_dot(grad_attn, out_ref[rows, :]).astype(jnp.bfloat16)
    bias_out[...] += jnp.sum(grad_attn.astype(jnp.float32), axis=0, keepdims=True)
    add_image_sums(sum_out, 0, hot_ref, image_count, grad_middle * attn)


def grad_middle_of(
    spot, chunks, attn, tokens, cotangent, hot, table, out_full, image_count, after
):
    count = len(chunks[0])
    pieces = [piece for chunk in chunks for piece in chunk]
    rows, width = pieces[0].shape
    features = out_full.shape[0] // count
    high = table.shape[1]
    whole = rows * len(chunks)
    mine = owned_chunks(rows, width, count)
    return tied_call(
        functools.partial(
            grad_middle_kernel, count=count, chunks=len(chunks), image_count=image_count
        ),
        (spot,),
        (*pieces, out_full, attn, tokens, cotangent, hot, table, table),
        after,
        grid=(len(chunks),),
        in_specs=[held((rows, width))] * len(pieces)
        + [
            held(out_full.shape),
            mine,
            mine,
            mine,
            owned_chunks(rows, hot.shape[1], count),
            column(high, width, 2),
            column(high, width, 4),
        ],
        out_specs=[
            down(rows, width),
            down(rows, width),
            fixed((1, image_count, width)),
            fixed((1, width)),
        ]
        + [down(rows, features)] * count,
        out_shape=[
            shaped((whole, width), jnp.float32),
            shaped((whole, width)),
            shaped((1, image_count, width), jnp.float32),
            shaped((1, width), jnp.float32),
        ]
        + [shaped((whole, features))] * count,
        vmem=60,
        cost=cost(6),
    )


def layer_out_kernel(
    mlp_ref, attn_ref, token_ref, hot_ref, gate_ref, gate_two_ref, bias_ref, rows_out
):
    middle = token_ref[...].astype(jnp.float32) + spread(hot_ref, gate_ref) * attn_ref[...]
    mlp = mlp_ref[...].astype(jnp.float32) + bias_ref[...].astype(jnp.float32)
    rows_out[...] = (middle + spread(hot_ref, gate_two_ref) * mlp).astype(jnp.bfloat16)


def layer_out_of(mlp, attn, tokens, hot, table, bias, block, after):
    rows, width = tokens.shape
    high = table.shape[1]
    return tied_call(
        layer_out_kernel,
        (),
        (mlp, attn, tokens, hot, table, table, bias),
        after,
        grid=(rows // block,),
        in_specs=[
            down(block, width),
            down(block, width),
            down(block, width),
            down(block, hot.shape[1]),
            column(high, width, 2),
            column(high, width, 5),
            held(bias.shape),
        ],
        out_specs=down(block, width),
        out_shape=shaped((rows, width)),
        vmem=20,
        cost=cost(4),
    )


def grad_tokens_kernel(spot_ref, *refs, count):
    pieces = refs[:count]
    token_ref, hot_ref, scale_ref, middle_ref, rows_out = refs[count:]
    normed, inverse = normed_rows(token_ref[...].astype(jnp.float32))
    gradient = sum_of(pieces) * (1.0 + spread(hot_ref, scale_ref))
    rows_out[...] = (middle_ref[...] + norm_back_rows(gradient, normed, inverse)).astype(jnp.bfloat16)


def grad_tokens_of(spot, pieces, tokens, hot, table, grad_middle, chunks, after):
    whole, width = grad_middle.shape
    rows = whole // chunks
    count = len(pieces)
    return tied_call(
        functools.partial(grad_tokens_kernel, count=count),
        (spot,),
        (*pieces, tokens, hot, table, grad_middle),
        after,
        grid=(chunks,),
        in_specs=[down(rows, width)] * count
        + [
            owned_chunks(rows, width, count),
            owned_chunks(rows, hot.shape[1], count),
            column(table.shape[1], width, 1),
            down(rows, width),
        ],
        out_specs=down(rows, width),
        out_shape=shaped((rows * chunks, width)),
        vmem=12,
        cost=cost(4),
    )


def grad_hidden_kernel(
    spot_ref, query_ref, near_ref, later_ref, before_ref, weight_ref, token_ref, hot_ref, all_out,
    sum_out, bias_out, *outs, image_count, own,
):
    clear_at_start(sum_out, bias_out)
    normed, _ = normed_rows(token_ref[...].astype(jnp.float32))
    pairs = (
        near_ref[...] + later_ref[...].astype(jnp.float32) + before_ref[...].astype(jnp.float32)
    ).astype(jnp.bfloat16)
    features = query_ref.shape[1]
    grad = jnp.concatenate([query_ref[...], pairs[:, : 2 * features]], axis=1)
    all_out[...] = grad
    bias_out[...] += jnp.sum(grad.astype(jnp.float32), axis=0, keepdims=True)
    part = rows_dot(grad, weight_ref[...])
    hand_out(spot_ref, outs, part, own)
    add_image_sums(sum_out, 0, hot_ref, image_count, part)
    add_image_sums(sum_out, 1, hot_ref, image_count, part * normed)


def grad_hidden_of(
    spot, query, near, later, before, weight, tokens, hot, image_count, block, own, count, after
):
    rows, features = query.shape
    width = tokens.shape[1]
    pair = down(block, whole_lanes(2 * features))
    return tied_call(
        functools.partial(grad_hidden_kernel, image_count=image_count, own=own),
        (spot,),
        (query, near, later, before, weight, tokens, hot),
        after,
        grid=(rows // block,),
        in_specs=[
            down(block, features),
            pair,
            pair,
            pair,
            held(weight.shape),
            down(block, width),
            down(block, hot.shape[1]),
        ],
        out_specs=[
            down(block, 3 * features),
            fixed((2, image_count, width)),
            fixed((1, 3 * features)),
        ]
        + [fixed((rows // count, width))] * count,
        out_shape=[
            shaped((rows, 3 * features)),
            shaped((2, image_count, width), jnp.float32),
            shaped((1, 3 * features), jnp.float32),
        ]
        + [shaped((rows // count, width))] * count,
        vmem=20,
        cost=cost(8),
    )


def place_kernel(spot_ref, *refs, chunks):
    out, pieces = refs[-1], refs[:-1]
    own = out.shape[0]
    for c in range(chunks):
        for mask, piece in enumerate(pieces):

            @pl.when(pl.program_id(0) == (spot_ref[0] ^ mask) + c * len(pieces))
            def _(piece=piece, c=c):
                out[...] = piece[c * own : (c + 1) * own, :].astype(out.dtype)


def place_rows(spot, pieces, chunks, kind, after):
    rows, width = pieces[0].shape
    own = rows // chunks
    return tied_call(
        functools.partial(place_kernel, chunks=chunks),
        (spot,),
        pieces,
        after,
        grid=(len(pieces) * chunks,),
        in_specs=[held((rows, width))] * len(pieces),
        out_specs=down(own, width),
        out_shape=shaped((rows * len(pieces), width), kind),
        vmem=12,
        cost=cost(3),
    )


def split_kernel(spot_ref, *refs, sizes, kept, count):
    values, place = [], 0
    for size in sizes:
        values.append(sum_of(refs[place : place + size]))
        place += size
    values = jnp.concatenate(values, axis=0)
    columns = values.shape[1] // count
    split_out, kept_out = refs[-2:]
    for mask in range(count):
        result = values[:, :columns]
        for j in range(1, count):
            result = jnp.where(
                spot_ref[0] ^ mask == j, values[:, j * columns : (j + 1) * columns], result
            )
        split_out[mask] = result
    rows = []
    for size in kept:
        value = sum_of(refs[place : place + size])
        place += size
        for j in range(value.shape[1] // columns):
            rows.append(value[:, j * columns : (j + 1) * columns])
    kept_out[...] = jnp.concatenate(rows, axis=0)


def split_columns(spot, groups, kept, count, after):
    operands = [value for group in groups + kept for value in group]
    rows = sum(group[0].shape[0] for group in groups)
    columns = operands[0].shape[1] // count
    shapes = [
        (count, rows, columns),
        (sum(group[0].shape[1] for group in kept) // columns, columns),
    ]
    return tied_call(
        functools.partial(
            split_kernel,
            sizes=[len(group) for group in groups],
            kept=[len(group) for group in kept],
            count=count,
        ),
        (spot,),
        operands,
        after,
        grid=(1,),
        in_specs=[held(value.shape) for value in operands],
        out_specs=[fixed(shape) for shape in shapes],
        out_shape=[shaped(shape, jnp.float32) for shape in shapes],
        vmem=12,
        cost=cost(1),
    )


def mlp_weights_kernel(hidden_ref, grad_ref, pre_ref, act_ref, out):
    units = pre_ref.shape[1]
    out[:, :units] = turned_dot(hidden_ref[...], pre_ref[...]).astype(jnp.bfloat16)
    out[:, units:] = turned_dot(grad_ref[...], act_ref[...]).astype(jnp.bfloat16)


def mlp_weights(grad_mlp, hidden, pre, act, after):
    rows, width = grad_mlp.shape
    units = pre.shape[1]
    if units % 128:
        sides = [turned_dot(hidden, pre), turned_dot(grad_mlp, act)]
        return jnp.concatenate([side.astype(jnp.bfloat16) for side in sides], axis=1)
    part = width // 3
    across = pl.BlockSpec((rows, part), lambda i, *_: (0, i))
    return tied_call(
        mlp_weights_kernel,
        (),
        (hidden, grad_mlp, pre, act),
        after,
        grid=(3,),
        in_specs=[across, across, held((rows, units)), held((rows, units))],
        out_specs=pl.BlockSpec((part, 2 * units), lambda i, *_: (i, 0)),
        out_shape=shaped((width, 2 * units)),
        vmem=28,
        cost=cost(7),
    )


def attn_weights_kernel(spot_ref, side_ref, hidden_ref, *refs, chunks, count, blocks):
    grad_ref, attended = refs[0], refs[1 : 1 + chunks]
    pieces, outs = refs[1 + chunks : 1 + chunks + count], refs[1 + chunks + count :]
    own = pieces[0].shape[0] // chunks
    high, low = turned_dot(hidden_ref[...], grad_ref[...]), 0.0
    for mask, piece in enumerate(pieces):
        place = pl.ds(pl.multiple_of((spot_ref[0] ^ mask) * own, own), own)
        theirs = jnp.concatenate([attended[c][place, :] for c in range(chunks)], axis=0)
        low = low + turned_dot(piece[...], theirs)
    total = jnp.concatenate([low.astype(jnp.bfloat16), high.astype(jnp.bfloat16)], axis=1)
    if not blocks:
        outs[0][...] = total
        return
    size = total.shape[0] // blocks
    for pair in range(blocks // 2):
        left = total[2 * pair * size : (2 * pair + 1) * size, :]
        right = total[(2 * pair + 1) * size : (2 * pair + 2) * size, :]
        outs[0][pair] = jnp.where(side_ref[0] == 0, left, right)
        outs[1][pair] = jnp.where(side_ref[0] == 0, right, left)


def attn_weights(spot, side, hidden, attended, grad, pieces, blocks, after):
    rows, width = hidden.shape
    chunks = len(attended)
    features = attended[0].shape[1]
    operands = (hidden, grad, *attended, *pieces)
    if blocks:
        shapes = [(blocks // 2, width // blocks, 4 * features)] * 2
    else:
        shapes = [(width, 4 * features)]
    return tied_call(
        functools.partial(
            attn_weights_kernel, chunks=chunks, count=len(pieces), blocks=blocks
        ),
        (spot, side),
        operands,
        after,
        grid=(1,),
        in_specs=[held(value.shape) for value in operands],
        out_specs=[fixed(shape) for shape in shapes],
        out_shape=[shaped(shape) for shape in shapes],
        vmem=40,
        cost=cost(7),
    )


def fold_kernel(side_ref, kept_ref, got_ref, keep_out, send_out):
    for pair in range(keep_out.shape[0]):
        left, right = [
            kept_ref[block].astype(jnp.float32) + got_ref[block].astype(jnp.float32)
            for block in (2 * pair, 2 * pair + 1)
        ]
        keep_out[pair] = jnp.where(side_ref[0] == 0, left, right).astype(keep_out.dtype)
        send_out[pair] = jnp.where(side_ref[0] == 0, right, left).astype(send_out.dtype)


def fold_blocks(side, kept, got, after):
    blocks, size, width = kept.shape
    shape = (blocks // 2, size, width)
    return tied_call(
        fold_kernel,
        (side,),
        (kept, got),
        after,
        grid=(1,),
        in_specs=[held(kept.shape)] * 2,
        out_specs=[fixed(shape)] * 2,
        out_shape=[shaped(shape)] * 2,
        vmem=12,
        cost=cost(2),
    )


def attn_total_kernel(*refs, count):
    pieces, (out_out, qkv_out) = refs[:count], refs[count:]
    total = sum_of(pieces)[0]
    features = out_out.shape[0]
    out_out[...] = total[:, :features].T
    for c in range(3):
        qkv_out[c] = total[:, (c + 1) * features : (c + 2) * features]


def attn_total_of(pieces, features, after):
    _, size, width = pieces[0].shape
    return tied_call(
        functools.partial(attn_total_kernel, count=len(pieces)),
        (),
        pieces,
        after,
        grid=(1,),
        in_specs=[held((1, size, width))] * len(pieces),
        out_specs=[fixed((features, size)), fixed((3, size, features))],
        out_shape=[
            shaped((features, size), jnp.float32),
            shaped((3, size, features), jnp.float32),
        ],
        vmem=12,
        cost=cost(1),
    )


def on_device(
    tokens,
    conditioning,
    image_index,
    qkv_weight,
    qv_bias,
    out_weight,
    out_bias,
    up_weight,
    up_bias,
    down_weight,
    down_bias,
    ada_weight,
    ada_bias,
    cotangent,
):
    row_count, width = tokens.shape
    feature_count = qkv_weight.shape[2]
    head_size = lax.axis_size("head")
    me = lax.axis_index("head")
    spot = me.astype(jnp.int32).reshape(1)
    my_index = lax.axis_index("seq")
    seq_size = lax.axis_size("seq")
    side = (my_index % 2).astype(jnp.int32).reshape(1)
    blocks = seq_size if width % (16 * seq_size) == 0 else 0
    image_count = conditioning.shape[0]
    columns = ada_weight.shape[2]
    my_images = lax.dynamic_slice_in_dim(image_index, my_index * row_count, row_count, 0)
    edge = jnp.full((row_count,), -1, jnp.int32)
    padded_images = jnp.concatenate([edge, image_index, edge + (image_count + 1)])
    wide_images = lax.dynamic_slice_in_dim(padded_images, my_index * row_count, 3 * row_count, 0)
    ranges = key_ranges(my_images, wide_images, image_count, KEY_TILE, QUERY_BLOCK)
    images = jnp.tile(jnp.arange(image_count, dtype=jnp.int32), 3)
    hot = (my_images[:, None] == images[None, :]).astype(jnp.bfloat16)

    out_full = lax.all_gather(out_weight, "head", axis=0, tiled=True)
    cond_float = conditioning.astype(jnp.float32)
    cond_act = jax.nn.silu(cond_float).astype(jnp.bfloat16)
    mod_mine = jnp.einsum("id,dkf->kif", cond_act, ada_weight, preferred_element_type=jnp.float32)
    mod_mine = mod_mine + ada_bias.astype(jnp.float32)[:, None]
    mod_pieces = gather_pieces(mod_mine, "head")
    modulation = jnp.concatenate([pick(me ^ j, mod_pieces) for j in range(head_size)], axis=2)
    table = jnp.concatenate(three_parts(modulation), axis=1)

    weight = qkv_weight.reshape(width, 3 * feature_count)
    qv_wide = qv_bias.astype(jnp.float32)
    bias = jnp.concatenate([qv_wide[0], jnp.zeros_like(qv_wide[0]), qv_wide[1]])[None]
    hidden_one, query, kv = project(tokens, hot, table, weight, bias, ROW_BLOCK, [])
    kv_before = step_along(kv, "seq", True)
    kv_after = step_along(kv, "seq", False)
    grad_mlp, grad_act, grad_down_bias, cot_sums = grad_act_of(
        cotangent, hot, table, down_weight, image_count, ROW_BLOCK, [hidden_one]
    )
    kvs = [kv_before, kv, kv_after]
    attended, attended_wide, logs, last = [], [], [], [grad_down_bias]
    for c in range(CHUNKS):
        got = attend(ranges, query, kvs, KEY_TILE, QUERY_BLOCK, c, CHUNKS, last)
        for values, kept in zip((attended, attended_wide, logs), got):
            values.append(kept)
        last = [got[2]]
    attended_wide = jnp.concatenate(attended_wide, axis=1)
    logs = jnp.concatenate(logs, axis=1)

    late_sums, up_sums, hidden_pieces, into, last = [], [], [], [], [logs]
    for c in range(CHUNKS):
        got = middle_of(
            spot, gather_pieces(attended[c], "head"), tokens, hot, table, out_full, out_bias[None],
            up_weight, up_bias[None], grad_act, image_count, ROW_BLOCK, c, into, last,
        )
        into = got[:4]
        late_sums.append(got[4].reshape(2 * image_count, width))
        up_sums.append(got[5])
        hidden_pieces.append(swap_pieces(got[6:], "head"))
        last = []
    attn, hidden_two, act, grad_pre = into
    mlp_part, mlp_sums = mlp_of(
        act, down_weight, cotangent, hot, image_count, ROW_BLOCK, hidden_pieces[0]
    )
    mlp = lax.psum(mlp_part, "head")
    weight_part = mlp_weights(grad_mlp, hidden_two, grad_pre, act, [mlp_sums])

    grad_middle, grad_own, gate_sums, out_sums, *attended_pieces = grad_middle_of(
        spot, hidden_pieces, attn, tokens, cotangent, hot, table, out_full, image_count,
        [weight_part],
    )

    own_rows = row_count // CHUNKS // head_size
    query_started, grad_rows, to_before, to_after = attend_far(
        spot, ranges, logs, query, swap_pieces(attended_pieces, "head"), attended_wide, kv_before,
        kv_after, KEY_TILE, QUERY_BLOCK, own_rows, [],
    )
    grad_attn = gather_pieces(grad_own, "head")
    from_after = step_along(to_before, "seq", False)
    from_before = step_along(to_after, "seq", True)
    grad_query, kv_near = attend_near(
        ranges, logs, query, grad_rows, attended_wide, kv, query_started, KEY_TILE, QUERY_BLOCK,
        [],
    )

    grad_all, first_sums, qkv_sums, *one_pieces = grad_hidden_of(
        spot, grad_query, kv_near, from_after, from_before, weight, tokens, hot, image_count,
        ROW_BLOCK, own_rows, head_size, grad_attn,
    )
    one_pieces = swap_pieces(one_pieces, "head")
    attn_part = attn_weights(
        spot, side, hidden_one, attended, grad_all, grad_attn, blocks, []
    )
    layer_out = layer_out_of(
        mlp, attn, tokens, hot, table, down_bias[None], ROW_BLOCK, [attn_part[0]]
    )
    own_tokens = grad_tokens_of(
        spot, one_pieces, tokens, hot, table, grad_middle, CHUNKS, [layer_out]
    )
    token_pieces = gather_pieces(own_tokens, "head")
    last = own_tokens
    if blocks:
        kept, sent = fold_blocks(
            ((my_index // 2) % 2).astype(jnp.int32).reshape(1),
            attn_part[0],
            swap(attn_part[1], "seq", 1),
            [own_tokens],
        )
        last = kept
    sum_stack, kept_rows = split_columns(
        spot,
        [[first_sums.reshape(2 * image_count, width)], [gate_sums[0]], late_sums, [mlp_sums[0]]]
        + [[out_sums]],
        [[qkv_sums], up_sums, [grad_down_bias]],
        head_size,
        [last],
    )
    sums = fold_pieces(sum_stack, "head")
    if blocks:
        mask = 2
        while mask < blocks // 2:
            mask *= 2
            kept, sent = fold_blocks(
                ((my_index // mask) % 2).astype(jnp.int32).reshape(1),
                kept,
                swap(sent, "seq", mask // 2),
                [sums],
            )
        attn_got = [kept, swap(sent, "seq", mask)]

    own_down = lax.dynamic_slice_in_dim(down_bias, me * columns, columns, 0).astype(jnp.float32)
    own_cot = lax.dynamic_slice_in_dim(cot_sums, me * columns, columns, 1) * own_down[None]
    mods = 6 * image_count
    sums = sums + jnp.pad(own_cot, ((5 * image_count, 1), (0, 0)))
    sums = butterfly_sum(jnp.concatenate([sums, kept_rows], axis=0), "seq")
    grad_mod = sums[:mods].reshape(6, image_count, columns)
    out_sum = sums[mods : mods + 1]
    grad_qv_bias = sums[mods + 1 : mods + 4 : 2]
    low_bias = sums[mods + 4 :].reshape(-1)
    units = up_weight.shape[1]
    grad_up_bias, grad_down_bias = low_bias[:units], low_bias[units:]
    mod_parts = jnp.concatenate(three_parts(grad_mod), axis=1)
    grad_cond_act = jnp.einsum(
        "kif,dkf->id", mod_parts, ada_weight, preferred_element_type=jnp.float32
    )
    grad_cond_act = jnp.sum(grad_cond_act.reshape(3, image_count, width), axis=0)
    spread_bias = jnp.concatenate(
        [jnp.where(me == j, out_sum, 0.0) for j in range(head_size)], axis=1
    )
    final = butterfly_sum(jnp.concatenate([grad_cond_act, spread_bias], axis=0), "head")
    _, silu_pull = jax.vjp(jax.nn.silu, cond_float)
    grad_conditioning = silu_pull(final[:image_count])[0]
    grad_out_bias = final[image_count]
    grad_ada_bias = jnp.sum(grad_mod, axis=1)
    grad_ada_weight = jnp.einsum(
        "id,kif->dkf",
        jnp.concatenate([cond_act] * 3, axis=0),
        mod_parts,
        preferred_element_type=jnp.float32,
    )

    grad_tokens = place_rows(spot, token_pieces, CHUNKS, jnp.float32, [])
    mlp_total = lax.psum_scatter(weight_part, "seq", scatter_dimension=0, tiled=True)
    mlp_total = mlp_total.astype(jnp.float32)
    if blocks:
        grad_out_weight, grad_qkv = attn_total_of(attn_got, feature_count, [])
        grad_qkv_weight = grad_qkv.transpose(1, 0, 2)
    else:
        attn_total = lax.psum_scatter(attn_part[0], "seq", scatter_dimension=0, tiled=True)
        attn_total = attn_total.astype(jnp.float32)
        grad_out_weight = attn_total[:, :feature_count].T
        grad_qkv_weight = attn_total[:, feature_count:].reshape(-1, 3, feature_count)
    return (
        layer_out,
        grad_tokens,
        grad_conditioning,
        grad_qkv_weight,
        grad_qv_bias,
        grad_out_weight,
        grad_out_bias,
        mlp_total[:, :units],
        grad_up_bias,
        mlp_total[:, units:].T,
        grad_down_bias,
        grad_ada_weight,
        grad_ada_bias,
    )


def solution(mesh):
    placed = (
        P("seq", None),
        P(),
        P(),
        P(None, None, "head"),
        P(None, "head"),
        P("head", None),
        P(),
        P(None, "head"),
        P("head"),
        P("head", None),
        P(),
        P(None, None, "head"),
        P(None, "head"),
        P("seq", None),
    )
    return jax.shard_map(
        on_device,
        mesh=mesh,
        in_specs=placed,
        out_specs=(
            P("seq", None),
            P("seq", None),
            P(),
            P("seq", None, "head"),
            P(None, "head"),
            P("head", "seq"),
            P(),
            P("seq", "head"),
            P("head"),
            P("head", "seq"),
            P(),
            P(None, None, "head"),
            P(None, "head"),
        ),
        check_vma=False,
    )
```

```python
import functools

import jax
import jax.numpy as jnp
from jax import lax
from jax.experimental import pallas as pl
from jax.experimental.pallas import tpu as pltpu
from jax.sharding import PartitionSpec as P

HDIM = 72


EPSILON = 1e-06
MASKED = -1e30
PRECISE = lax.Precision.HIGHEST
CHUNKS = 2
KEY_TILE = 512
QUERY_BLOCK = 256
ROW_BLOCK = 256
ROOT = 0.7978845608028654
CUBIC = 0.044715
LOG2E = 1.4426950408889634
MIB = 1 << 20
PACE = 1.15e9


def peers(axis):
    return range(1, lax.axis_size(axis))


def swap(value, axis, mask):
    count = lax.axis_size(axis)
    return lax.ppermute(value, axis, [(i, i ^ mask) for i in range(count)])


def gather_pieces(value, axis):
    return [value] + [swap(value, axis, mask) for mask in peers(axis)]


def fold_pieces(stack, axis):
    amount = stack.shape[0]
    while amount > 1:
        amount //= 2
        stack = stack[:amount] + swap(stack[amount:], axis, amount)
    return stack[0]


def swap_pieces(pieces, axis):
    return [pieces[0]] + [swap(pieces[mask], axis, mask) for mask in peers(axis)]


def butterfly_sum(value, axis):
    mask = 1
    while mask < lax.axis_size(axis):
        value = value + swap(value, axis, mask)
        mask *= 2
    return value


def step_along(value, axis, ahead):
    count = lax.axis_size(axis)
    pairs = [(i, i + 1) if ahead else (i + 1, i) for i in range(count - 1)]
    return lax.ppermute(value, axis, pairs)


def three_parts(values):
    first = lax.reduce_precision(values, 8, 7)
    second = lax.reduce_precision(values - first, 8, 7)
    third = values - first - second
    return [part.astype(jnp.bfloat16) for part in (first, second, third)]


def pick(which, cases):
    result = cases[0]
    for number, case in enumerate(cases[1:], 1):
        result = jnp.where(which == number, case, result)
    return result


def tied_call(
    kernel, prefetch, operands, after, *, grid, in_specs, out_specs, out_shape, vmem, cost,
    scratch_shapes=(), into=(),
):
    after = [*into, *after]
    count, ties = len(prefetch), len(after)

    def body(*refs):
        return kernel(*refs[:count], *refs[count + ties :])

    return pl.pallas_call(
        body,
        grid_spec=pltpu.PrefetchScalarGridSpec(
            num_scalar_prefetch=count,
            grid=grid,
            in_specs=[pl.BlockSpec(memory_space=pl.ANY)] * ties + in_specs,
            out_specs=out_specs,
            scratch_shapes=scratch_shapes,
        ),
        out_shape=out_shape,
        input_output_aliases={count + number: number for number in range(len(into))},
        compiler_params=pltpu.CompilerParams(vmem_limit_bytes=vmem * MIB),
        cost_estimate=cost,
    )(*prefetch, *after, *operands)


def cost(micros):
    return pl.CostEstimate(
        flops=max(1, int(micros * PACE)), bytes_accessed=1, transcendentals=0
    )


def fixed(shape):
    return pl.BlockSpec(shape, lambda i, *_: (0,) * len(shape))


def held(shape):
    return pl.BlockSpec(
        shape, lambda i, *_: (0,) * len(shape), pipeline_mode=pl.Buffered(buffer_count=1)
    )


def down(rows, width, base=0):
    return pl.BlockSpec((rows, width), lambda i, *_: (base + i, 0))


def owned(rows, width, base):
    return pl.BlockSpec((rows, width), lambda i, spot: (base + spot[0], 0))


def column(table_rows, width, component):
    return pl.BlockSpec(
        (None, table_rows, width),
        lambda i, *_: (component, 0, 0),
        pipeline_mode=pl.Buffered(buffer_count=1),
    )


def whole_lanes(width):
    return -(-width // 128) * 128


def shaped(shape, kind=jnp.bfloat16):
    return jax.ShapeDtypeStruct(shape, kind)


def rows_dot(left, right):
    return lax.dot_general(
        left, right, (((1,), (1,)), ((), ())), preferred_element_type=jnp.float32
    )


def turned_dot(left, right):
    return lax.dot_general(
        left, right, (((0,), (0,)), ((), ())), preferred_element_type=jnp.float32
    )


def normed_rows(values):
    center = values - jnp.mean(values, axis=-1, keepdims=True)
    inverse = lax.rsqrt(jnp.mean(center * center, axis=-1, keepdims=True) + EPSILON)
    return center * inverse, inverse


def norm_back_rows(gradient, normed, inverse):
    return (
        gradient
        - jnp.mean(gradient, axis=-1, keepdims=True)
        - normed * jnp.mean(gradient * normed, axis=-1, keepdims=True)
    ) * inverse


def spread(hot_ref, table_ref):
    return jnp.dot(hot_ref[...], table_ref[...], preferred_element_type=jnp.float32)


def add_image_sums(sum_ref, spot, hot_ref, image_count, values):
    hot = hot_ref[:, :image_count]
    first = values.astype(jnp.bfloat16)
    second = (values - first.astype(jnp.float32)).astype(jnp.bfloat16)
    sum_ref[spot] += turned_dot(hot, first) + turned_dot(hot, second)


def clear_at_start(*refs):
    @pl.when(pl.program_id(0) == 0)
    def _():
        for ref in refs:
            ref[...] = jnp.zeros_like(ref)


def hand_out(spot_ref, outs, values, own):
    amount = values.shape[0] // own
    for place in range(amount):
        target = pl.program_id(0) * amount + place
        piece = values[place * own : (place + 1) * own, :].astype(outs[0].dtype)
        rows = pl.ds(pl.multiple_of(target // len(outs) * own, own), own)
        for mask, out in enumerate(outs):

            @pl.when(target % len(outs) == spot_ref[0] ^ mask)
            def _(out=out, piece=piece, rows=rows):
                out[rows, :] = piece


def sum_of(pieces):
    total = pieces[0][...].astype(jnp.float32)
    for piece in pieces[1:]:
        total = total + piece[...].astype(jnp.float32)
    return total


def head_window(place, features):
    start = place // 128 * 128
    return slice(start, min(features, start + 256))


def head_only(block, place):
    lanes = head_window(place, block.shape[1])
    window = block[:, lanes]
    lane = lax.broadcasted_iota(jnp.int32, window.shape, 1) + (lanes.start - place)
    return jnp.where((lane >= 0) & (lane < HDIM), window, jnp.zeros_like(window))


def visible_keys(first_ref, length_ref, base, tile_rows):
    first = first_ref[...] - base
    place = lax.broadcasted_iota(jnp.int32, (tile_rows, first.shape[1]), 0)
    offset = place - first
    return (offset >= 0) & (offset < length_ref[...])


def each_tile(low, high, source, tiles, body):
    lax.fori_loop(
        jnp.maximum(low, source * tiles),
        jnp.minimum(high, (source + 1) * tiles),
        lambda number, carry: body(number, carry),
        0,
    )


def attend_kernel(
    low_ref, high_ref, first_ref, length_ref, query_ref, *refs, tile, step_base
):
    kv_refs = refs[:3]
    low_out, wide_out, log_out, total, row_max, row_sum = refs[3:]
    features = query_ref.shape[1]
    heads = features // HDIM
    step = pl.program_id(0) + step_base
    queries = [head_only(query_ref[...], head * HDIM) for head in range(heads)]
    rescale = HDIM ** (-0.5) * LOG2E
    value_start = features // 128 * 128
    total[...] = jnp.zeros_like(total)
    row_max[...] = jnp.full_like(row_max, MASKED)
    row_sum[...] = jnp.zeros_like(row_sum)
    for source, kv_ref in enumerate(kv_refs):
        tiles = kv_ref.shape[0] // tile

        def body(number, carry, source=source, kv_ref=kv_ref, tiles=tiles):
            rows = pl.ds(pl.multiple_of((number - source * tiles) * tile, tile), tile)
            keys = kv_ref[rows, :features]
            values = kv_ref[rows, value_start:].astype(jnp.float32).T
            seen = visible_keys(first_ref, length_ref, number * tile, tile)
            for head in range(heads):
                scores = rows_dot(keys[:, head_window(head * HDIM, features)], queries[head])
                scores = jnp.where(seen, scores, MASKED)
                old = row_max[head : head + 1, :]
                new = jnp.maximum(old, jnp.max(scores, axis=0, keepdims=True))
                shrink = jnp.exp2((old - new) * rescale)
                shares = jnp.exp2((scores - new) * rescale)
                row_max[head : head + 1, :] = new
                row_sum[head : head + 1, :] = row_sum[
                    head : head + 1, :
                ] * shrink + jnp.sum(shares, axis=0, keepdims=True)
                mine = slice(head * HDIM, (head + 1) * HDIM)
                place = features - value_start + head * HDIM
                total[mine, :] = total[mine, :] * shrink + jnp.dot(
                    values[place : place + HDIM, :].astype(jnp.bfloat16),
                    shares.astype(jnp.bfloat16),
                    preferred_element_type=jnp.float32,
                )
            return carry

        each_tile(low_ref[step], high_ref[step], source, tiles, body)
    log_out[...] = row_max[...] * rescale + jnp.log2(row_sum[...])
    for head in range(heads):
        mine = slice(head * HDIM, (head + 1) * HDIM)
        total[mine, :] = total[mine, :] / row_sum[head : head + 1, :]
    wide_out[...] = total[...]
    low_out[...] = total[...].T.astype(jnp.bfloat16)


def attend(ranges, query, kvs, tile, block, chunk, chunks, after):
    lows, highs, firsts, lengths = ranges
    rows, features = query.shape
    heads = features // HDIM
    amount = rows // chunks
    steps = amount // block
    base = chunk * steps
    across = pl.BlockSpec((1, block), lambda i, *_: (0, base + i))
    return tied_call(
        functools.partial(attend_kernel, tile=tile, step_base=base),
        (lows, highs),
        (firsts, lengths, query, *kvs),
        after,
        grid=(steps,),
        in_specs=[across, across, down(block, features, base)] + [held(kvs[0].shape)] * 3,
        out_specs=[
            down(block, features),
            pl.BlockSpec((features, block), lambda i, *_: (0, i)),
            pl.BlockSpec((heads, block), lambda i, *_: (0, i)),
        ],
        out_shape=[
            shaped((amount, features)),
            shaped((features, amount), jnp.float32),
            shaped((heads, amount), jnp.float32),
        ],
        scratch_shapes=[
            pltpu.VMEM((features, block), jnp.float32),
            pltpu.VMEM((heads, block), jnp.float32),
            pltpu.VMEM((heads, block), jnp.float32),
        ],
        vmem=16,
        cost=cost(10),
    )


def attend_back_steps(
    step, low_ref, high_ref, first_ref, length_ref, log_ref, query_ref, grad_rows, wide, kv_refs,
    sources, total, kv_totals, tile,
):
    features = query_ref.shape[1]
    heads = features // HDIM
    rescale = HDIM ** (-0.5) * LOG2E
    queries = [head_only(query_ref[...], head * HDIM) for head in range(heads)]
    shifted = jnp.concatenate([jnp.zeros_like(grad_rows), grad_rows], axis=1)
    grads = [head_only(shifted, features + head * HDIM) for head in range(heads)]
    products = grad_rows.astype(jnp.float32).T * wide
    deltas = [
        jnp.sum(products[head * HDIM : (head + 1) * HDIM, :], axis=0, keepdims=True)
        for head in range(heads)
    ]
    for source, kv_ref, kv_total in zip(sources, kv_refs, kv_totals):
        tiles = kv_ref.shape[0] // tile

        def body(number, carry, source=source, kv_ref=kv_ref, kv_total=kv_total, tiles=tiles):
            rows = pl.ds(pl.multiple_of((number - source * tiles) * tile, tile), tile)
            pairs = kv_ref[rows, :]
            keys_down = kv_ref[rows, :features].astype(jnp.float32).T
            seen = visible_keys(first_ref, length_ref, number * tile, tile)
            for head in range(heads):
                key_lanes = head_window(head * HDIM, features)
                value_lanes = head_window(features + head * HDIM, 2 * features)
                scores = rows_dot(pairs[:, key_lanes], queries[head])
                shares = jnp.where(
                    seen, jnp.exp2(scores * rescale - log_ref[head : head + 1, :]), 0.0
                )
                grad_shares = rows_dot(pairs[:, value_lanes], grads[head])
                grad_scores = (shares * (grad_shares - deltas[head])).astype(jnp.bfloat16)
                kv_total[rows, value_lanes] += jnp.dot(
                    shares.astype(jnp.bfloat16), grads[head], preferred_element_type=jnp.float32
                )
                kv_total[rows, key_lanes] += jnp.dot(
                    grad_scores, queries[head], preferred_element_type=jnp.float32
                )
                mine = slice(head * HDIM, (head + 1) * HDIM)
                total[mine, :] += jnp.dot(
                    keys_down[mine, :].astype(jnp.bfloat16),
                    grad_scores,
                    preferred_element_type=jnp.float32,
                )
            return carry

        each_tile(low_ref[step], high_ref[step], source, tiles, body)


def write_pairs(out, kv_total, features):
    values = kv_total[...]
    lane = lax.broadcasted_iota(jnp.int32, values.shape, 1)
    out[...] = jnp.where(lane < features, values * HDIM ** (-0.5), values).astype(out.dtype)


def attend_far_kernel(
    low_ref, high_ref, spot_ref, first_ref, length_ref, log_ref, query_ref, wide_ref, before_ref,
    after_ref, *refs, tile, own,
):
    pieces = refs[:-7]
    query_out, grad_out, before_out, after_out, total, before_total, after_total = refs[-7:]
    step = pl.program_id(0)
    block, features = query_ref.shape
    clear_at_start(before_total, after_total)
    total[...] = jnp.zeros_like(total)
    parts = []
    for place in range(block // own):
        target = step * (block // own) + place
        rows = pl.ds(pl.multiple_of(target // len(pieces) * own, own), own)
        part = jnp.zeros((own, features), query_ref.dtype)
        for mask, piece in enumerate(pieces):
            part = jnp.where(target % len(pieces) == spot_ref[0] ^ mask, piece[rows, :], part)
        parts.append(part)
    grad_rows = jnp.concatenate(parts, axis=0)
    grad_out[...] = grad_rows
    attend_back_steps(
        step, low_ref, high_ref, first_ref, length_ref, log_ref, query_ref, grad_rows,
        wide_ref[...], (before_ref, after_ref), (0, 2), total, (before_total, after_total), tile,
    )
    query_out[...] = total[...]

    @pl.when(step == pl.num_programs(0) - 1)
    def _():
        write_pairs(before_out, before_total, features)
        write_pairs(after_out, after_total, features)


def attend_near_kernel(
    low_ref, high_ref, first_ref, length_ref, log_ref, query_ref, wide_ref, kv_ref, grad_ref,
    start_ref, query_out, kv_out, total, kv_total, *, tile,
):
    step = pl.program_id(0)
    clear_at_start(kv_total)
    total[...] = start_ref[...]
    attend_back_steps(
        step, low_ref, high_ref, first_ref, length_ref, log_ref, query_ref, grad_ref[...],
        wide_ref[...], (kv_ref,), (1,), total, (kv_total,), tile,
    )
    query_out[...] = (total[...].T * HDIM ** (-0.5)).astype(query_out.dtype)

    @pl.when(step == pl.num_programs(0) - 1)
    def _():
        write_pairs(kv_out, kv_total, query_ref.shape[1])


def attend_far(
    spot, ranges, logs, query, pieces, wide, before, later, tile, block, own, after
):
    lows, highs, firsts, lengths = ranges
    rows, features = query.shape
    across = pl.BlockSpec((1, block), lambda i, *_: (0, i))
    turned = pl.BlockSpec((features, block), lambda i, *_: (0, i))
    logged = pl.BlockSpec((features // HDIM, block), lambda i, *_: (0, i))
    pairs = (rows, whole_lanes(2 * features))
    return tied_call(
        functools.partial(attend_far_kernel, tile=tile, own=own),
        (lows, highs, spot),
        (firsts, lengths, logs, query, wide, before, later, *pieces),
        after,
        grid=(rows // block,),
        in_specs=[across, across, logged, down(block, features), turned, held(pairs), held(pairs)]
        + [held(pieces[0].shape)] * len(pieces),
        out_specs=[turned, down(block, features), fixed(pairs), fixed(pairs)],
        out_shape=[
            shaped((features, rows), jnp.float32),
            shaped((rows, features)),
            shaped(pairs),
            shaped(pairs),
        ],
        scratch_shapes=[
            pltpu.VMEM((features, block), jnp.float32),
            pltpu.VMEM(pairs, jnp.float32),
            pltpu.VMEM(pairs, jnp.float32),
        ],
        vmem=28,
        cost=cost(8),
    )


def attend_near(ranges, logs, query, grad, wide, kv, started, tile, block, after):
    lows, highs, firsts, lengths = ranges
    rows, features = query.shape
    across = pl.BlockSpec((1, block), lambda i, *_: (0, i))
    turned = pl.BlockSpec((features, block), lambda i, *_: (0, i))
    logged = pl.BlockSpec((features // HDIM, block), lambda i, *_: (0, i))
    pairs = (rows, whole_lanes(2 * features))
    return tied_call(
        functools.partial(attend_near_kernel, tile=tile),
        (lows, highs),
        (firsts, lengths, logs, query, wide, kv, grad, started),
        after,
        grid=(rows // block,),
        in_specs=[
            across, across, logged, down(block, features), turned, held(pairs),
            down(block, features), turned,
        ],
        out_specs=[down(block, features), fixed(pairs)],
        out_shape=[shaped((rows, features)), shaped(pairs, jnp.float32)],
        scratch_shapes=[
            pltpu.VMEM((features, block), jnp.float32),
            pltpu.VMEM(pairs, jnp.float32),
        ],
        vmem=24,
        cost=cost(16),
    )


def key_ranges(my_images, wide_images, image_count, tile, block):
    images = jnp.arange(image_count, dtype=jnp.int32)
    before = jnp.sum((wide_images[None, :] < images[:, None]).astype(jnp.int32), axis=1)
    amount = jnp.sum((wide_images[None, :] == images[:, None]).astype(jnp.int32), axis=1)
    mine = (my_images[None, :] == images[:, None]).astype(jnp.int32)
    firsts = jnp.sum(mine * before[:, None], axis=0)
    lengths = jnp.sum(mine * amount[:, None], axis=0)
    ends = firsts + lengths
    lows = firsts[::block] // tile
    highs = (ends[block - 1 :: block] + tile - 1) // tile
    return lows, highs, firsts[None, :], lengths[None, :]


def project_kernel(
    token_ref, hot_ref, shift_ref, scale_ref, weight_ref, bias_ref, hidden_out, query_out, kv_out
):
    features = query_out.shape[1]
    normed, _ = normed_rows(token_ref[...].astype(jnp.float32))
    hidden = normed * (1.0 + spread(hot_ref, scale_ref)) + spread(hot_ref, shift_ref)
    hidden = hidden.astype(jnp.bfloat16)
    hidden_out[...] = hidden
    projected = jnp.dot(hidden, weight_ref[...], preferred_element_type=jnp.float32)
    projected = (projected + bias_ref[...]).astype(jnp.bfloat16)
    query_out[...] = projected[:, :features]
    spare = kv_out.shape[1] - 2 * features
    empty = jnp.zeros((projected.shape[0], spare), projected.dtype)
    kv_out[...] = jnp.concatenate([projected[:, features:], empty][: 1 + (spare > 0)], axis=1)


def project(tokens, hot, table, weight, bias, block, after):
    rows, width = tokens.shape
    features = weight.shape[1] // 3
    high = table.shape[1]
    return tied_call(
        project_kernel,
        (),
        (tokens, hot, table, table, weight, bias),
        after,
        grid=(rows // block,),
        in_specs=[
            down(block, width),
            down(block, hot.shape[1]),
            column(high, width, 0),
            column(high, width, 1),
            held(weight.shape),
            held(bias.shape),
        ],
        out_specs=[
            down(block, width),
            down(block, features),
            down(block, whole_lanes(2 * features)),
        ],
        out_shape=[
            shaped((rows, width)),
            shaped((rows, features)),
            shaped((rows, whole_lanes(2 * features))),
        ],
        vmem=20,
        cost=cost(6),
    )


def grad_act_kernel(
    cot_ref, hot_ref, gate_ref, weight_ref, grad_out, act_out, bias_out, sum_out, *, image_count
):
    clear_at_start(bias_out, sum_out)
    cot = cot_ref[...]
    grad = (spread(hot_ref, gate_ref) * cot.astype(jnp.float32)).astype(jnp.bfloat16)
    grad_out[...] = grad
    bias_out[...] += jnp.sum(grad.astype(jnp.float32), axis=0, keepdims=True)
    sum_out[...] += turned_dot(hot_ref[:, :image_count], cot)
    act_out[...] = rows_dot(grad, weight_ref[...])


def grad_act_of(cotangent, hot, table, weight, image_count, block, after):
    rows, width = cotangent.shape
    units = weight.shape[0]
    return tied_call(
        functools.partial(grad_act_kernel, image_count=image_count),
        (),
        (cotangent, hot, table, weight),
        after,
        grid=(rows // block,),
        in_specs=[
            down(block, width),
            down(block, hot.shape[1]),
            column(table.shape[1], width, 5),
            held(weight.shape),
        ],
        out_specs=[
            down(block, width),
            down(block, units),
            fixed((1, width)),
            fixed((image_count, width)),
        ],
        out_shape=[
            shaped((rows, width)),
            shaped((rows, units), jnp.float32),
            shaped((1, width), jnp.float32),
            shaped((image_count, width), jnp.float32),
        ],
        vmem=20,
        cost=cost(5),
    )


def peer_rows(spot_ref, mask, rows):
    return pl.ds(pl.multiple_of((spot_ref[0] ^ mask) * rows, rows), rows)


def middle_kernel(spot_ref, *refs, count, image_count):
    pieces = refs[:count]
    (
        out_ref, token_ref, hot_ref, gate_ref, shift_ref, scale_ref, out_bias_ref, up_ref,
        up_bias_ref, grad_act_ref, attn_out, hidden_out, act_out, grad_out, sum_out, bias_out,
    ) = refs[count:-count]
    clear_at_start(sum_out, bias_out)
    attn = out_bias_ref[...].astype(jnp.float32)
    for mask, piece in enumerate(pieces):
        rows = peer_rows(spot_ref, mask, piece.shape[1])
        attn = attn + jnp.dot(piece[...], out_ref[rows, :], preferred_element_type=jnp.float32)
    attn_out[...] = attn
    middle = token_ref[...].astype(jnp.float32) + spread(hot_ref, gate_ref) * attn
    normed, _ = normed_rows(middle)
    hidden = normed * (1.0 + spread(hot_ref, scale_ref)) + spread(hot_ref, shift_ref)
    hidden = hidden.astype(jnp.bfloat16)
    hidden_out[...] = hidden
    pre = jnp.dot(hidden, up_ref[...], preferred_element_type=jnp.float32)
    pre = pre + up_bias_ref[...].astype(jnp.float32)
    square = pre * pre
    bend = jnp.tanh(ROOT * pre * (1.0 + CUBIC * square))
    half = 0.5 * (1.0 + bend)
    act_out[...] = (pre * half).astype(jnp.bfloat16)
    slope = half + 0.5 * ROOT * pre * (1.0 - bend * bend) * (1.0 + 3.0 * CUBIC * square)
    grad = (grad_act_ref[...] * slope).astype(jnp.bfloat16)
    grad_out[...] = grad
    bias_out[...] += jnp.sum(grad.astype(jnp.float32), axis=0, keepdims=True)
    part = rows_dot(grad, up_ref[...])
    hand_out(spot_ref, refs[-count:], part, refs[-1].shape[0])
    add_image_sums(sum_out, 0, hot_ref, image_count, part)
    add_image_sums(sum_out, 1, hot_ref, image_count, part * normed)


def middle_of(
    spot, pieces, tokens, hot, table, out_full, out_bias, up_weight, up_bias, grad_act,
    image_count, block, chunk, into, after,
):
    rows, features = pieces[0].shape
    width, units = up_weight.shape
    whole = tokens.shape[0]
    high = table.shape[1]
    count = len(pieces)
    base = chunk * (rows // block)
    return tied_call(
        functools.partial(middle_kernel, count=count, image_count=image_count),
        (spot,),
        (
            *pieces, out_full, tokens, hot, table, table, table, out_bias, up_weight, up_bias,
            grad_act,
        ),
        after,
        grid=(rows // block,),
        in_specs=[down(block, features)] * count
        + [
            held(out_full.shape),
            down(block, width, base),
            down(block, hot.shape[1], base),
            column(high, width, 2),
            column(high, width, 3),
            column(high, width, 4),
            held(out_bias.shape),
            held(up_weight.shape),
            held(up_bias.shape),
            down(block, units, base),
        ],
        out_specs=[
            down(block, width, base),
            down(block, width, base),
            down(block, units, base),
            down(block, units, base),
            fixed((2, image_count, width)),
            fixed((1, units)),
        ]
        + [fixed((rows // count, width))] * count,
        into=into,
        out_shape=[
            shaped((whole, width), jnp.float32),
            shaped((whole, width)),
            shaped((whole, units)),
            shaped((whole, units)),
            shaped((2, image_count, width), jnp.float32),
            shaped((1, units), jnp.float32),
        ]
        + [shaped((rows // count, width))] * count,
        vmem=36,
        cost=cost(12),
    )


def mlp_kernel(act_ref, weight_ref, cot_ref, hot_ref, part_out, sum_out, *, image_count):
    clear_at_start(sum_out)
    part = jnp.dot(act_ref[...], weight_ref[...], preferred_element_type=jnp.float32)
    part_out[...] = part.astype(jnp.bfloat16)
    add_image_sums(sum_out, 0, hot_ref, image_count, part * cot_ref[...].astype(jnp.float32))


def mlp_of(act, weight, cotangent, hot, image_count, block, after):
    rows, units = act.shape
    width = weight.shape[1]
    return tied_call(
        functools.partial(mlp_kernel, image_count=image_count),
        (),
        (act, weight, cotangent, hot),
        after,
        grid=(rows // block,),
        in_specs=[
            down(block, units),
            held(weight.shape),
            down(block, width),
            down(block, hot.shape[1]),
        ],
        out_specs=[down(block, width), fixed((1, image_count, width))],
        out_shape=[shaped((rows, width)), shaped((1, image_count, width), jnp.float32)],
        vmem=20,
        cost=cost(6),
    )


def owned_chunks(rows, width, count):
    return pl.BlockSpec((rows, width), lambda c, spot: (c * count + spot[0], 0))


def grad_middle_kernel(spot_ref, *refs, count, chunks, image_count):
    pieces = refs[: count * chunks]
    (
        out_ref, attn_ref, token_ref, cot_ref, hot_ref, gate_ref, scale_ref, middle_out, attn_out,
        sum_out, bias_out,
    ) = refs[count * chunks : -count]
    clear_at_start(sum_out, bias_out)
    gate = spread(hot_ref, gate_ref)
    attn = attn_ref[...]
    normed, inverse = normed_rows(token_ref[...].astype(jnp.float32) + gate * attn)
    hidden = pick(
        pl.program_id(0), [sum_of(pieces[c * count : (c + 1) * count]) for c in range(chunks)]
    )
    gradient = hidden * (1.0 + spread(hot_ref, scale_ref))
    grad_middle = cot_ref[...].astype(jnp.float32) + norm_back_rows(gradient, normed, inverse)
    middle_out[...] = grad_middle
    grad_attn = (gate * grad_middle).astype(jnp.bfloat16)
    attn_out[...] = grad_attn
    for mask, block_out in enumerate(refs[-count:]):
        rows = peer_rows(spot_ref, mask, block_out.shape[1])
        block_out[...] = rows_dot(grad_attn, out_ref[rows, :]).astype(jnp.bfloat16)
    bias_out[...] += jnp.sum(grad_attn.astype(jnp.float32), axis=0, keepdims=True)
    add_image_sums(sum_out, 0, hot_ref, image_count, grad_middle * attn)


def grad_middle_of(
    spot, chunks, attn, tokens, cotangent, hot, table, out_full, image_count, after
):
    count = len(chunks[0])
    pieces = [piece for chunk in chunks for piece in chunk]
    rows, width = pieces[0].shape
    features = out_full.shape[0] // count
    high = table.shape[1]
    whole = rows * len(chunks)
    mine = owned_chunks(rows, width, count)
    return tied_call(
        functools.partial(
            grad_middle_kernel, count=count, chunks=len(chunks), image_count=image_count
        ),
        (spot,),
        (*pieces, out_full, attn, tokens, cotangent, hot, table, table),
        after,
        grid=(len(chunks),),
        in_specs=[held((rows, width))] * len(pieces)
        + [
            held(out_full.shape),
            mine,
            mine,
            mine,
            owned_chunks(rows, hot.shape[1], count),
            column(high, width, 2),
            column(high, width, 4),
        ],
        out_specs=[
            down(rows, width),
            down(rows, width),
            fixed((1, image_count, width)),
            fixed((1, width)),
        ]
        + [down(rows, features)] * count,
        out_shape=[
            shaped((whole, width), jnp.float32),
            shaped((whole, width)),
            shaped((1, image_count, width), jnp.float32),
            shaped((1, width), jnp.float32),
        ]
        + [shaped((whole, features))] * count,
        vmem=60,
        cost=cost(6),
    )


def layer_out_kernel(
    mlp_ref, attn_ref, token_ref, hot_ref, gate_ref, gate_two_ref, bias_ref, rows_out
):
    middle = token_ref[...].astype(jnp.float32) + spread(hot_ref, gate_ref) * attn_ref[...]
    mlp = mlp_ref[...].astype(jnp.float32) + bias_ref[...].astype(jnp.float32)
    rows_out[...] = (middle + spread(hot_ref, gate_two_ref) * mlp).astype(jnp.bfloat16)


def layer_out_of(mlp, attn, tokens, hot, table, bias, block, after):
    rows, width = tokens.shape
    high = table.shape[1]
    return tied_call(
        layer_out_kernel,
        (),
        (mlp, attn, tokens, hot, table, table, bias),
        after,
        grid=(rows // block,),
        in_specs=[
            down(block, width),
            down(block, width),
            down(block, width),
            down(block, hot.shape[1]),
            column(high, width, 2),
            column(high, width, 5),
            held(bias.shape),
        ],
        out_specs=down(block, width),
        out_shape=shaped((rows, width)),
        vmem=20,
        cost=cost(4),
    )


def grad_tokens_kernel(spot_ref, *refs, count):
    pieces = refs[:count]
    token_ref, hot_ref, scale_ref, middle_ref, rows_out = refs[count:]
    normed, inverse = normed_rows(token_ref[...].astype(jnp.float32))
    gradient = sum_of(pieces) * (1.0 + spread(hot_ref, scale_ref))
    rows_out[...] = (middle_ref[...] + norm_back_rows(gradient, normed, inverse)).astype(jnp.bfloat16)


def grad_tokens_of(spot, pieces, tokens, hot, table, grad_middle, chunks, after):
    whole, width = grad_middle.shape
    rows = whole // chunks
    count = len(pieces)
    return tied_call(
        functools.partial(grad_tokens_kernel, count=count),
        (spot,),
        (*pieces, tokens, hot, table, grad_middle),
        after,
        grid=(chunks,),
        in_specs=[down(rows, width)] * count
        + [
            owned_chunks(rows, width, count),
            owned_chunks(rows, hot.shape[1], count),
            column(table.shape[1], width, 1),
            down(rows, width),
        ],
        out_specs=down(rows, width),
        out_shape=shaped((rows * chunks, width)),
        vmem=12,
        cost=cost(4),
    )


def grad_hidden_kernel(
    spot_ref, query_ref, near_ref, later_ref, before_ref, weight_ref, token_ref, hot_ref, all_out,
    sum_out, bias_out, *outs, image_count, own,
):
    clear_at_start(sum_out, bias_out)
    normed, _ = normed_rows(token_ref[...].astype(jnp.float32))
    pairs = (
        near_ref[...] + later_ref[...].astype(jnp.float32) + before_ref[...].astype(jnp.float32)
    ).astype(jnp.bfloat16)
    features = query_ref.shape[1]
    grad = jnp.concatenate([query_ref[...], pairs[:, : 2 * features]], axis=1)
    all_out[...] = grad
    bias_out[...] += jnp.sum(grad.astype(jnp.float32), axis=0, keepdims=True)
    part = rows_dot(grad, weight_ref[...])
    hand_out(spot_ref, outs, part, own)
    add_image_sums(sum_out, 0, hot_ref, image_count, part)
    add_image_sums(sum_out, 1, hot_ref, image_count, part * normed)


def grad_hidden_of(
    spot, query, near, later, before, weight, tokens, hot, image_count, block, own, count, after
):
    rows, features = query.shape
    width = tokens.shape[1]
    pair = down(block, whole_lanes(2 * features))
    return tied_call(
        functools.partial(grad_hidden_kernel, image_count=image_count, own=own),
        (spot,),
        (query, near, later, before, weight, tokens, hot),
        after,
        grid=(rows // block,),
        in_specs=[
            down(block, features),
            pair,
            pair,
            pair,
            held(weight.shape),
            down(block, width),
            down(block, hot.shape[1]),
        ],
        out_specs=[
            down(block, 3 * features),
            fixed((2, image_count, width)),
            fixed((1, 3 * features)),
        ]
        + [fixed((rows // count, width))] * count,
        out_shape=[
            shaped((rows, 3 * features)),
            shaped((2, image_count, width), jnp.float32),
            shaped((1, 3 * features), jnp.float32),
        ]
        + [shaped((rows // count, width))] * count,
        vmem=20,
        cost=cost(8),
    )


def place_kernel(spot_ref, *refs, chunks):
    out, pieces = refs[-1], refs[:-1]
    own = out.shape[0]
    for c in range(chunks):
        for mask, piece in enumerate(pieces):

            @pl.when(pl.program_id(0) == (spot_ref[0] ^ mask) + c * len(pieces))
            def _(piece=piece, c=c):
                out[...] = piece[c * own : (c + 1) * own, :].astype(out.dtype)


def place_rows(spot, pieces, chunks, kind, after):
    rows, width = pieces[0].shape
    own = rows // chunks
    return tied_call(
        functools.partial(place_kernel, chunks=chunks),
        (spot,),
        pieces,
        after,
        grid=(len(pieces) * chunks,),
        in_specs=[held((rows, width))] * len(pieces),
        out_specs=down(own, width),
        out_shape=shaped((rows * len(pieces), width), kind),
        vmem=12,
        cost=cost(3),
    )


def split_kernel(spot_ref, *refs, sizes, kept, count):
    values, place = [], 0
    for size in sizes:
        values.append(sum_of(refs[place : place + size]))
        place += size
    values = jnp.concatenate(values, axis=0)
    columns = values.shape[1] // count
    split_out, kept_out = refs[-2:]
    for mask in range(count):
        result = values[:, :columns]
        for j in range(1, count):
            result = jnp.where(
                spot_ref[0] ^ mask == j, values[:, j * columns : (j + 1) * columns], result
            )
        split_out[mask] = result
    rows = []
    for size in kept:
        value = sum_of(refs[place : place + size])
        place += size
        for j in range(value.shape[1] // columns):
            rows.append(value[:, j * columns : (j + 1) * columns])
    kept_out[...] = jnp.concatenate(rows, axis=0)


def split_columns(spot, groups, kept, count, after):
    operands = [value for group in groups + kept for value in group]
    rows = sum(group[0].shape[0] for group in groups)
    columns = operands[0].shape[1] // count
    shapes = [
        (count, rows, columns),
        (sum(group[0].shape[1] for group in kept) // columns, columns),
    ]
    return tied_call(
        functools.partial(
            split_kernel,
            sizes=[len(group) for group in groups],
            kept=[len(group) for group in kept],
            count=count,
        ),
        (spot,),
        operands,
        after,
        grid=(1,),
        in_specs=[held(value.shape) for value in operands],
        out_specs=[fixed(shape) for shape in shapes],
        out_shape=[shaped(shape, jnp.float32) for shape in shapes],
        vmem=12,
        cost=cost(1),
    )


def mlp_weights_kernel(hidden_ref, grad_ref, pre_ref, act_ref, out):
    units = pre_ref.shape[1]
    out[:, :units] = turned_dot(hidden_ref[...], pre_ref[...]).astype(jnp.bfloat16)
    out[:, units:] = turned_dot(grad_ref[...], act_ref[...]).astype(jnp.bfloat16)


def mlp_weights(grad_mlp, hidden, pre, act, after):
    rows, width = grad_mlp.shape
    units = pre.shape[1]
    if units % 128:
        sides = [turned_dot(hidden, pre), turned_dot(grad_mlp, act)]
        return jnp.concatenate([side.astype(jnp.bfloat16) for side in sides], axis=1)
    part = width // 3
    across = pl.BlockSpec((rows, part), lambda i, *_: (0, i))
    return tied_call(
        mlp_weights_kernel,
        (),
        (hidden, grad_mlp, pre, act),
        after,
        grid=(3,),
        in_specs=[across, across, held((rows, units)), held((rows, units))],
        out_specs=pl.BlockSpec((part, 2 * units), lambda i, *_: (i, 0)),
        out_shape=shaped((width, 2 * units)),
        vmem=28,
        cost=cost(7),
    )


def mlp_total_kernel(total_ref, up_out, down_out):
    units = up_out.shape[1]
    total = total_ref[...].astype(jnp.float32)
    up_out[...] = total[:, :units]
    down_out[...] = total[:, units:].T


def mlp_total_of(total, units):
    size = total.shape[0]
    if units % 128:
        total = total.astype(jnp.float32)
        return total[:, :units], total[:, units:].T
    return tied_call(
        mlp_total_kernel,
        (),
        (total,),
        [],
        grid=(1,),
        in_specs=[held(total.shape)],
        out_specs=[fixed((size, units)), fixed((units, size))],
        out_shape=[shaped((size, units), jnp.float32), shaped((units, size), jnp.float32)],
        vmem=12,
        cost=cost(1),
    )


def attn_weights_kernel(spot_ref, side_ref, hidden_ref, *refs, chunks, count, blocks):
    grad_ref, attended = refs[0], refs[1 : 1 + chunks]
    pieces, outs = refs[1 + chunks : 1 + chunks + count], refs[1 + chunks + count :]
    own = pieces[0].shape[0] // chunks
    high, low = turned_dot(hidden_ref[...], grad_ref[...]), 0.0
    for mask, piece in enumerate(pieces):
        place = pl.ds(pl.multiple_of((spot_ref[0] ^ mask) * own, own), own)
        theirs = jnp.concatenate([attended[c][place, :] for c in range(chunks)], axis=0)
        low = low + turned_dot(piece[...], theirs)
    total = jnp.concatenate([low.astype(jnp.bfloat16), high.astype(jnp.bfloat16)], axis=1)
    if not blocks:
        outs[0][...] = total
        return
    size = total.shape[0] // blocks
    for pair in range(blocks // 2):
        left = total[2 * pair * size : (2 * pair + 1) * size, :]
        right = total[(2 * pair + 1) * size : (2 * pair + 2) * size, :]
        outs[0][pair] = jnp.where(side_ref[0] == 0, left, right)
        outs[1][pair] = jnp.where(side_ref[0] == 0, right, left)


def attn_weights(spot, side, hidden, attended, grad, pieces, blocks, after):
    rows, width = hidden.shape
    chunks = len(attended)
    features = attended[0].shape[1]
    operands = (hidden, grad, *attended, *pieces)
    if blocks:
        shapes = [(blocks // 2, width // blocks, 4 * features)] * 2
    else:
        shapes = [(width, 4 * features)]
    return tied_call(
        functools.partial(
            attn_weights_kernel, chunks=chunks, count=len(pieces), blocks=blocks
        ),
        (spot, side),
        operands,
        after,
        grid=(1,),
        in_specs=[held(value.shape) for value in operands],
        out_specs=[fixed(shape) for shape in shapes],
        out_shape=[shaped(shape) for shape in shapes],
        vmem=40,
        cost=cost(7),
    )


def fold_kernel(side_ref, kept_ref, got_ref, keep_out, send_out):
    for pair in range(keep_out.shape[0]):
        left, right = [
            kept_ref[block].astype(jnp.float32) + got_ref[block].astype(jnp.float32)
            for block in (2 * pair, 2 * pair + 1)
        ]
        keep_out[pair] = jnp.where(side_ref[0] == 0, left, right).astype(keep_out.dtype)
        send_out[pair] = jnp.where(side_ref[0] == 0, right, left).astype(send_out.dtype)


def fold_blocks(side, kept, got, after):
    blocks, size, width = kept.shape
    shape = (blocks // 2, size, width)
    return tied_call(
        fold_kernel,
        (side,),
        (kept, got),
        after,
        grid=(1,),
        in_specs=[held(kept.shape)] * 2,
        out_specs=[fixed(shape)] * 2,
        out_shape=[shaped(shape)] * 2,
        vmem=12,
        cost=cost(2),
    )


def attn_total_kernel(*refs, count):
    pieces, (out_out, qkv_out) = refs[:count], refs[count:]
    total = sum_of(pieces)[0]
    features = out_out.shape[0]
    out_out[...] = total[:, :features].T
    for c in range(3):
        qkv_out[c] = total[:, (c + 1) * features : (c + 2) * features]


def attn_total_of(pieces, features, after):
    _, size, width = pieces[0].shape
    return tied_call(
        functools.partial(attn_total_kernel, count=len(pieces)),
        (),
        pieces,
        after,
        grid=(1,),
        in_specs=[held((1, size, width))] * len(pieces),
        out_specs=[fixed((features, size)), fixed((3, size, features))],
        out_shape=[
            shaped((features, size), jnp.float32),
            shaped((3, size, features), jnp.float32),
        ],
        vmem=12,
        cost=cost(1),
    )


def on_device(
    tokens,
    conditioning,
    image_index,
    qkv_weight,
    qv_bias,
    out_weight,
    out_bias,
    up_weight,
    up_bias,
    down_weight,
    down_bias,
    ada_weight,
    ada_bias,
    cotangent,
):
    row_count, width = tokens.shape
    feature_count = qkv_weight.shape[2]
    head_size = lax.axis_size("head")
    me = lax.axis_index("head")
    spot = me.astype(jnp.int32).reshape(1)
    my_index = lax.axis_index("seq")
    seq_size = lax.axis_size("seq")
    side = (my_index % 2).astype(jnp.int32).reshape(1)
    blocks = seq_size if width % (16 * seq_size) == 0 else 0
    image_count = conditioning.shape[0]
    columns = ada_weight.shape[2]
    my_images = lax.dynamic_slice_in_dim(image_index, my_index * row_count, row_count, 0)
    edge = jnp.full((row_count,), -1, jnp.int32)
    padded_images = jnp.concatenate([edge, image_index, edge + (image_count + 1)])
    wide_images = lax.dynamic_slice_in_dim(padded_images, my_index * row_count, 3 * row_count, 0)
    ranges = key_ranges(my_images, wide_images, image_count, KEY_TILE, QUERY_BLOCK)
    images = jnp.tile(jnp.arange(image_count, dtype=jnp.int32), 3)
    hot = (my_images[:, None] == images[None, :]).astype(jnp.bfloat16)

    out_full = lax.all_gather(out_weight, "head", axis=0, tiled=True)
    cond_float = conditioning.astype(jnp.float32)
    cond_act = jax.nn.silu(cond_float).astype(jnp.bfloat16)
    mod_mine = jnp.einsum("id,dkf->kif", cond_act, ada_weight, preferred_element_type=jnp.float32)
    mod_mine = mod_mine + ada_bias.astype(jnp.float32)[:, None]
    mod_pieces = gather_pieces(mod_mine, "head")
    modulation = jnp.concatenate([pick(me ^ j, mod_pieces) for j in range(head_size)], axis=2)
    table = jnp.concatenate(three_parts(modulation), axis=1)

    weight = qkv_weight.reshape(width, 3 * feature_count)
    qv_wide = qv_bias.astype(jnp.float32)
    bias = jnp.concatenate([qv_wide[0], jnp.zeros_like(qv_wide[0]), qv_wide[1]])[None]
    hidden_one, query, kv = project(tokens, hot, table, weight, bias, ROW_BLOCK, [])
    kv_before = step_along(kv, "seq", True)
    kv_after = step_along(kv, "seq", False)
    grad_mlp, grad_act, grad_down_bias, cot_sums = grad_act_of(
        cotangent, hot, table, down_weight, image_count, ROW_BLOCK, [hidden_one]
    )
    kvs = [kv_before, kv, kv_after]
    attended, attended_wide, logs, last = [], [], [], [grad_down_bias]
    for c in range(CHUNKS):
        got = attend(ranges, query, kvs, KEY_TILE, QUERY_BLOCK, c, CHUNKS, last)
        for values, kept in zip((attended, attended_wide, logs), got):
            values.append(kept)
        last = [got[2]]
    attended_wide = jnp.concatenate(attended_wide, axis=1)
    logs = jnp.concatenate(logs, axis=1)

    late_sums, up_sums, hidden_pieces, into, last = [], [], [], [], [logs]
    for c in range(CHUNKS):
        got = middle_of(
            spot, gather_pieces(attended[c], "head"), tokens, hot, table, out_full, out_bias[None],
            up_weight, up_bias[None], grad_act, image_count, ROW_BLOCK, c, into, last,
        )
        into = got[:4]
        late_sums.append(got[4].reshape(2 * image_count, width))
        up_sums.append(got[5])
        hidden_pieces.append(swap_pieces(got[6:], "head"))
        last = []
    attn, hidden_two, act, grad_pre = into
    mlp_part, mlp_sums = mlp_of(
        act, down_weight, cotangent, hot, image_count, ROW_BLOCK, hidden_pieces[0]
    )
    mlp = lax.psum(mlp_part, "head")
    weight_part = mlp_weights(grad_mlp, hidden_two, grad_pre, act, [mlp_sums])

    grad_middle, grad_own, gate_sums, out_sums, *attended_pieces = grad_middle_of(
        spot, hidden_pieces, attn, tokens, cotangent, hot, table, out_full, image_count,
        [weight_part],
    )

    own_rows = row_count // CHUNKS // head_size
    query_started, grad_rows, to_before, to_after = attend_far(
        spot, ranges, logs, query, swap_pieces(attended_pieces, "head"), attended_wide, kv_before,
        kv_after, KEY_TILE, QUERY_BLOCK, own_rows, [],
    )
    grad_attn = gather_pieces(grad_own, "head")
    from_after = step_along(to_before, "seq", False)
    from_before = step_along(to_after, "seq", True)
    grad_query, kv_near = attend_near(
        ranges, logs, query, grad_rows, attended_wide, kv, query_started, KEY_TILE, QUERY_BLOCK,
        [],
    )

    grad_all, first_sums, qkv_sums, *one_pieces = grad_hidden_of(
        spot, grad_query, kv_near, from_after, from_before, weight, tokens, hot, image_count,
        ROW_BLOCK, own_rows, head_size, grad_attn,
    )
    one_pieces = swap_pieces(one_pieces, "head")
    attn_part = attn_weights(
        spot, side, hidden_one, attended, grad_all, grad_attn, blocks, []
    )
    layer_out = layer_out_of(
        mlp, attn, tokens, hot, table, down_bias[None], ROW_BLOCK, [attn_part[0]]
    )
    own_tokens = grad_tokens_of(
        spot, one_pieces, tokens, hot, table, grad_middle, CHUNKS, [layer_out]
    )
    token_pieces = gather_pieces(own_tokens, "head")
    last = own_tokens
    if blocks:
        kept, sent = fold_blocks(
            ((my_index // 2) % 2).astype(jnp.int32).reshape(1),
            attn_part[0],
            swap(attn_part[1], "seq", 1),
            [own_tokens],
        )
        last = kept
    sum_stack, kept_rows = split_columns(
        spot,
        [[first_sums.reshape(2 * image_count, width)], [gate_sums[0]], late_sums, [mlp_sums[0]]]
        + [[out_sums]],
        [[qkv_sums], up_sums, [grad_down_bias]],
        head_size,
        [last],
    )
    sums = fold_pieces(sum_stack, "head")
    if blocks:
        mask = 2
        while mask < blocks // 2:
            mask *= 2
            kept, sent = fold_blocks(
                ((my_index // mask) % 2).astype(jnp.int32).reshape(1),
                kept,
                swap(sent, "seq", mask // 2),
                [sums],
            )
        attn_got = [kept, swap(sent, "seq", mask)]

    own_down = lax.dynamic_slice_in_dim(down_bias, me * columns, columns, 0).astype(jnp.float32)
    own_cot = lax.dynamic_slice_in_dim(cot_sums, me * columns, columns, 1) * own_down[None]
    mods = 6 * image_count
    sums = sums + jnp.pad(own_cot, ((5 * image_count, 1), (0, 0)))
    sums = butterfly_sum(jnp.concatenate([sums, kept_rows], axis=0), "seq")
    grad_mod = sums[:mods].reshape(6, image_count, columns)
    out_sum = sums[mods : mods + 1]
    grad_qv_bias = sums[mods + 1 : mods + 4 : 2]
    low_bias = sums[mods + 4 :].reshape(-1)
    units = up_weight.shape[1]
    grad_up_bias, grad_down_bias = low_bias[:units], low_bias[units:]
    mod_parts = jnp.concatenate(three_parts(grad_mod), axis=1)
    grad_cond_act = jnp.einsum(
        "kif,dkf->id", mod_parts, ada_weight, preferred_element_type=jnp.float32
    )
    grad_cond_act = jnp.sum(grad_cond_act.reshape(3, image_count, width), axis=0)
    spread_bias = jnp.concatenate(
        [jnp.where(me == j, out_sum, 0.0) for j in range(head_size)], axis=1
    )
    final = butterfly_sum(jnp.concatenate([grad_cond_act, spread_bias], axis=0), "head")
    _, silu_pull = jax.vjp(jax.nn.silu, cond_float)
    grad_conditioning = silu_pull(final[:image_count])[0]
    grad_out_bias = final[image_count]
    grad_ada_bias = jnp.sum(grad_mod, axis=1)
    grad_ada_weight = jnp.einsum(
        "id,kif->dkf",
        jnp.concatenate([cond_act] * 3, axis=0),
        mod_parts,
        preferred_element_type=jnp.float32,
    )

    grad_tokens = place_rows(spot, token_pieces, CHUNKS, jnp.float32, [])
    mlp_total = lax.psum_scatter(weight_part, "seq", scatter_dimension=0, tiled=True)
    grad_up_weight, grad_down_weight = mlp_total_of(mlp_total, units)
    if blocks:
        grad_out_weight, grad_qkv = attn_total_of(attn_got, feature_count, [])
        grad_qkv_weight = grad_qkv.transpose(1, 0, 2)
    else:
        attn_total = lax.psum_scatter(attn_part[0], "seq", scatter_dimension=0, tiled=True)
        attn_total = attn_total.astype(jnp.float32)
        grad_out_weight = attn_total[:, :feature_count].T
        grad_qkv_weight = attn_total[:, feature_count:].reshape(-1, 3, feature_count)
    return (
        layer_out,
        grad_tokens,
        grad_conditioning,
        grad_qkv_weight,
        grad_qv_bias,
        grad_out_weight,
        grad_out_bias,
        grad_up_weight,
        grad_up_bias,
        grad_down_weight,
        grad_down_bias,
        grad_ada_weight,
        grad_ada_bias,
    )


def solution(mesh):
    placed = (
        P("seq", None),
        P(),
        P(),
        P(None, None, "head"),
        P(None, "head"),
        P("head", None),
        P(),
        P(None, "head"),
        P("head"),
        P("head", None),
        P(),
        P(None, None, "head"),
        P(None, "head"),
        P("seq", None),
    )
    return jax.shard_map(
        on_device,
        mesh=mesh,
        in_specs=placed,
        out_specs=(
            P("seq", None),
            P("seq", None),
            P(),
            P("seq", None, "head"),
            P(None, "head"),
            P("head", "seq"),
            P(),
            P("seq", "head"),
            P("head"),
            P("head", "seq"),
            P(),
            P(None, None, "head"),
            P(None, "head"),
        ),
        check_vma=False,
    )
```
